256 devices in a mesh: dp: 8 (over y, z_lo), row: 8 (over z_hi, core), col: 4 (over x).
Axes of the slice: x: 4, y: 4, z: 8 (z_hi: 4, z_lo: 2; z = z_hi * 2 + z_lo), core: 2. Of those that a mesh axis runs over, the one named last changes fastest.
Arguments:
- single: bfloat16 [8, 8, 512, 768], P('dp', 'col', 'row'), may hold values from -6 to 6
- pair_features: bfloat16 [8, 512, 512, 128], P('dp', 'row', 'col'), may hold values from -80 to 80
- key_valid: int32 [8, 512], P('dp'), may hold values from 0 to 1, as said below
- pair_gain: float32 [128], replicated, may hold values from 0.1 to 1.9
- w_query: bfloat16 [768, 768], P(('row', 'col')), may hold values from -0.21875 to 0.21875
- w_key: bfloat16 [768, 768], P(('row', 'col')), may hold values from -0.21875 to 0.21875
- w_value: bfloat16 [768, 768], P(('row', 'col')), may hold values from -0.21875 to 0.21875
- w_out: bfloat16 [768, 768], P(('row', 'col')), may hold values from -0.21875 to 0.21875
- pair_bias_weight: bfloat16 [128, 16], replicated, may hold values from -20 to 20
- out_cotangent: bfloat16 [8, 8, 512, 768], P('dp', 'col', 'row'), may hold values from -0.0390625 to 0.0390625
Outputs:
- attended: bfloat16 [8, 8, 512, 768], P('dp', 'col', 'row')
- grad_query: float32 [768, 768], P(('row', 'col'))
- grad_key: float32 [768, 768], P(('row', 'col'))
- grad_value: float32 [768, 768], P(('row', 'col'))
- grad_out: float32 [768, 768], P(('row', 'col'))
- grad_bias: float32 [128, 16], replicated
The draws below stay inside these ranges and needn't reach their ends.
Inputs may be any that keep to these rules, and one draw needn't show every extreme that they name: `key_valid`: each row is 1 on a prefix of at least 256 positions and 0 after it.
All inputs are finite; a program needn't handle non-finite values.
Results may differ from the reference program's by a relative error of at most 0.038.
The reference program's roundings to bfloat16 on the way count: a program that leaves them out, or rounds other values in their place, can miss the bound.
Values may be sent and summed in bfloat16 or wider, within the bound.
A program may use at most 128 MiB of HBM per device.

```python
import math
import jax
import jax.numpy as jnp
from jax import lax

D = 768
HEADS = 16
PAIR_DIM = 128
TOKENS = 512
COPIES = 8
COMPLEXES = 8


def bias_directions(key):
    return jax.random.normal(key, (PAIR_DIM, HEADS), jnp.float32)


def draw_pair_bias_weight(key, part):
    base = bias_directions(key)
    return (base * 0.15).astype(jnp.bfloat16)


def draw_pair_features(key, part):
    key = jax.random.fold_in(key, 7)
    keys = jax.random.split(key, 2)
    noise = jax.random.normal(keys[0], (COMPLEXES, TOKENS, TOKENS, PAIR_DIM), jnp.float32)
    spread = jnp.exp(jax.random.uniform(keys[1], (COMPLEXES, TOKENS, TOKENS, 1), jnp.float32, 0.0, 2.3))
    drawn = noise * spread
    return drawn.astype(jnp.bfloat16)


def draw_key_valid(key, part):
    key = jax.random.fold_in(key, 3)
    lengths = jax.random.randint(key, (COMPLEXES, 1), TOKENS // 2, TOKENS + 1)
    return (jnp.arange(TOKENS)[None, :] < lengths).astype(jnp.int32)


def with_spikes(result, key, source, target, parts, factor):
    owner, partner = [(jnp.arange(result.shape[axis_at]) // (result.shape[axis_at] // parts)).reshape([-1 if axis == axis_at else 1 for axis in range(result.ndim)]) for axis_at in (source, target)]
    chosen = jax.random.permutation(key, parts)[partner]
    strong = (owner == chosen) | (owner == (partner + parts // 2) % parts)
    return jnp.where(strong, factor * result, result)


def block_scale(stream_key, extent, cuts, low, top_value):
    level = 1.0
    for dim, shards_of in cuts:
        steps = jax.random.uniform(jax.random.fold_in(jax.random.fold_in(stream_key, 6), dim), (shards_of,), jnp.float32, low / len(cuts), top_value / len(cuts))
        level = level * jnp.repeat(jnp.exp(steps), extent[dim] // shards_of).reshape((-1,) + (1,) * (len(extent) - 1 - dim))
    return level


def normal_values(key, dims, scale, limit, cuts=(), kind=jnp.bfloat16):
    values = jax.random.normal(key, dims, jnp.float32) * scale
    if len(cuts) > 0:
        values = block_scale(key, dims, cuts, -0.22, 0.18) * values
    return jnp.clip(values, min=-limit, max=limit).astype(kind)


def bell_draw_with(key, dims, scale, reach, cuts, heavy, held_as=jnp.bfloat16):
    entries = scale * jax.random.normal(key, dims, jnp.float32)
    if cuts:
        entries = entries * block_scale(key, dims, cuts, -0.22, 0.18)
    return jnp.clip(with_spikes(entries, jax.random.fold_in(key, 3), *heavy), -reach, reach).astype(held_as)


def setup_inputs(seed: int = 0) -> dict:
    streams_of = jax.random.split(jax.random.key(seed), 11)
    single = normal_values(streams_of[0], (COMPLEXES, COPIES, TOKENS, D), 1.0, 6.0, ((0, 8), (1, 4), (2, 8)))
    pair_features = draw_pair_features(jax.random.fold_in(streams_of[10], 71), 0)
    key_valid = draw_key_valid(jax.random.fold_in(streams_of[10], 71), 0)
    pair_gain = jnp.clip(1.0 + 0.18 * jax.random.normal(streams_of[3], (PAIR_DIM,), jnp.float32), 0.1, 1.9)
    w_query = normal_values(streams_of[4], (D, D), D ** -0.5, 0.21875, ((0, 32),))
    w_key = normal_values(streams_of[5], (D, D), D ** -0.5, 0.21875, ((0, 32),))
    w_value = normal_values(streams_of[6], (D, D), D ** -0.5, 0.21875, ((0, 32),))
    w_out = normal_values(streams_of[7], (D, D), D ** -0.5, 0.21875, ((0, 32),))
    pair_bias_weight = draw_pair_bias_weight(jax.random.fold_in(streams_of[10], 71), 0)
    out_cotangent = bell_draw_with(streams_of[9], (COMPLEXES, COPIES, TOKENS, D), 0.005, 0.0390625, ((0, 8), (1, 4), (2, 8)), (2, 3, 8, 2.0))
    return dict(single=single, pair_features=pair_features, key_valid=key_valid, pair_gain=pair_gain, w_query=w_query, w_key=w_key, w_value=w_value, w_out=w_out, pair_bias_weight=pair_bias_weight, out_cotangent=out_cotangent)


NORM_EPSILON = 1e-05
MASKED = -1000000000.0

def rounded(values):
    return lax.optimization_barrier(values.astype(jnp.bfloat16)).astype(jnp.float32)

def normalize_pair(pair_tile, pair_gain):
    values = pair_tile.astype(jnp.float32)
    center = lax.optimization_barrier(jnp.mean(values, axis=-1, keepdims=True))
    centered = values - center
    variance = lax.optimization_barrier(jnp.mean(centered * centered, axis=-1, keepdims=True))
    return (centered * lax.rsqrt(variance + NORM_EPSILON) * pair_gain).astype(jnp.bfloat16)

def single_molecule(activations, pair_tile, valid_keys, cotangent, pair_gain, w_query, w_key, w_value, w_out, pair_bias_weight):
    token_count = activations.shape[1]
    features = activations.shape[2]
    head_count = pair_bias_weight.shape[1]
    head_size = features // head_count
    scaling = 1.0 / math.sqrt(head_size)
    normed = normalize_pair(pair_tile, pair_gain).reshape(token_count * token_count, -1)
    bias = lax.dot_general(pair_bias_weight, normed, (((0,), (1,)), ((), ())), preferred_element_type=jnp.float32)
    bias = bias.reshape(head_count, token_count, token_count)
    keeping = (valid_keys == 1)[None, None, :]

    def per_copy(running, inputs):
        copy_acts, copy_cot = inputs
        query = jnp.dot(copy_acts, w_query, preferred_element_type=jnp.float32).astype(jnp.bfloat16)
        key_proj = jnp.dot(copy_acts, w_key, preferred_element_type=jnp.float32).astype(jnp.bfloat16)
        value_proj = jnp.dot(copy_acts, w_value, preferred_element_type=jnp.float32).astype(jnp.bfloat16)
        query_heads = query.astype(jnp.float32).reshape(token_count, head_count, head_size)
        key_heads = key_proj.astype(jnp.float32).reshape(token_count, head_count, head_size)
        value_heads = value_proj.astype(jnp.float32).reshape(token_count, head_count, head_size)
        scores = jnp.einsum('ihd,jhd->hij', query_heads, key_heads) * scaling + bias
        scores = jnp.where(keeping, scores, MASKED)
        peak = lax.optimization_barrier(jnp.max(scores, axis=2, keepdims=True))
        shifted = jnp.exp(scores - peak)
        totals = lax.optimization_barrier(jnp.sum(shifted, axis=2, keepdims=True))
        softmax_weight_rows = rounded(shifted)
        merged = jnp.einsum('hij,jhd->ihd', softmax_weight_rows, value_heads)
        attention = (merged / jnp.transpose(totals, (1, 0, 2))).reshape(token_count, features).astype(jnp.bfloat16)
        attended = jnp.dot(attention, w_out, preferred_element_type=jnp.float32).astype(jnp.bfloat16)
        grad_out = jnp.dot(attention.T, copy_cot, preferred_element_type=jnp.float32)
        attention_grad = lax.dot_general(copy_cot, w_out, (((1,), (1,)), ((), ())), preferred_element_type=jnp.float32).astype(jnp.bfloat16)
        grad_heads = attention_grad.astype(jnp.float32).reshape(token_count, head_count, head_size)
        attention_heads = attention.astype(jnp.float32).reshape(token_count, head_count, head_size)
        delta = jnp.transpose(lax.optimization_barrier(jnp.sum(grad_heads * attention_heads, axis=2)))[:, :, None]
        probs = shifted / totals
        probs_low = rounded(probs)
        prob_grad = jnp.einsum('ihd,jhd->hij', grad_heads, value_heads)
        score_grad = rounded(probs * (prob_grad - delta))
        query_gradient_total = (jnp.einsum('hij,jhd->ihd', score_grad, key_heads) * scaling).reshape(token_count, features).astype(jnp.bfloat16)
        key_grad = (jnp.einsum('hij,ihd->jhd', score_grad, query_heads) * scaling).reshape(token_count, features)
        value_grad = jnp.einsum('hij,ihd->jhd', probs_low, grad_heads).reshape(token_count, features)
        acts_wide = copy_acts.astype(jnp.float32)
        grad_query = jnp.dot(copy_acts.T, query_gradient_total, preferred_element_type=jnp.float32)
        grad_key = jnp.dot(acts_wide.T, key_grad, precision=lax.Precision.HIGHEST)
        grad_value = jnp.dot(acts_wide.T, value_grad, precision=lax.Precision.HIGHEST)
        updated = (running[0] + grad_query, running[1] + grad_key, running[2] + grad_value, running[3] + grad_out, running[4] + score_grad)
        return (updated, attended)
    initial = (jnp.zeros((features, features), jnp.float32), jnp.zeros((features, features), jnp.float32), jnp.zeros((features, features), jnp.float32), jnp.zeros((features, features), jnp.float32), jnp.zeros((head_count, token_count, token_count), jnp.float32))
    running, attended = lax.scan(per_copy, initial, (activations, cotangent))
    bias_grad = running[4].astype(jnp.bfloat16).reshape(head_count, token_count * token_count)
    grad_bias = lax.dot_general(normed, bias_grad, (((0,), (1,)), ((), ())), preferred_element_type=jnp.float32)
    return (attended, (running[0], running[1], running[2], running[3], grad_bias))

def reference(single, pair_features, key_valid, pair_gain, w_query, w_key, w_value, w_out, pair_bias_weight, out_cotangent):
    features = single.shape[3]
    channels = pair_features.shape[3]
    initial = (jnp.zeros((features, features), jnp.float32), jnp.zeros((features, features), jnp.float32), jnp.zeros((features, features), jnp.float32), jnp.zeros((features, features), jnp.float32), jnp.zeros((channels, pair_bias_weight.shape[1]), jnp.float32))

    def complex_step(running, inputs):
        activations, pair_tile, valid_keys, cotangent = inputs
        attended, grads = single_molecule(activations, pair_tile, valid_keys, cotangent, pair_gain, w_query, w_key, w_value, w_out, pair_bias_weight)
        return (jax.tree.map(jnp.add, running, grads), attended)
    running, attended = lax.scan(complex_step, initial, (single, pair_features, key_valid, out_cotangent))
    return (attended, running[0], running[1], running[2], running[3], running[4])
```

```python
import math

import jax
import jax.numpy as jnp
from jax import lax
from jax.experimental import pallas as pl
from jax.experimental.pallas import tpu as pltpu
from jax.sharding import PartitionSpec as P

NORM_EPSILON = 1e-05
MASKED = -1000000000.0
MESH = pl.DeviceIdType.MESH
F32 = jnp.float32
BF16 = jnp.bfloat16
VMEM_LIMIT = 56 * 1024 * 1024


def place():
    dp, row, col = lax.axis_index("dp"), lax.axis_index("row"), lax.axis_index("col")
    return dp // 2, dp % 2, row // 2, row % 2, col


def device(y, z_lo, z_hi, core, x):
    return (y * 2 + z_lo, z_hi * 2 + core, x)


def greet(peers):
    barrier = pltpu.get_barrier_semaphore()
    for peer in peers:
        pl.semaphore_signal(barrier, inc=1, device_id=peer, device_id_type=MESH)
    pl.semaphore_wait(barrier, len(peers))


class Sender:
    def __init__(self, send_sem, recv_sem):
        self.send_sem, self.recv_sem, self.started = send_sem, recv_sem, []

    def send(self, key, src, dst, peer):
        copy = pltpu.make_async_remote_copy(
            src_ref=src,
            dst_ref=dst,
            send_sem=self.send_sem.at[key],
            recv_sem=self.recv_sem.at[key],
            device_id=peer,
            device_id_type=MESH,
        )
        copy.start()
        self.started.append(copy)
        return copy

    def finish(self):
        for copy in self.started:
            copy.wait_send()


def gather_kernel(w_ref, acts_ref, bias_ref, w_full, acts_full, bias_full, local_sem, send_sem, recv_sem):
    y, z_lo, z_hi, core, x = place()
    row = z_hi * 2 + core
    y_peers = [device((y + d) % 4, z_lo, z_hi, core, x) for d in (1, 2, 3)]
    z_peers = [device(y, z_lo, (z_hi + d) % 4, core, x) for d in (1, 2, 3)]
    x_peers = [device(y, z_lo, z_hi, core, (x + d) % 4) for d in (1, 2, 3)]
    partner = device(y, z_lo, z_hi, 1 - core, x)
    greet(y_peers + z_peers + x_peers + [partner])

    out = Sender(send_sem, recv_sem)
    own_w = pltpu.make_async_copy(w_ref.at[y], w_full.at[y, z_hi, core, x], local_sem.at[0])
    own_acts = pltpu.make_async_copy(acts_ref, acts_full.at[:, row], local_sem.at[1])
    columns = pl.ds(pl.multiple_of(x * 128, 128), 128)
    own_bias = pltpu.make_async_copy(bias_ref, bias_full.at[:, :, columns], local_sem.at[2])
    own_w.start()
    z_copies = [
        out.send(d, w_ref.at[y], w_full.at[y, z_hi, core, x], z_peers[d]) for d in range(3)
    ]
    own_acts.start()
    own_bias.start()
    acts_copies = [
        out.send(34 + d, acts_ref, acts_full.at[:, row], z_peers[d]) for d in range(3)
    ]
    acts_core = [out.send(37, acts_ref, acts_full.at[:, row], partner)]
    bias_copies = [
        out.send(41 + d, bias_ref, bias_full.at[:, :, columns], x_peers[d]) for d in range(3)
    ]

    own_w.wait()
    for copy in z_copies:
        copy.wait_recv()
    line = w_full.at[y, :, core, x]
    x_copies = [out.send(3 + d, line, line, x_peers[d]) for d in range(3)]
    y_copies, core_copies = [], []
    for c in range(4):
        if c > 0:
            x_copies[c - 1].wait_recv()
        line = w_full.at[y, :, core, (x + 4 - c) % 4]
        for e in range(3):
            y_copies.append(out.send(6 + 3 * c + e, line, line, y_peers[e]))
        core_copies.append(out.send(18 + c, line, line, partner))
    for d in range(3):
        acts_copies[d].wait_recv()
        block = acts_full.at[:, ((z_hi + 3 - d) % 4) * 2 + core]
        acts_core.append(out.send(38 + d, block, block, partner))
    for c in range(4):
        for e in range(3):
            y_copies[3 * c + e].wait_recv()
            line = w_full.at[(y + 3 - e) % 4, :, core, (x + 4 - c) % 4]
            core_copies.append(out.send(22 + 3 * c + e, line, line, partner))
    for copy in bias_copies + acts_core + core_copies:
        copy.wait_recv()
    own_acts.wait()
    own_bias.wait()
    out.finish()


def gather(weights, acts, bias):
    any_space = pl.BlockSpec(memory_space=pl.ANY)
    return pl.pallas_call(
        gather_kernel,
        out_shape=(
            jax.ShapeDtypeStruct((4, 4, 2, 4, 24, 768), BF16),
            jax.ShapeDtypeStruct((2, 8, 64, 768), BF16),
            jax.ShapeDtypeStruct((16, 64, 512), F32),
        ),
        in_specs=[any_space] * 3,
        out_specs=[any_space] * 3,
        scratch_shapes=[
            pltpu.SemaphoreType.DMA((3,)),
            pltpu.SemaphoreType.DMA((44,)),
            pltpu.SemaphoreType.DMA((44,)),
        ],
        compiler_params=pltpu.CompilerParams(collective_id=0, has_side_effects=True),
        name="gather",
    )(weights, acts, bias)


def reduce_kernel(
    g_ref, bias_grad_ref, normed_ref, out_ref, bias_out_ref,
    from_core, to_y, from_y, to_x, from_x, to_z, from_z, own, last, from_last,
    bias_in, partial, partial_in, send_sem, recv_sem,
):
    y, z_lo, z_hi, core, x = place()
    z = z_hi * 2 + z_lo
    y_peers = [device((y + d) % 4, z_lo, z_hi, core, x) for d in (1, 2, 3)]
    x_peers = [device(y, z_lo, z_hi, core, (x + d) % 4) for d in (1, 2, 3)]
    z_peers = [device(y, (z + d) % 2, ((z + d) % 8) // 2, core, x) for d in range(1, 8)]
    partner = device(y, z_lo, z_hi, 1 - core, x)
    greet(y_peers + x_peers + z_peers + [partner])

    out = Sender(send_sem, recv_sem)
    order = (1, 2, 3, 0)
    core_copies = {}
    for f in order:
        c = (x + f) % 4
        core_copies[f] = out.send(f, g_ref.at[:, :, 1 - core, c], from_core.at[f], partner)
    bias_copies = [
        out.send(29 + d, bias_grad_ref.at[(x + 1 + d) % 4], bias_in.at[d], x_peers[d])
        for d in range(3)
    ]
    y_copies = {}
    for f in order:
        c = (x + f) % 4
        core_copies[f].wait_recv()
        for d in range(3):
            w = (y + 1 + d) % 4

            def add(k, _, f=f, d=d, w=w, c=c):
                total = g_ref[w, k, core, c].astype(F32) + from_core[f, w, k].astype(F32)
                to_y[d, f, k] = total.astype(BF16)
                return 0

            lax.fori_loop(0, 4, add, 0)
            y_copies[f, d] = out.send(4 + 3 * f + d, to_y.at[d, f], from_y.at[d, f], y_peers[d])

    for copy in bias_copies:
        copy.wait_recv()

    def tile_rows(block, total):
        for u in range(8):
            i = block * 8 + u
            summed = (
                bias_grad_ref[x, i].astype(F32)
                + bias_in[0, i].astype(F32)
                + bias_in[1, i].astype(F32)
                + bias_in[2, i].astype(F32)
            ).astype(BF16)
            total = total + jnp.dot(summed, normed_ref[i], preferred_element_type=F32)
        return total

    partial[0] = lax.fori_loop(0, 8, tile_rows, jnp.zeros((16, 128), F32))
    slot = 0
    for stage, peers in enumerate(([partner], y_peers, x_peers, z_peers)):
        copies = [
            out.send(32 + slot + d, partial.at[stage], partial_in.at[slot + d], peers[d])
            for d in range(len(peers))
        ]
        total = partial[stage]
        for d, copy in enumerate(copies):
            copy.wait_recv()
            total = total + partial_in[slot + d]
        slot += len(peers)
        if stage < 3:
            partial[stage + 1] = total
        else:
            bias_out_ref[...] = total

    x_copies = []
    for f in order:
        c = (x + f) % 4
        for d in range(3):
            y_copies[f, d].wait_recv()

        def add_planes(k, _, f=f, c=c):
            total = (
                g_ref[y, k, core, c].astype(F32)
                + from_core[f, y, k].astype(F32)
                + from_y[0, f, k].astype(F32)
                + from_y[1, f, k].astype(F32)
                + from_y[2, f, k].astype(F32)
            )
            if f > 0:
                to_x[f - 1, k] = total.astype(BF16)
            else:
                own[k] = total
            return 0

        lax.fori_loop(0, 4, add_planes, 0)
        if f > 0:
            x_copies.append(out.send(15 + f, to_x.at[f - 1], from_x.at[f - 1], x_peers[f - 1]))
    for copy in x_copies:
        copy.wait_recv()

    def add_columns(k, _):
        total = (
            own[k]
            + from_x[0, k].astype(F32)
            + from_x[1, k].astype(F32)
            + from_x[2, k].astype(F32)
        )
        own[k] = total
        to_z[k] = total.astype(BF16)
        return 0

    lax.fori_loop(0, 4, add_columns, 0)
    z_copies = []
    for d in range(7):
        target = ((z + 1 + d) % 8) // 2
        z_copies.append(out.send(19 + d, to_z.at[target], from_z.at[d], z_peers[d]))
    for copy in z_copies:
        copy.wait_recv()
    total = own[z_hi]
    for d in range(7):
        total = total + from_z[d].astype(F32)
    last[...] = total
    last_copies = [
        out.send(26 + d, last, from_last.at[d], y_peers[d]) for d in range(3)
    ]
    out_ref[y] = total
    for d, copy in enumerate(last_copies):
        copy.wait_recv()
        out_ref[(y + 3 - d) % 4] = from_last[d]
    out.finish()


def reduce_all(grads, bias_grad, normed):
    vmem = pl.BlockSpec(memory_space=pltpu.VMEM)
    return pl.pallas_call(
        reduce_kernel,
        out_shape=(
            jax.ShapeDtypeStruct((4, 24, 768), F32),
            jax.ShapeDtypeStruct((16, 128), F32),
        ),
        in_specs=[vmem] * 3,
        out_specs=[vmem] * 2,
        scratch_shapes=[
            pltpu.VMEM((4, 4, 4, 24, 768), BF16),
            pltpu.VMEM((3, 4, 4, 24, 768), BF16),
            pltpu.VMEM((3, 4, 4, 24, 768), BF16),
            pltpu.VMEM((3, 4, 24, 768), BF16),
            pltpu.VMEM((3, 4, 24, 768), BF16),
            pltpu.VMEM((4, 24, 768), BF16),
            pltpu.VMEM((7, 24, 768), BF16),
            pltpu.VMEM((4, 24, 768), F32),
            pltpu.VMEM((24, 768), F32),
            pltpu.VMEM((3, 24, 768), F32),
            pltpu.VMEM((3, 64, 16, 128), BF16),
            pltpu.VMEM((4, 16, 128), F32),
            pltpu.VMEM((14, 16, 128), F32),
            pltpu.SemaphoreType.DMA((46,)),
            pltpu.SemaphoreType.DMA((46,)),
        ],
        compiler_params=pltpu.CompilerParams(
            collective_id=1, has_side_effects=True, vmem_limit_bytes=VMEM_LIMIT
        ),
        name="reduce",
    )(grads, bias_grad, normed)


def normalize_pair(pair_tile, pair_gain):
    values = pair_tile.astype(F32)
    center = jnp.mean(values, axis=-1, keepdims=True)
    centered = values - center
    variance = jnp.mean(centered * centered, axis=-1, keepdims=True)
    return (centered * lax.rsqrt(variance + NORM_EPSILON) * pair_gain).astype(BF16)


def project(flat, matrix):
    return jnp.dot(flat, matrix, preferred_element_type=F32).astype(BF16)


def transposed_product(left, right):
    return lax.dot_general(left, right, (((0,), (0,)), ((), ())), preferred_element_type=F32)


def per_device(
    single, pair_features, key_valid, pair_gain, w_query, w_key, w_value, w_out, pair_bias_weight,
    out_cotangent,
):
    own_acts = single[0]
    copies, own_count, features = own_acts.shape
    head_count = 16
    head_size = features // head_count
    scaling = 1.0 / math.sqrt(head_size)
    normed = normalize_pair(pair_features[0], pair_gain)
    tile_bias = lax.dot_general(
        pair_bias_weight, normed, (((0,), (2,)), ((), ())), preferred_element_type=F32
    )
    w_all, acts_all, bias = gather(
        jnp.stack((w_query, w_key, w_value, w_out)), own_acts, tile_bias
    )
    w_all = w_all.reshape(4, features, features)
    token_count = 512
    acts_flat = acts_all.reshape(copies * token_count, features)
    own_flat = own_acts.reshape(copies * own_count, features)
    query = project(own_flat, w_all[0])
    key_proj = project(acts_flat, w_all[1])
    value_proj = project(acts_flat, w_all[2])
    query_heads = query.reshape(copies, own_count, head_count, head_size)
    key_heads = key_proj.reshape(copies, token_count, head_count, head_size)
    value_heads = value_proj.reshape(copies, token_count, head_count, head_size)
    scores = (
        jnp.einsum("sihd,sjhd->shij", query_heads, key_heads, preferred_element_type=F32) * scaling
        + bias[None]
    )
    scores = jnp.where(key_valid[0][None, None, None, :] == 1, scores, MASKED)
    peak = jnp.max(scores, axis=3, keepdims=True)
    shifted = jnp.exp(scores - peak)
    totals = jnp.sum(shifted, axis=3)
    merged = jnp.einsum(
        "shij,sjhd->sihd", shifted.astype(BF16), value_heads, preferred_element_type=F32
    )
    attention = (merged / jnp.transpose(totals, (0, 2, 1))[..., None]).astype(BF16)
    attention_flat = attention.reshape(copies * own_count, features)
    attended = project(attention_flat, w_all[3]).reshape(copies, own_count, features)
    cot_flat = out_cotangent[0].reshape(-1, features)
    grad_out_part = transposed_product(attention_flat, cot_flat)
    out_grad = lax.dot_general(
        cot_flat, w_all[3], (((1,), (1,)), ((), ())), preferred_element_type=F32
    )
    grad_heads = out_grad.astype(BF16).reshape(copies, own_count, head_count, head_size)
    delta = jnp.sum(grad_heads.astype(F32) * attention.astype(F32), axis=3)
    probs = shifted / totals[..., None]
    probs_low = probs.astype(BF16)
    prob_grad = jnp.einsum(
        "sihd,sjhd->shij", grad_heads, value_heads, preferred_element_type=F32
    )
    score_grad = (probs * (prob_grad - jnp.transpose(delta, (0, 2, 1))[..., None])).astype(BF16)
    query_grad = (
        jnp.einsum("shij,sjhd->sihd", score_grad, key_heads, preferred_element_type=F32) * scaling
    )
    query_grad = query_grad.reshape(copies * own_count, features).astype(BF16)
    key_grad = (
        jnp.einsum("shij,sihd->sjhd", score_grad, query_heads, preferred_element_type=F32)
        * scaling
    )
    value_grad = jnp.einsum(
        "shij,sihd->sjhd", probs_low, grad_heads, preferred_element_type=F32
    )
    key_grad = key_grad.reshape(copies * token_count, features).astype(BF16)
    value_grad = value_grad.reshape(copies * token_count, features).astype(BF16)
    grads = jnp.stack(
        (
            transposed_product(own_flat, query_grad).astype(BF16),
            transposed_product(acts_flat, key_grad).astype(BF16),
            transposed_product(acts_flat, value_grad).astype(BF16),
            grad_out_part.astype(BF16),
        )
    ).reshape(4, 4, 2, 4, 24, features)
    bias_grad = jnp.sum(score_grad.astype(F32), axis=0).astype(BF16)
    bias_grad = jnp.transpose(bias_grad.reshape(head_count, own_count, 4, 128), (2, 1, 0, 3))
    results, grad_bias = reduce_all(grads, bias_grad, normed)
    return (attended[None], results[0], results[1], results[2], results[3], grad_bias.T)


def solution(mesh):
    weight = P(("row", "col"), None)
    tokens = P("dp", "col", "row", None)
    return jax.shard_map(
        per_device,
        mesh=mesh,
        in_specs=(
            tokens, P("dp", "row", "col", None), P("dp", None), P(), weight, weight, weight, weight,
            P(), tokens,
        ),
        out_specs=(tokens, weight, weight, weight, weight, P()),
        check_vma=False,
    )
```

```python
import math

import jax
import jax.numpy as jnp
from jax import lax
from jax.experimental import pallas as pl
from jax.experimental.pallas import tpu as pltpu
from jax.sharding import PartitionSpec as P

NORM_EPSILON = 1e-05
MASKED = -1000000000.0
MESH = pl.DeviceIdType.MESH
F32 = jnp.float32
BF16 = jnp.bfloat16
VMEM_LIMIT = 56 * 1024 * 1024


def place():
    dp, row, col = lax.axis_index("dp"), lax.axis_index("row"), lax.axis_index("col")
    return dp // 2, dp % 2, row // 2, row % 2, col


def device(y, z_lo, z_hi, core, x):
    return (y * 2 + z_lo, z_hi * 2 + core, x)


def greet(peers):
    barrier = pltpu.get_barrier_semaphore()
    for peer in peers:
        pl.semaphore_signal(barrier, inc=1, device_id=peer, device_id_type=MESH)
    pl.semaphore_wait(barrier, len(peers))


class Sender:
    def __init__(self, send_sem, recv_sem):
        self.send_sem, self.recv_sem, self.started = send_sem, recv_sem, []

    def send(self, src, dst, peer):
        key = len(self.started)
        copy = pltpu.make_async_remote_copy(
            src_ref=src,
            dst_ref=dst,
            send_sem=self.send_sem.at[key],
            recv_sem=self.recv_sem.at[key],
            device_id=peer,
            device_id_type=MESH,
        )
        copy.start()
        self.started.append(copy)
        return copy

    def finish(self):
        for copy in self.started:
            copy.wait_send()


def gather_kernel(
    w_ref, acts_ref, pair_ref, gain_ref, pair_weight_ref,
    w_full, acts_full, bias_full, normed_ref,
    tile_bias, local_sem, send_sem, recv_sem,
):
    y, z_lo, z_hi, core, x = place()
    row = z_hi * 2 + core
    y_next, y_back = [device((y + d) % 4, z_lo, z_hi, core, x) for d in (1, 3)]
    x_next, x_back = [device(y, z_lo, z_hi, core, (x + d) % 4) for d in (1, 3)]
    z_peers = [device(y, z_lo, (z_hi + d) % 4, core, x) for d in (1, 2, 3)]
    z_next, z_back = z_peers[0], z_peers[2]
    partner = device(y, z_lo, z_hi, 1 - core, x)
    greet([y_next, y_back, x_next, x_back, partner] + z_peers)

    def normalize_rows(block):
        def one_row(k, _):
            i = block * 16 + k
            values = pair_ref[i].astype(F32)
            center = jnp.mean(values, axis=-1, keepdims=True)
            centered = values - center
            variance = jnp.mean(centered * centered, axis=-1, keepdims=True)
            normed = (
                centered * lax.rsqrt(variance + NORM_EPSILON) * gain_ref[...]
            ).astype(BF16)
            normed_ref[i] = normed
            tile_bias[:, i, :] = lax.dot_general(
                pair_weight_ref[...], normed, (((1,), (1,)), ((), ())),
                preferred_element_type=F32,
            )
            return 0

        lax.fori_loop(0, 16, one_row, 0, unroll=4)

    def columns(owner):
        return pl.ds(pl.multiple_of((owner % 4) * 128, 128), 128)

    def line(plane, owner, part=slice(0, 4)):
        return w_full.at[plane % 4, part, core, owner % 4]

    def rows(z_owner):
        return acts_full.at[:, (z_owner % 4) * 2 + core]

    out = Sender(send_sem, recv_sem)
    send = out.send
    first, second = slice(0, 2), slice(2, 4)
    own_w = pltpu.make_async_copy(w_ref.at[y], w_full.at[y, z_hi, core, x], local_sem.at[0])
    own_acts = pltpu.make_async_copy(acts_ref, acts_full.at[:, row], local_sem.at[1])
    own_w.start()
    z_copies = [send(w_ref.at[y], w_full.at[y, z_hi, core, x], peer) for peer in z_peers]
    own_acts.start()
    acts_up = send(acts_ref, rows(z_hi), z_next)
    acts_down = send(acts_ref, rows(z_hi), z_back)
    core_copies = [send(acts_ref, rows(z_hi), partner)]
    normalize_rows(0)

    def swap_planes(owner):
        own = line(y, owner)
        core_copies.append(send(own, own, partner))
        return send(own, own, y_next), send(own, own, y_back)

    own_w.wait()
    for copy in z_copies:
        copy.wait_recv()
    own = line(y, x)
    x_up = send(own, own, x_next)
    x_down = send(own, own, x_back)
    planes = [swap_planes(x)]
    normalize_rows(1)
    x_up.wait_recv()
    part = line(y, x + 3, first)
    x_far_up = send(part, part, x_next)
    x_down.wait_recv()
    part = line(y, x + 1, second)
    x_far_down = send(part, part, x_back)
    planes.append(swap_planes(x + 3))
    planes.append(swap_planes(x + 1))
    acts_up.wait_recv()
    part = acts_full.at[0, ((z_hi + 3) % 4) * 2 + core]
    acts_far_up = send(part, part, z_next)
    acts_down.wait_recv()
    part = acts_full.at[1, ((z_hi + 1) % 4) * 2 + core]
    acts_far_down = send(part, part, z_back)
    core_copies.append(send(rows(z_hi + 3), rows(z_hi + 3), partner))
    core_copies.append(send(rows(z_hi + 1), rows(z_hi + 1), partner))
    x_far_up.wait_recv()
    x_far_down.wait_recv()
    planes.append(swap_planes(x + 2))
    owners = (x, x + 3, x + 1, x + 2)
    far = []

    def relay_planes(n):
        up, down = planes[n]
        owner = owners[n]
        up.wait_recv()
        part = line(y + 3, owner, first)
        far_up = send(part, part, y_next)
        down.wait_recv()
        part = line(y + 1, owner, second)
        far.append((far_up, send(part, part, y_back)))
        for plane in (y + 3, y + 1):
            whole = line(plane, owner)
            core_copies.append(send(whole, whole, partner))

    relay_planes(0)
    normalize_rows(2)
    relay_planes(1)
    normalize_rows(3)
    own_bias = pltpu.make_async_copy(tile_bias, bias_full.at[:, :, columns(x)], local_sem.at[2])
    own_bias.start()
    bias_up = send(tile_bias, bias_full.at[:, :, columns(x)], x_next)
    bias_down = send(tile_bias, bias_full.at[:, :, columns(x)], x_back)
    relay_planes(2)
    relay_planes(3)
    acts_far_up.wait_recv()
    acts_far_down.wait_recv()
    core_copies.append(send(rows(z_hi + 2), rows(z_hi + 2), partner))
    for n in range(4):
        for copy in far[n]:
            copy.wait_recv()
        whole = line(y + 2, owners[n])
        core_copies.append(send(whole, whole, partner))
        if n == 1:
            bias_up.wait_recv()
            part = bias_full.at[slice(0, 8), :, columns(x + 3)]
            bias_far_up = send(part, part, x_next)
            bias_down.wait_recv()
            part = bias_full.at[slice(8, 16), :, columns(x + 1)]
            bias_far_down = send(part, part, x_back)
    for copy in core_copies + [bias_far_up, bias_far_down]:
        copy.wait_recv()
    own_acts.wait()
    own_bias.wait()
    out.finish()


def gather(weights, acts, pair_tile, pair_gain, pair_weight):
    any_space = pl.BlockSpec(memory_space=pl.ANY)
    vmem = pl.BlockSpec(memory_space=pltpu.VMEM)
    return pl.pallas_call(
        gather_kernel,
        out_shape=(
            jax.ShapeDtypeStruct((4, 4, 2, 4, 24, 768), BF16),
            jax.ShapeDtypeStruct((2, 8, 64, 768), BF16),
            jax.ShapeDtypeStruct((16, 64, 512), F32),
            jax.ShapeDtypeStruct((64, 128, 128), BF16),
        ),
        in_specs=[any_space, any_space, vmem, vmem, vmem],
        out_specs=[any_space, any_space, any_space, vmem],
        scratch_shapes=[
            pltpu.VMEM((16, 64, 128), F32),
            pltpu.SemaphoreType.DMA((3,)),
            pltpu.SemaphoreType.DMA((56,)),
            pltpu.SemaphoreType.DMA((56,)),
        ],
        compiler_params=pltpu.CompilerParams(
            collective_id=0, has_side_effects=True, vmem_limit_bytes=VMEM_LIMIT
        ),
        name="gather",
    )(weights, acts, pair_tile, pair_gain, pair_weight)


def reduce_kernel(
    g_ref, bias_grad_ref, normed_ref, out_ref, bias_out_ref,
    from_core, to_far, from_far, to_y, from_y, to_x, from_x, x_halves, to_z, from_z,
    own, last, from_last,
    bias_halves, bias_sent, bias_in, bias_sum, partial, partial_in, send_sem, recv_sem,
):
    y, z_lo, z_hi, core, x = place()
    z = z_hi * 2 + z_lo
    y_peers = [device((y + d) % 4, z_lo, z_hi, core, x) for d in (1, 2, 3)]
    x_peers = [device(y, z_lo, z_hi, core, (x + d) % 4) for d in (1, 2, 3)]
    z_peers = [device(y, (z + d) % 2, ((z + d) % 8) // 2, core, x) for d in range(1, 8)]
    partner = device(y, z_lo, z_hi, 1 - core, x)
    y_next, y_back, x_next, x_back = y_peers[0], y_peers[2], x_peers[0], x_peers[2]
    greet(y_peers + x_peers + z_peers + [partner])

    out = Sender(send_sem, recv_sem)
    send = out.send
    first, second = slice(0, 2), slice(2, 4)
    order = (2, 1, 3, 0)
    core_copies = {}
    for f in order:
        core_copies[f] = send(g_ref.at[:, :, 1 - core, (x + f) % 4], from_core.at[f], partner)
    far_block = bias_grad_ref.at[(x + 2) % 4]
    bias_far = [
        send(far_block.at[slice(0, 8)], bias_halves.at[0], x_next),
        send(far_block.at[slice(8, 16)], bias_halves.at[1], x_back),
    ]

    def both_cores(f, w, k):
        return g_ref[w, k, core, (x + f) % 4].astype(F32) + from_core[f, w, k].astype(F32)

    far, near = {}, {}

    def start_chunk(f):
        core_copies[f].wait_recv()

        def add(k, _):
            to_far[f, k] = both_cores(f, (y + 2) % 4, k).astype(BF16)
            return 0

        lax.fori_loop(0, 4, add, 0)
        far[f] = (
            send(to_far.at[f, first], from_far.at[0, f], y_next),
            send(to_far.at[f, second], from_far.at[1, f], y_back),
        )

    def pass_chunk(f):
        far[f][0].wait_recv()
        far[f][1].wait_recv()

        def add(k, _):
            up, down = (y + 1) % 4, (y + 3) % 4
            to_y[0, f, k] = (
                both_cores(f, up, k) + from_far[0, f, k].astype(F32)
            ).astype(BF16)
            to_y[0, f, k + 2] = both_cores(f, up, k + 2).astype(BF16)
            to_y[1, f, k] = both_cores(f, down, k).astype(BF16)
            to_y[1, f, k + 2] = (
                both_cores(f, down, k + 2) + from_far[1, f, k].astype(F32)
            ).astype(BF16)
            return 0

        lax.fori_loop(0, 2, add, 0)
        near[f] = (
            send(to_y.at[0, f], from_y.at[0, f], y_next),
            send(to_y.at[1, f], from_y.at[1, f], y_back),
        )

    start_chunk(2)
    start_chunk(1)
    pass_chunk(2)
    start_chunk(3)
    pass_chunk(1)
    start_chunk(0)
    for copy in bias_far:
        copy.wait_recv()

    def add_bias(h, _):
        up, down = (x + 1) % 4, (x + 3) % 4
        bias_sent[0, h] = (
            bias_grad_ref[up, h].astype(F32) + bias_halves[0, h].astype(F32)
        ).astype(BF16)
        bias_sent[0, h + 8] = bias_grad_ref[up, h + 8]
        bias_sent[1, h] = bias_grad_ref[down, h]
        bias_sent[1, h + 8] = (
            bias_grad_ref[down, h + 8].astype(F32) + bias_halves[1, h].astype(F32)
        ).astype(BF16)
        return 0

    lax.fori_loop(0, 8, add_bias, 0)
    bias_near = [
        send(bias_sent.at[0], bias_in.at[0], x_next),
        send(bias_sent.at[1], bias_in.at[1], x_back),
    ]
    pass_chunk(3)
    pass_chunk(0)

    for copy in bias_near:
        copy.wait_recv()

    def sum_bias(h, _):
        summed = (
            bias_grad_ref[x, h].astype(F32)
            + bias_in[0, h].astype(F32)
            + bias_in[1, h].astype(F32)
        )
        bias_sum[h] = summed.astype(BF16).astype(F32)
        return 0

    lax.fori_loop(0, 16, sum_bias, 0)

    def tile_rows(block, total):
        for u in range(8):
            i = block * 8 + u
            total = total + jnp.dot(
                bias_sum[:, i, :].astype(BF16), normed_ref[i], preferred_element_type=F32
            )
        return total

    partial[0] = lax.fori_loop(0, 8, tile_rows, jnp.zeros((16, 128), F32))
    stages = ([partner], y_peers, x_peers, z_peers)
    starts = (0, 1, 4, 7)
    in_flight = {}

    def start_stage(n):
        in_flight[n] = [
            send(partial.at[n], partial_in.at[starts[n] + d], peer)
            for d, peer in enumerate(stages[n])
        ]

    def end_stage(n):
        total = partial[n]
        for d, copy in enumerate(in_flight[n]):
            copy.wait_recv()
            total = total + partial_in[starts[n] + d]
        if n < 3:
            partial[n + 1] = total
            start_stage(n + 1)
        else:
            bias_out_ref[...] = total

    def all_planes(f, k):
        return (
            both_cores(f, y, k) + from_y[0, f, k].astype(F32) + from_y[1, f, k].astype(F32)
        )

    def wait_planes(f):
        near[f][0].wait_recv()
        near[f][1].wait_recv()

    start_stage(0)
    wait_planes(2)

    def add_far(k, _):
        to_x[2, k] = all_planes(2, k).astype(BF16)
        return 0

    lax.fori_loop(0, 4, add_far, 0)
    x_far = [
        send(to_x.at[2, first], x_halves.at[0], x_next),
        send(to_x.at[2, second], x_halves.at[1], x_back),
    ]
    end_stage(0)
    wait_planes(1)
    x_far[0].wait_recv()

    def add_up(k, _):
        to_x[0, k] = (all_planes(1, k) + x_halves[0, k].astype(F32)).astype(BF16)
        to_x[0, k + 2] = all_planes(1, k + 2).astype(BF16)
        return 0

    lax.fori_loop(0, 2, add_up, 0)
    x_up = send(to_x.at[0], from_x.at[0], x_next)
    end_stage(1)
    wait_planes(3)
    x_far[1].wait_recv()

    def add_down(k, _):
        to_x[1, k] = all_planes(3, k).astype(BF16)
        to_x[1, k + 2] = (all_planes(3, k + 2) + x_halves[1, k].astype(F32)).astype(BF16)
        return 0

    lax.fori_loop(0, 2, add_down, 0)
    x_down = send(to_x.at[1], from_x.at[1], x_back)
    end_stage(2)
    wait_planes(0)
    x_up.wait_recv()
    x_down.wait_recv()

    def add_own(k, _):
        total = all_planes(0, k) + from_x[0, k].astype(F32) + from_x[1, k].astype(F32)
        own[k] = total
        to_z[k] = total.astype(BF16)
        return 0

    lax.fori_loop(0, 4, add_own, 0)
    z_copies = []
    for d in range(7):
        target = ((z + 1 + d) % 8) // 2
        z_copies.append(send(to_z.at[target], from_z.at[d], z_peers[d]))
    end_stage(3)
    total = own[z_hi]
    for d, copy in enumerate(z_copies):
        copy.wait_recv()
        total = total + from_z[d].astype(F32)
    last[...] = total.astype(BF16)
    last_copies = [send(last, from_last.at[d], y_peers[d]) for d in range(3)]
    out_ref[y] = total.astype(BF16).astype(F32)
    for d, copy in enumerate(last_copies):
        copy.wait_recv()
        out_ref[(y + 3 - d) % 4] = from_last[d].astype(F32)
    out.finish()


def reduce_all(grads, bias_grad, normed):
    vmem = pl.BlockSpec(memory_space=pltpu.VMEM)
    return pl.pallas_call(
        reduce_kernel,
        out_shape=(
            jax.ShapeDtypeStruct((4, 24, 768), F32),
            jax.ShapeDtypeStruct((16, 128), F32),
        ),
        in_specs=[vmem] * 3,
        out_specs=[vmem] * 2,
        scratch_shapes=[
            pltpu.VMEM((4, 4, 4, 24, 768), BF16),
            pltpu.VMEM((4, 4, 24, 768), BF16),
            pltpu.VMEM((2, 4, 2, 24, 768), BF16),
            pltpu.VMEM((2, 4, 4, 24, 768), BF16),
            pltpu.VMEM((2, 4, 4, 24, 768), BF16),
            pltpu.VMEM((3, 4, 24, 768), BF16),
            pltpu.VMEM((2, 4, 24, 768), BF16),
            pltpu.VMEM((2, 2, 24, 768), BF16),
            pltpu.VMEM((4, 24, 768), BF16),
            pltpu.VMEM((7, 24, 768), BF16),
            pltpu.VMEM((4, 24, 768), F32),
            pltpu.VMEM((24, 768), BF16),
            pltpu.VMEM((3, 24, 768), BF16),
            pltpu.VMEM((2, 8, 64, 128), BF16),
            pltpu.VMEM((2, 16, 64, 128), BF16),
            pltpu.VMEM((2, 16, 64, 128), BF16),
            pltpu.VMEM((16, 64, 128), F32),
            pltpu.VMEM((4, 16, 128), F32),
            pltpu.VMEM((14, 16, 128), F32),
            pltpu.SemaphoreType.DMA((52,)),
            pltpu.SemaphoreType.DMA((52,)),
        ],
        compiler_params=pltpu.CompilerParams(
            collective_id=1, has_side_effects=True, vmem_limit_bytes=VMEM_LIMIT
        ),
        name="reduce",
    )(grads, bias_grad, normed)


def transposed_product(left, right):
    return lax.dot_general(left, right, (((0,), (0,)), ((), ())), preferred_element_type=F32)


WINDOWS = ((0, 0, 5), (128, 5, 3), (384, 8, 5), (512, 13, 3))


def head_mask(start, head):
    lanes = lax.broadcasted_iota(jnp.int32, (64, 256), 1) + start
    return (lanes >= head * 48) & (lanes < head * 48 + 48)


def attention_kernel(
    own_ref, acts_ref, cot_ref, w_ref, bias_ref, valid_ref,
    attended_ref, grads_ref, bias_grad_ref,
    query, key, value, grad, attention, query_grad, key_grad, value_grad, bias_total,
    scores, pulled, weights, probs_low, score_grad,
):
    scaling = 1.0 / math.sqrt(48)
    own = own_ref[...]
    cot = cot_ref[...]
    query[...] = jnp.dot(own, w_ref[0], preferred_element_type=F32).astype(BF16)
    grad[...] = lax.dot_general(
        cot, w_ref[3], (((1,), (1,)), ((), ())), preferred_element_type=F32
    ).astype(BF16)

    def project_rows(block, _):
        rows = pl.ds(pl.multiple_of(block * 256, 256), 256)
        part = acts_ref[rows, :]
        key[rows, :] = jnp.dot(part, w_ref[1], preferred_element_type=F32).astype(BF16)
        value[rows, :] = jnp.dot(part, w_ref[2], preferred_element_type=F32).astype(BF16)
        return 0

    lax.fori_loop(0, 4, project_rows, 0)
    bias_total[...] = jnp.zeros_like(bias_total)
    attention[...] = jnp.zeros_like(attention)
    query_grad[...] = jnp.zeros_like(query_grad)
    key_grad[...] = jnp.zeros_like(key_grad)
    value_grad[...] = jnp.zeros_like(value_grad)
    keep = valid_ref[...] == 1

    def one_copy(s, _):
        q_rows = pl.ds(pl.multiple_of(s * 64, 64), 64)
        k_rows = pl.ds(pl.multiple_of(s * 512, 512), 512)
        for start, first, count in WINDOWS:
            lanes = slice(start, start + 256)
            stacked = slice(0, count * 64)
            k_win = key[k_rows, lanes]
            v_win = value[k_rows, lanes]
            q_win = query[q_rows, lanes]
            g_win = grad[q_rows, lanes]
            masks = [head_mask(start, first + n) for n in range(count)]
            zero = jnp.zeros_like(q_win)
            q_stack = jnp.concatenate([jnp.where(m, q_win, zero) for m in masks], axis=0)
            g_stack = jnp.concatenate([jnp.where(m, g_win, zero) for m in masks], axis=0)
            scores[stacked, :] = lax.dot_general(
                q_stack, k_win, (((1,), (1,)), ((), ())), preferred_element_type=F32
            )
            pulled[stacked, :] = lax.dot_general(
                g_stack, v_win, (((1,), (1,)), ((), ())), preferred_element_type=F32
            )
            inverses = []
            for n in range(count):
                rows = slice(n * 64, n * 64 + 64)
                block = scores[rows, :] * scaling + bias_ref[first + n]
                block = jnp.where(keep, block, MASKED)
                shifted = jnp.exp(block - jnp.max(block, axis=1, keepdims=True))
                inverses.append(1.0 / jnp.sum(shifted, axis=1, keepdims=True))
                scores[rows, :] = shifted
                weights[rows, :] = shifted.astype(BF16)
            merged = jnp.dot(weights[stacked, :], v_win, preferred_element_type=F32)
            attended_win = jnp.zeros((64, 256), F32)
            for n in range(count):
                attended_win = jnp.where(
                    masks[n], merged[n * 64 : n * 64 + 64] * inverses[n], attended_win
                )
            attention[q_rows, lanes] += attended_win
            product = g_win.astype(F32) * attended_win.astype(BF16).astype(F32)
            for n in range(count):
                rows = slice(n * 64, n * 64 + 64)
                delta = jnp.sum(jnp.where(masks[n], product, 0.0), axis=1, keepdims=True)
                probs = scores[rows, :] * inverses[n]
                probs_low[rows, :] = probs.astype(BF16)
                change = (probs * (pulled[rows, :] - delta)).astype(BF16)
                score_grad[rows, :] = change
                bias_total[first + n] += change.astype(F32)
            back = jnp.dot(score_grad[stacked, :], k_win, preferred_element_type=F32)
            back_win = jnp.zeros((64, 256), F32)
            for n in range(count):
                back_win = jnp.where(masks[n], back[n * 64 : n * 64 + 64], back_win)
            query_grad[q_rows, lanes] += back_win
            key_grad[k_rows, lanes] += lax.dot_general(
                score_grad[stacked, :], q_stack, (((0,), (0,)), ((), ())),
                preferred_element_type=F32,
            )
            value_grad[k_rows, lanes] += lax.dot_general(
                probs_low[stacked, :], g_stack, (((0,), (0,)), ((), ())),
                preferred_element_type=F32,
            )
        return 0

    lax.fori_loop(0, 2, one_copy, 0)
    merged_heads = attention[...].astype(BF16)
    attended_ref[...] = jnp.dot(
        merged_heads, w_ref[3], preferred_element_type=F32
    ).astype(BF16)
    q_low = (query_grad[...] * scaling).astype(BF16)
    key[...] = (key_grad[...] * scaling).astype(BF16)
    value[...] = value_grad[...].astype(BF16)
    for block in range(3):
        lanes = slice(block * 256, block * 256 + 256)
        grads_ref[0, lanes, :] = transposed_product(own[:, lanes], q_low).astype(BF16)
        grads_ref[3, lanes, :] = transposed_product(merged_heads[:, lanes], cot).astype(BF16)
        part = acts_ref[:, lanes]
        grads_ref[1, lanes, :] = transposed_product(part, key[...]).astype(BF16)
        grads_ref[2, lanes, :] = transposed_product(part, value[...]).astype(BF16)
    for column in range(4):
        bias_grad_ref[column] = bias_total[:, :, column * 128 : column * 128 + 128].astype(BF16)


def attend(own, acts, cot, weights, bias, valid):
    vmem = pl.BlockSpec(memory_space=pltpu.VMEM)
    return pl.pallas_call(
        attention_kernel,
        out_shape=(
            jax.ShapeDtypeStruct((128, 768), BF16),
            jax.ShapeDtypeStruct((4, 768, 768), BF16),
            jax.ShapeDtypeStruct((4, 16, 64, 128), BF16),
        ),
        in_specs=[vmem] * 6,
        out_specs=[vmem] * 3,
        scratch_shapes=[
            pltpu.VMEM((128, 768), BF16),
            pltpu.VMEM((1024, 768), BF16),
            pltpu.VMEM((1024, 768), BF16),
            pltpu.VMEM((128, 768), BF16),
            pltpu.VMEM((128, 768), F32),
            pltpu.VMEM((128, 768), F32),
            pltpu.VMEM((1024, 768), F32),
            pltpu.VMEM((1024, 768), F32),
            pltpu.VMEM((16, 64, 512), F32),
            pltpu.VMEM((320, 512), F32),
            pltpu.VMEM((320, 512), F32),
            pltpu.VMEM((320, 512), BF16),
            pltpu.VMEM((320, 512), BF16),
            pltpu.VMEM((320, 512), BF16),
        ],
        compiler_params=pltpu.CompilerParams(vmem_limit_bytes=VMEM_LIMIT),
        name="attend",
    )(own, acts, cot, weights, bias, valid)


def per_device(
    single, pair_features, key_valid, pair_gain, w_query, w_key, w_value, w_out, pair_bias_weight,
    out_cotangent,
):
    own_acts = single[0]
    copies, own_count, features = own_acts.shape
    w_all, acts_all, bias, normed = gather(
        jnp.stack((w_query, w_key, w_value, w_out)),
        own_acts,
        pair_features[0],
        pair_gain[None],
        pair_bias_weight.T,
    )
    attended, grads, bias_grad = attend(
        own_acts.reshape(copies * own_count, features),
        acts_all.reshape(copies * 512, features),
        out_cotangent[0].reshape(copies * own_count, features),
        w_all.reshape(4, features, features),
        bias,
        key_valid,
    )
    grads = grads.reshape(4, 4, 2, 4, 24, features)
    results, grad_bias = reduce_all(grads, bias_grad, normed)
    return (
        attended.reshape(1, copies, own_count, features),
        results[0], results[1], results[2], results[3], grad_bias.T,
    )


def solution(mesh):
    weight = P(("row", "col"), None)
    tokens = P("dp", "col", "row", None)
    return jax.shard_map(
        per_device,
        mesh=mesh,
        in_specs=(
            tokens, P("dp", "row", "col", None), P("dp", None), P(), weight, weight, weight, weight,
            P(), tokens,
        ),
        out_specs=(tokens, weight, weight, weight, weight, P()),
        check_vma=False,
    )
```

```python
import math

import jax
import jax.numpy as jnp
from jax import lax
from jax.experimental import pallas as pl
from jax.experimental.pallas import tpu as pltpu
from jax.sharding import PartitionSpec as P

NORM_EPSILON = 1e-05
MASKED = -1000000000.0
MESH = pl.DeviceIdType.MESH
F32 = jnp.float32
BF16 = jnp.bfloat16
VMEM_LIMIT = 56 * 1024 * 1024


def place():
    dp, row, col = lax.axis_index("dp"), lax.axis_index("row"), lax.axis_index("col")
    return dp // 2, dp % 2, row // 2, row % 2, col


def device(y, z_lo, z_hi, core, x):
    return (y * 2 + z_lo, z_hi * 2 + core, x)


def greet(peers):
    barrier = pltpu.get_barrier_semaphore()
    for peer in peers:
        pl.semaphore_signal(barrier, inc=1, device_id=peer, device_id_type=MESH)
    pl.semaphore_wait(barrier, len(peers))


class Sender:
    def __init__(self, send_sem, recv_sem):
        self.send_sem, self.recv_sem, self.started = send_sem, recv_sem, []

    def send(self, src, dst, peer):
        key = len(self.started)
        copy = pltpu.make_async_remote_copy(
            src_ref=src,
            dst_ref=dst,
            send_sem=self.send_sem.at[key],
            recv_sem=self.recv_sem.at[key],
            device_id=peer,
            device_id_type=MESH,
        )
        copy.start()
        self.started.append(copy)
        return copy

    def finish(self):
        for copy in self.started:
            copy.wait_send()


def gather_kernel(
    wq_ref, wk_ref, wv_ref, wo_ref, acts_ref, pair_ref, gain_ref, pair_weight_ref,
    w_full, acts_full, bias_full, normed_ref,
    tile_bias, local_sem, send_sem, recv_sem,
):
    y, z_lo, z_hi, core, x = place()
    row = z_hi * 2 + core
    y_next, y_back = [device((y + d) % 4, z_lo, z_hi, core, x) for d in (1, 3)]
    x_next, x_back = [device(y, z_lo, z_hi, core, (x + d) % 4) for d in (1, 3)]
    z_peers = [device(y, z_lo, (z_hi + d) % 4, core, x) for d in (1, 2, 3)]
    z_next, z_back = z_peers[0], z_peers[2]
    partner = device(y, z_lo, z_hi, 1 - core, x)
    greet([y_next, y_back, x_next, x_back, partner] + z_peers)

    def normalize_rows(block):
        def one_row(k, _):
            i = block * 16 + k
            values = pair_ref[i].astype(F32)
            center = jnp.mean(values, axis=-1, keepdims=True)
            centered = values - center
            variance = jnp.mean(centered * centered, axis=-1, keepdims=True)
            normed = (
                centered * lax.rsqrt(variance + NORM_EPSILON) * gain_ref[...]
            ).astype(BF16)
            normed_ref[i] = normed
            tile_bias[:, i, :] = lax.dot_general(
                pair_weight_ref[...], normed, (((1,), (1,)), ((), ())),
                preferred_element_type=F32,
            )
            return 0

        lax.fori_loop(0, 16, one_row, 0, unroll=4)

    def columns(owner):
        return pl.ds(pl.multiple_of((owner % 4) * 128, 128), 128)

    def line(plane, owner, part=slice(0, 4)):
        return w_full.at[plane % 4, part, core, owner % 4]

    def rows(z_owner):
        return acts_full.at[:, (z_owner % 4) * 2 + core]

    out = Sender(send_sem, recv_sem)
    send = out.send
    first, second = slice(0, 2), slice(2, 4)
    for plane, w_ref in enumerate((wq_ref, wk_ref, wv_ref, wo_ref)):

        @pl.when(y == plane)
        def _(plane=plane, w_ref=w_ref):
            target = w_full.at[plane, z_hi, core, x]
            pltpu.make_async_copy(w_ref, target, local_sem.at[0]).start()
            for d, peer in enumerate(z_peers):
                pltpu.make_async_remote_copy(
                    src_ref=w_ref, dst_ref=target, send_sem=send_sem.at[d],
                    recv_sem=recv_sem.at[d], device_id=peer, device_id_type=MESH,
                ).start()

    own_w = pltpu.make_async_copy(wq_ref, w_full.at[y, z_hi, core, x], local_sem.at[0])
    own_acts = pltpu.make_async_copy(acts_ref, acts_full.at[:, row], local_sem.at[1])
    z_copies = [
        pltpu.make_async_remote_copy(
            src_ref=wq_ref, dst_ref=w_full.at[y, z_hi, core, x], send_sem=send_sem.at[d],
            recv_sem=recv_sem.at[d], device_id=peer, device_id_type=MESH,
        )
        for d, peer in enumerate(z_peers)
    ]
    out.started.extend(z_copies)
    own_acts.start()
    acts_up = send(acts_ref, rows(z_hi), z_next)
    acts_down = send(acts_ref, rows(z_hi), z_back)
    core_copies = [send(acts_ref, rows(z_hi), partner)]
    normalize_rows(0)

    def swap_planes(owner):
        own = line(y, owner)
        core_copies.append(send(own, own, partner))
        return send(own, own, y_next), send(own, own, y_back)

    def tile_rows(chunk):
        return slice(chunk * 16, chunk * 16 + 16)

    def bias_block(owner, chunk, heads=slice(0, 16)):
        return bias_full.at[heads, tile_rows(chunk), columns(owner)]

    bias_near, bias_far = [], []

    def send_bias(chunk):
        source = tile_bias.at[:, tile_rows(chunk), :]
        bias_near.append(
            (send(source, bias_block(x, chunk), x_next), send(source, bias_block(x, chunk), x_back))
        )

    def relay_bias(chunk):
        up, down = bias_near[chunk]
        up.wait_recv()
        part = bias_block(x + 3, chunk, slice(0, 8))
        bias_far.append(send(part, part, x_next))
        down.wait_recv()
        part = bias_block(x + 1, chunk, slice(8, 16))
        bias_far.append(send(part, part, x_back))

    own_w.wait()
    for copy in z_copies:
        copy.wait_recv()
    own = line(y, x)
    x_up = send(own, own, x_next)
    x_down = send(own, own, x_back)
    planes = [swap_planes(x)]
    send_bias(0)
    normalize_rows(1)
    send_bias(1)
    x_up.wait_recv()
    part = line(y, x + 3, first)
    x_far_up = send(part, part, x_next)
    x_down.wait_recv()
    part = line(y, x + 1, second)
    x_far_down = send(part, part, x_back)
    planes.append(swap_planes(x + 3))
    planes.append(swap_planes(x + 1))
    normalize_rows(2)
    send_bias(2)
    acts_up.wait_recv()
    part = acts_full.at[0, ((z_hi + 3) % 4) * 2 + core]
    acts_far_up = send(part, part, z_next)
    acts_down.wait_recv()
    part = acts_full.at[1, ((z_hi + 1) % 4) * 2 + core]
    acts_far_down = send(part, part, z_back)
    core_copies.append(send(rows(z_hi + 3), rows(z_hi + 3), partner))
    core_copies.append(send(rows(z_hi + 1), rows(z_hi + 1), partner))
    relay_bias(0)
    x_far_up.wait_recv()
    x_far_down.wait_recv()
    planes.append(swap_planes(x + 2))
    owners = (x, x + 3, x + 1, x + 2)
    far = []

    def relay_planes(n):
        up, down = planes[n]
        owner = owners[n]
        up.wait_recv()
        part = line(y + 3, owner, first)
        far_up = send(part, part, y_next)
        down.wait_recv()
        part = line(y + 1, owner, second)
        far.append((far_up, send(part, part, y_back)))
        for plane in (y + 3, y + 1):
            whole = line(plane, owner)
            core_copies.append(send(whole, whole, partner))

    relay_planes(0)
    normalize_rows(3)
    send_bias(3)
    own_bias = pltpu.make_async_copy(tile_bias, bias_full.at[:, :, columns(x)], local_sem.at[2])
    own_bias.start()
    relay_bias(1)
    relay_planes(1)
    relay_bias(2)
    relay_planes(2)
    relay_bias(3)
    relay_planes(3)
    acts_far_up.wait_recv()
    acts_far_down.wait_recv()
    core_copies.append(send(rows(z_hi + 2), rows(z_hi + 2), partner))
    for n in range(4):
        for copy in far[n]:
            copy.wait_recv()
        whole = line(y + 2, owners[n])
        core_copies.append(send(whole, whole, partner))
    for copy in core_copies + bias_far:
        copy.wait_recv()
    own_acts.wait()
    own_bias.wait()
    out.finish()


def gather(w_query, w_key, w_value, w_out, acts, pair_tile, pair_gain, pair_weight):
    any_space = pl.BlockSpec(memory_space=pl.ANY)
    vmem = pl.BlockSpec(memory_space=pltpu.VMEM)
    return pl.pallas_call(
        gather_kernel,
        out_shape=(
            jax.ShapeDtypeStruct((4, 4, 2, 4, 24, 768), BF16),
            jax.ShapeDtypeStruct((2, 8, 64, 768), BF16),
            jax.ShapeDtypeStruct((16, 64, 512), F32),
            jax.ShapeDtypeStruct((64, 128, 128), BF16),
        ),
        in_specs=[any_space] * 5 + [vmem] * 3,
        out_specs=[any_space, any_space, any_space, vmem],
        scratch_shapes=[
            pltpu.VMEM((16, 64, 128), F32),
            pltpu.SemaphoreType.DMA((3,)),
            pltpu.SemaphoreType.DMA((63,)),
            pltpu.SemaphoreType.DMA((63,)),
        ],
        compiler_params=pltpu.CompilerParams(
            collective_id=0, has_side_effects=True, vmem_limit_bytes=VMEM_LIMIT
        ),
        name="gather",
    )(w_query, w_key, w_value, w_out, acts, pair_tile, pair_gain, pair_weight)


def reduce_kernel(
    g_ref, bias_grad_ref, normed_ref, out_ref, bias_out_ref,
    from_core, to_far, from_far, to_y, from_y, to_x, from_x, x_halves, to_z, from_z,
    own, last, from_last,
    bias_halves, bias_sent, bias_in, bias_sum, partial, partial_in, send_sem, recv_sem,
):
    y, z_lo, z_hi, core, x = place()
    z = z_hi * 2 + z_lo
    y_peers = [device((y + d) % 4, z_lo, z_hi, core, x) for d in (1, 2, 3)]
    x_peers = [device(y, z_lo, z_hi, core, (x + d) % 4) for d in (1, 2, 3)]
    z_peers = [device(y, (z + d) % 2, ((z + d) % 8) // 2, core, x) for d in range(1, 8)]
    partner = device(y, z_lo, z_hi, 1 - core, x)
    y_next, y_back, x_next, x_back = y_peers[0], y_peers[2], x_peers[0], x_peers[2]
    greet(y_peers + x_peers + z_peers + [partner])

    out = Sender(send_sem, recv_sem)
    send = out.send
    first, second = slice(0, 2), slice(2, 4)
    order = (2, 1, 3, 0)
    core_copies = {}
    for f in order:
        core_copies[f] = send(g_ref.at[:, :, 1 - core, (x + f) % 4], from_core.at[f], partner)
    far_block = bias_grad_ref.at[(x + 2) % 4]
    bias_far = [
        send(far_block.at[slice(0, 8)], bias_halves.at[0], x_next),
        send(far_block.at[slice(8, 16)], bias_halves.at[1], x_back),
    ]

    def both_cores(f, w, k):
        return g_ref[w, k, core, (x + f) % 4].astype(F32) + from_core[f, w, k].astype(F32)

    far, near = {}, {}

    def start_chunk(f):
        core_copies[f].wait_recv()

        def add(k, _):
            to_far[f, k] = both_cores(f, (y + 2) % 4, k).astype(BF16)
            return 0

        lax.fori_loop(0, 4, add, 0)
        far[f] = (
            send(to_far.at[f, first], from_far.at[0, f], y_next),
            send(to_far.at[f, second], from_far.at[1, f], y_back),
        )

    def pass_chunk(f):
        far[f][0].wait_recv()
        far[f][1].wait_recv()

        def add(k, _):
            up, down = (y + 1) % 4, (y + 3) % 4
            to_y[0, f, k] = (
                both_cores(f, up, k) + from_far[0, f, k].astype(F32)
            ).astype(BF16)
            to_y[0, f, k + 2] = both_cores(f, up, k + 2).astype(BF16)
            to_y[1, f, k] = both_cores(f, down, k).astype(BF16)
            to_y[1, f, k + 2] = (
                both_cores(f, down, k + 2) + from_far[1, f, k].astype(F32)
            ).astype(BF16)
            return 0

        lax.fori_loop(0, 2, add, 0)
        near[f] = (
            send(to_y.at[0, f], from_y.at[0, f], y_next),
            send(to_y.at[1, f], from_y.at[1, f], y_back),
        )

    start_chunk(2)
    start_chunk(1)
    pass_chunk(2)
    start_chunk(3)
    pass_chunk(1)
    start_chunk(0)
    for copy in bias_far:
        copy.wait_recv()

    def add_bias(h, _):
        up, down = (x + 1) % 4, (x + 3) % 4
        bias_sent[0, h] = (
            bias_grad_ref[up, h].astype(F32) + bias_halves[0, h].astype(F32)
        ).astype(BF16)
        bias_sent[0, h + 8] = bias_grad_ref[up, h + 8]
        bias_sent[1, h] = bias_grad_ref[down, h]
        bias_sent[1, h + 8] = (
            bias_grad_ref[down, h + 8].astype(F32) + bias_halves[1, h].astype(F32)
        ).astype(BF16)
        return 0

    lax.fori_loop(0, 8, add_bias, 0)
    bias_near = [
        send(bias_sent.at[0], bias_in.at[0], x_next),
        send(bias_sent.at[1], bias_in.at[1], x_back),
    ]
    pass_chunk(3)
    pass_chunk(0)

    for copy in bias_near:
        copy.wait_recv()

    def sum_bias(h, _):
        summed = (
            bias_grad_ref[x, h].astype(F32)
            + bias_in[0, h].astype(F32)
            + bias_in[1, h].astype(F32)
        )
        bias_sum[h] = summed.astype(BF16).astype(F32)
        return 0

    lax.fori_loop(0, 16, sum_bias, 0)

    def tile_rows(block, total):
        for u in range(8):
            i = block * 8 + u
            total = total + jnp.dot(
                bias_sum[:, i, :].astype(BF16), normed_ref[i], preferred_element_type=F32
            )
        return total

    partial[0] = lax.fori_loop(0, 8, tile_rows, jnp.zeros((16, 128), F32))
    stages = ([partner], y_peers, x_peers, z_peers)
    starts = (0, 1, 4, 7)
    in_flight = {}

    def start_stage(n):
        in_flight[n] = [
            send(partial.at[n], partial_in.at[starts[n] + d], peer)
            for d, peer in enumerate(stages[n])
        ]

    def end_stage(n):
        total = partial[n]
        for d, copy in enumerate(in_flight[n]):
            copy.wait_recv()
            total = total + partial_in[starts[n] + d]
        if n < 3:
            partial[n + 1] = total
            start_stage(n + 1)
        else:
            bias_out_ref[...] = total

    def all_planes(f, k):
        return (
            both_cores(f, y, k) + from_y[0, f, k].astype(F32) + from_y[1, f, k].astype(F32)
        )

    def wait_planes(f):
        near[f][0].wait_recv()
        near[f][1].wait_recv()

    start_stage(0)
    wait_planes(2)

    def add_far(k, _):
        to_x[2, k] = all_planes(2, k).astype(BF16)
        return 0

    lax.fori_loop(0, 4, add_far, 0)
    x_far = [
        send(to_x.at[2, first], x_halves.at[0], x_next),
        send(to_x.at[2, second], x_halves.at[1], x_back),
    ]
    end_stage(0)
    wait_planes(1)
    x_far[0].wait_recv()

    def add_up(k, _):
        to_x[0, k] = (all_planes(1, k) + x_halves[0, k].astype(F32)).astype(BF16)
        to_x[0, k + 2] = all_planes(1, k + 2).astype(BF16)
        return 0

    lax.fori_loop(0, 2, add_up, 0)
    x_up = send(to_x.at[0], from_x.at[0], x_next)
    end_stage(1)
    wait_planes(3)
    x_far[1].wait_recv()

    def add_down(k, _):
        to_x[1, k] = all_planes(3, k).astype(BF16)
        to_x[1, k + 2] = (all_planes(3, k + 2) + x_halves[1, k].astype(F32)).astype(BF16)
        return 0

    lax.fori_loop(0, 2, add_down, 0)
    x_down = send(to_x.at[1], from_x.at[1], x_back)
    end_stage(2)
    wait_planes(0)
    x_up.wait_recv()
    x_down.wait_recv()

    def add_own(k, _):
        total = all_planes(0, k) + from_x[0, k].astype(F32) + from_x[1, k].astype(F32)
        own[k] = total
        to_z[k] = total.astype(BF16)
        return 0

    lax.fori_loop(0, 4, add_own, 0)
    z_copies = []
    for d in range(7):
        target = ((z + 1 + d) % 8) // 2
        z_copies.append(send(to_z.at[target], from_z.at[d], z_peers[d]))
    end_stage(3)
    total = own[z_hi]
    for d, copy in enumerate(z_copies):
        copy.wait_recv()
        total = total + from_z[d].astype(F32)
    last[...] = total.astype(BF16)
    last_copies = [send(last, from_last.at[d], y_peers[d]) for d in range(3)]
    out_ref[y] = total.astype(BF16).astype(F32)
    for d, copy in enumerate(last_copies):
        copy.wait_recv()
        out_ref[(y + 3 - d) % 4] = from_last[d].astype(F32)
    out.finish()


def reduce_all(grads, bias_grad, normed):
    vmem = pl.BlockSpec(memory_space=pltpu.VMEM)
    return pl.pallas_call(
        reduce_kernel,
        out_shape=(
            jax.ShapeDtypeStruct((4, 24, 768), F32),
            jax.ShapeDtypeStruct((16, 128), F32),
        ),
        in_specs=[vmem] * 3,
        out_specs=[vmem] * 2,
        scratch_shapes=[
            pltpu.VMEM((4, 4, 4, 24, 768), BF16),
            pltpu.VMEM((4, 4, 24, 768), BF16),
            pltpu.VMEM((2, 4, 2, 24, 768), BF16),
            pltpu.VMEM((2, 4, 4, 24, 768), BF16),
            pltpu.VMEM((2, 4, 4, 24, 768), BF16),
            pltpu.VMEM((3, 4, 24, 768), BF16),
            pltpu.VMEM((2, 4, 24, 768), BF16),
            pltpu.VMEM((2, 2, 24, 768), BF16),
            pltpu.VMEM((4, 24, 768), BF16),
            pltpu.VMEM((7, 24, 768), BF16),
            pltpu.VMEM((4, 24, 768), F32),
            pltpu.VMEM((24, 768), BF16),
            pltpu.VMEM((3, 24, 768), BF16),
            pltpu.VMEM((2, 8, 64, 128), BF16),
            pltpu.VMEM((2, 16, 64, 128), BF16),
            pltpu.VMEM((2, 16, 64, 128), BF16),
            pltpu.VMEM((16, 64, 128), F32),
            pltpu.VMEM((4, 16, 128), F32),
            pltpu.VMEM((14, 16, 128), F32),
            pltpu.SemaphoreType.DMA((52,)),
            pltpu.SemaphoreType.DMA((52,)),
        ],
        compiler_params=pltpu.CompilerParams(
            collective_id=1, has_side_effects=True, vmem_limit_bytes=VMEM_LIMIT
        ),
        name="reduce",
    )(grads, bias_grad, normed)


def transposed_product(left, right):
    return lax.dot_general(left, right, (((0,), (0,)), ((), ())), preferred_element_type=F32)


WINDOWS = ((0, 0, 5), (128, 5, 3), (384, 8, 5), (512, 13, 3))


def head_mask(start, head):
    lanes = lax.broadcasted_iota(jnp.int32, (64, 256), 1) + start
    return (lanes >= head * 48) & (lanes < head * 48 + 48)


def attention_kernel(
    own_ref, acts_ref, cot_ref, w_ref, bias_ref, valid_ref,
    attended_ref, grads_ref, bias_grad_ref,
    query, key, value, grad, attention, query_grad, key_grad, value_grad, bias_total,
    scores, pulled, weights, probs_low, score_grad, joint,
):
    scaling = 1.0 / math.sqrt(48)
    own = own_ref[...]
    cot = cot_ref[...]
    query[...] = jnp.dot(own, w_ref[0], preferred_element_type=F32).astype(BF16)
    grad[...] = lax.dot_general(
        cot, w_ref[3], (((1,), (1,)), ((), ())), preferred_element_type=F32
    ).astype(BF16)

    def project_rows(block, _):
        rows = pl.ds(pl.multiple_of(block * 256, 256), 256)
        part = acts_ref[rows, :]
        key[rows, :] = jnp.dot(part, w_ref[1], preferred_element_type=F32).astype(BF16)
        value[rows, :] = jnp.dot(part, w_ref[2], preferred_element_type=F32).astype(BF16)
        return 0

    lax.fori_loop(0, 4, project_rows, 0)
    bias_total[...] = jnp.zeros_like(bias_total)
    attention[...] = jnp.zeros_like(attention)
    query_grad[...] = jnp.zeros_like(query_grad)
    key_grad[...] = jnp.zeros_like(key_grad)
    value_grad[...] = jnp.zeros_like(value_grad)
    keep = valid_ref[...] == 1

    def one_copy(s, _):
        q_rows = pl.ds(pl.multiple_of(s * 64, 64), 64)
        k_rows = pl.ds(pl.multiple_of(s * 512, 512), 512)
        for start, first, count in WINDOWS:
            lanes = slice(start, start + 256)
            stacked = slice(0, count * 64)
            k_win = key[k_rows, lanes]
            v_win = value[k_rows, lanes]
            q_win = query[q_rows, lanes]
            g_win = grad[q_rows, lanes]
            masks = [head_mask(start, first + n) for n in range(count)]
            zero = jnp.zeros_like(q_win)
            q_stack = jnp.concatenate([jnp.where(m, q_win, zero) for m in masks], axis=0)
            g_stack = jnp.concatenate([jnp.where(m, g_win, zero) for m in masks], axis=0)
            scores[stacked, :] = lax.dot_general(
                q_stack, k_win, (((1,), (1,)), ((), ())), preferred_element_type=F32
            )
            pulled[stacked, :] = lax.dot_general(
                g_stack, v_win, (((1,), (1,)), ((), ())), preferred_element_type=F32
            )
            inverses = []
            for n in range(count):
                rows = slice(n * 64, n * 64 + 64)
                block = scores[rows, :] * scaling + bias_ref[first + n]
                block = jnp.where(keep, block, MASKED)
                shifted = jnp.exp(block - jnp.max(block, axis=1, keepdims=True))
                inverses.append(1.0 / jnp.sum(shifted, axis=1, keepdims=True))
                scores[rows, :] = shifted
                weights[rows, :] = shifted.astype(BF16)
            merged = jnp.dot(weights[stacked, :], v_win, preferred_element_type=F32)
            attended_win = jnp.zeros((64, 256), F32)
            for n in range(count):
                attended_win = jnp.where(
                    masks[n], merged[n * 64 : n * 64 + 64] * inverses[n], attended_win
                )
            attention[q_rows, lanes] += attended_win
            product = g_win.astype(F32) * attended_win.astype(BF16).astype(F32)
            for n in range(count):
                rows = slice(n * 64, n * 64 + 64)
                delta = jnp.sum(jnp.where(masks[n], product, 0.0), axis=1, keepdims=True)
                probs = scores[rows, :] * inverses[n]
                probs_low[rows, :] = probs.astype(BF16)
                change = (probs * (pulled[rows, :] - delta)).astype(BF16)
                score_grad[rows, :] = change
                bias_total[first + n] += change.astype(F32)
            back = jnp.dot(score_grad[stacked, :], k_win, preferred_element_type=F32)
            back_win = jnp.zeros((64, 256), F32)
            for n in range(count):
                back_win = jnp.where(masks[n], back[n * 64 : n * 64 + 64], back_win)
            query_grad[q_rows, lanes] += back_win
            key_grad[k_rows, lanes] += lax.dot_general(
                score_grad[stacked, :], q_stack, (((0,), (0,)), ((), ())),
                preferred_element_type=F32,
            )
            value_grad[k_rows, lanes] += lax.dot_general(
                probs_low[stacked, :], g_stack, (((0,), (0,)), ((), ())),
                preferred_element_type=F32,
            )
        return 0

    lax.fori_loop(0, 2, one_copy, 0)
    merged_heads = attention[...].astype(BF16)
    attended_ref[...] = jnp.dot(
        merged_heads, w_ref[3], preferred_element_type=F32
    ).astype(BF16)
    q_low = (query_grad[...] * scaling).astype(BF16)
    joint[:, 0:768] = (key_grad[...] * scaling).astype(BF16)
    joint[:, 768:1536] = value_grad[...].astype(BF16)
    for block in range(3):
        lanes = slice(block * 256, block * 256 + 256)
        grads_ref[0, lanes, :] = transposed_product(own[:, lanes], q_low).astype(BF16)
        grads_ref[3, lanes, :] = transposed_product(merged_heads[:, lanes], cot).astype(BF16)
        part = acts_ref[:, lanes]
        both = transposed_product(part, joint[...]).astype(BF16)
        grads_ref[1, lanes, :] = both[:, 0:768]
        grads_ref[2, lanes, :] = both[:, 768:1536]
    for column in range(4):
        bias_grad_ref[column] = bias_total[:, :, column * 128 : column * 128 + 128].astype(BF16)


def attend(own, acts, cot, weights, bias, valid):
    vmem = pl.BlockSpec(memory_space=pltpu.VMEM)
    return pl.pallas_call(
        attention_kernel,
        out_shape=(
            jax.ShapeDtypeStruct((128, 768), BF16),
            jax.ShapeDtypeStruct((4, 768, 768), BF16),
            jax.ShapeDtypeStruct((4, 16, 64, 128), BF16),
        ),
        in_specs=[vmem] * 6,
        out_specs=[vmem] * 3,
        scratch_shapes=[
            pltpu.VMEM((128, 768), BF16),
            pltpu.VMEM((1024, 768), BF16),
            pltpu.VMEM((1024, 768), BF16),
            pltpu.VMEM((128, 768), BF16),
            pltpu.VMEM((128, 768), F32),
            pltpu.VMEM((128, 768), F32),
            pltpu.VMEM((1024, 768), F32),
            pltpu.VMEM((1024, 768), F32),
            pltpu.VMEM((16, 64, 512), F32),
            pltpu.VMEM((320, 512), F32),
            pltpu.VMEM((320, 512), F32),
            pltpu.VMEM((320, 512), BF16),
            pltpu.VMEM((320, 512), BF16),
            pltpu.VMEM((320, 512), BF16),
            pltpu.VMEM((1024, 1536), BF16),
        ],
        compiler_params=pltpu.CompilerParams(vmem_limit_bytes=VMEM_LIMIT),
        name="attend",
    )(own, acts, cot, weights, bias, valid)


def per_device(
    single, pair_features, key_valid, pair_gain, w_query, w_key, w_value, w_out, pair_bias_weight,
    out_cotangent,
):
    own_acts = single[0]
    copies, own_count, features = own_acts.shape
    w_all, acts_all, bias, normed = gather(
        w_query, w_key, w_value, w_out, own_acts,
        pair_features[0],
        pair_gain[None],
        pair_bias_weight.T,
    )
    attended, grads, bias_grad = attend(
        own_acts.reshape(copies * own_count, features),
        acts_all.reshape(copies * 512, features),
        out_cotangent[0].reshape(copies * own_count, features),
        w_all.reshape(4, features, features),
        bias,
        key_valid,
    )
    grads = grads.reshape(4, 4, 2, 4, 24, features)
    results, grad_bias = reduce_all(grads, bias_grad, normed)
    return (
        attended.reshape(1, copies, own_count, features),
        results[0], results[1], results[2], results[3], grad_bias.T,
    )


def solution(mesh):
    weight = P(("row", "col"), None)
    tokens = P("dp", "col", "row", None)
    return jax.shard_map(
        per_device,
        mesh=mesh,
        in_specs=(
            tokens, P("dp", "row", "col", None), P("dp", None), P(), weight, weight, weight, weight,
            P(), tokens,
        ),
        out_specs=(tokens, weight, weight, weight, weight, P()),
        check_vma=False,
    )
```

```python
import math

import jax
import jax.numpy as jnp
from jax import lax
from jax.experimental import pallas as pl
from jax.experimental.pallas import tpu as pltpu
from jax.sharding import PartitionSpec as P

NORM_EPSILON = 1e-05
MASKED = -1000000000.0
MESH = pl.DeviceIdType.MESH
F32 = jnp.float32
BF16 = jnp.bfloat16
VMEM_LIMIT = 56 * 1024 * 1024


def place():
    dp, row, col = lax.axis_index("dp"), lax.axis_index("row"), lax.axis_index("col")
    return dp // 2, dp % 2, row // 2, row % 2, col


def device(y, z_lo, z_hi, core, x):
    return (y * 2 + z_lo, z_hi * 2 + core, x)


def greet(peers):
    barrier = pltpu.get_barrier_semaphore()
    for peer in peers:
        pl.semaphore_signal(barrier, inc=1, device_id=peer, device_id_type=MESH)


def await_greetings(peers):
    pl.semaphore_wait(pltpu.get_barrier_semaphore(), len(peers))


class Sender:
    def __init__(self, send_sem, recv_sem):
        self.send_sem, self.recv_sem, self.started = send_sem, recv_sem, []

    def send(self, src, dst, peer):
        key = len(self.started)
        copy = pltpu.make_async_remote_copy(
            src_ref=src,
            dst_ref=dst,
            send_sem=self.send_sem.at[key],
            recv_sem=self.recv_sem.at[key],
            device_id=peer,
            device_id_type=MESH,
        )
        copy.start()
        self.started.append(copy)
        return copy

    def finish(self):
        for copy in self.started:
            copy.wait_send()


def gather_kernel(
    wq_ref, wk_ref, wv_ref, wo_ref, acts_ref, pair_ref, gain_ref, pair_weight_ref,
    w_full, acts_full, bias_full, normed_ref,
    tile_bias, pair, normed_rows, local_sem, send_sem, recv_sem,
):
    y, z_lo, z_hi, core, x = place()
    row = z_hi * 2 + core
    y_next, y_back = [device((y + d) % 4, z_lo, z_hi, core, x) for d in (1, 3)]
    x_next, x_back = [device(y, z_lo, z_hi, core, (x + d) % 4) for d in (1, 3)]
    z_peers = [device(y, z_lo, (z_hi + d) % 4, core, x) for d in (1, 2, 3)]
    z_next, z_back = z_peers[0], z_peers[2]
    partner = device(y, z_lo, z_hi, 1 - core, x)
    peers = [y_next, y_back, x_next, x_back, partner] + z_peers
    greet(peers)

    def block_rows(block):
        return slice(block * 16, block * 16 + 16)

    loads = [
        pltpu.make_async_copy(
            pair_ref.at[block_rows(b)], pair.at[block_rows(b)], local_sem.at[3 + b]
        )
        for b in range(4)
    ]
    for load in loads:
        load.start()
    stores = []
    await_greetings(peers)

    def normalize_rows(block):
        loads[block].wait()

        def one_row(k, _):
            i = block * 16 + k
            values = pair[i].astype(F32)
            center = jnp.mean(values, axis=-1, keepdims=True)
            centered = values - center
            variance = jnp.mean(centered * centered, axis=-1, keepdims=True)
            normed = (
                centered * lax.rsqrt(variance + NORM_EPSILON) * gain_ref[...]
            ).astype(BF16)
            normed_rows[i] = normed
            tile_bias[block, :, k, :] = lax.dot_general(
                pair_weight_ref[...], normed, (((1,), (1,)), ((), ())),
                preferred_element_type=F32,
            )
            return 0

        lax.fori_loop(0, 16, one_row, 0, unroll=4)
        store = pltpu.make_async_copy(
            normed_rows.at[block_rows(block)], normed_ref.at[block_rows(block)],
            local_sem.at[7 + block],
        )
        store.start()
        stores.append(store)

    def line(plane, owner, part=slice(0, 4)):
        return w_full.at[plane % 4, part, core, owner % 4]

    def rows(z_owner):
        return acts_full.at[:, (z_owner % 4) * 2 + core]

    out = Sender(send_sem, recv_sem)
    send = out.send
    first, second = slice(0, 2), slice(2, 4)
    for plane, w_ref in enumerate((wq_ref, wk_ref, wv_ref, wo_ref)):

        @pl.when(y == plane)
        def _(plane=plane, w_ref=w_ref):
            target = w_full.at[plane, z_hi, core, x]
            pltpu.make_async_copy(w_ref, target, local_sem.at[0]).start()
            for d, peer in enumerate(z_peers):
                pltpu.make_async_remote_copy(
                    src_ref=w_ref, dst_ref=target, send_sem=send_sem.at[d],
                    recv_sem=recv_sem.at[d], device_id=peer, device_id_type=MESH,
                ).start()

    own_w = pltpu.make_async_copy(wq_ref, w_full.at[y, z_hi, core, x], local_sem.at[0])
    own_acts = pltpu.make_async_copy(acts_ref, acts_full.at[:, row], local_sem.at[1])
    z_copies = [
        pltpu.make_async_remote_copy(
            src_ref=wq_ref, dst_ref=w_full.at[y, z_hi, core, x], send_sem=send_sem.at[d],
            recv_sem=recv_sem.at[d], device_id=peer, device_id_type=MESH,
        )
        for d, peer in enumerate(z_peers)
    ]
    out.started.extend(z_copies)
    own_acts.start()
    acts_up = send(acts_ref, rows(z_hi), z_next)
    acts_down = send(acts_ref, rows(z_hi), z_back)
    core_copies = [send(acts_ref, rows(z_hi), partner)]
    normalize_rows(0)

    def swap_planes(owner):
        own = line(y, owner)
        core_copies.append(send(own, own, partner))
        return send(own, own, y_next), send(own, own, y_back)

    def bias_block(owner, chunk, heads=slice(0, 16)):
        return bias_full.at[chunk, owner % 4, heads]

    bias_near, bias_far = [], []

    def send_bias(chunk):
        source = tile_bias.at[chunk]
        bias_near.append(
            (send(source, bias_block(x, chunk), x_next), send(source, bias_block(x, chunk), x_back))
        )

    def relay_bias(chunk):
        up, down = bias_near[chunk]
        up.wait_recv()
        part = bias_block(x + 3, chunk, slice(0, 8))
        bias_far.append(send(part, part, x_next))
        down.wait_recv()
        part = bias_block(x + 1, chunk, slice(8, 16))
        bias_far.append(send(part, part, x_back))

    own_w.wait()
    for copy in z_copies:
        copy.wait_recv()
    own = line(y, x)
    x_up = send(own, own, x_next)
    x_down = send(own, own, x_back)
    planes = [swap_planes(x)]
    send_bias(0)
    normalize_rows(1)
    send_bias(1)
    x_up.wait_recv()
    part = line(y, x + 3, first)
    x_far_up = send(part, part, x_next)
    x_down.wait_recv()
    part = line(y, x + 1, second)
    x_far_down = send(part, part, x_back)
    planes.append(swap_planes(x + 3))
    planes.append(swap_planes(x + 1))
    normalize_rows(2)
    send_bias(2)
    acts_up.wait_recv()
    part = acts_full.at[0, ((z_hi + 3) % 4) * 2 + core]
    acts_far_up = send(part, part, z_next)
    acts_down.wait_recv()
    part = acts_full.at[1, ((z_hi + 1) % 4) * 2 + core]
    acts_far_down = send(part, part, z_back)
    core_copies.append(send(rows(z_hi + 3), rows(z_hi + 3), partner))
    core_copies.append(send(rows(z_hi + 1), rows(z_hi + 1), partner))
    relay_bias(0)
    x_far_up.wait_recv()
    x_far_down.wait_recv()
    planes.append(swap_planes(x + 2))
    owners = (x, x + 3, x + 1, x + 2)
    far = []

    def relay_planes(n):
        up, down = planes[n]
        owner = owners[n]
        up.wait_recv()
        part = line(y + 3, owner, first)
        far_up = send(part, part, y_next)
        down.wait_recv()
        part = line(y + 1, owner, second)
        far.append((far_up, send(part, part, y_back)))
        for plane in (y + 3, y + 1):
            whole = line(plane, owner)
            core_copies.append(send(whole, whole, partner))

    relay_planes(0)
    normalize_rows(3)
    send_bias(3)
    own_bias = pltpu.make_async_copy(tile_bias, bias_full.at[:, x], local_sem.at[2])
    own_bias.start()
    relay_bias(1)
    relay_planes(1)
    relay_bias(2)
    relay_planes(2)
    relay_bias(3)
    relay_planes(3)
    acts_far_up.wait_recv()
    acts_far_down.wait_recv()
    core_copies.append(send(rows(z_hi + 2), rows(z_hi + 2), partner))
    for n in range(4):
        for copy in far[n]:
            copy.wait_recv()
        whole = line(y + 2, owners[n])
        core_copies.append(send(whole, whole, partner))
    for copy in core_copies + bias_far:
        copy.wait_recv()
    own_acts.wait()
    own_bias.wait()
    for store in stores:
        store.wait()
    out.finish()


def gather(w_query, w_key, w_value, w_out, acts, pair_tile, pair_gain, pair_weight):
    any_space = pl.BlockSpec(memory_space=pl.ANY)
    vmem = pl.BlockSpec(memory_space=pltpu.VMEM)
    return pl.pallas_call(
        gather_kernel,
        out_shape=(
            jax.ShapeDtypeStruct((4, 4, 2, 4, 24, 768), BF16),
            jax.ShapeDtypeStruct((2, 8, 64, 768), BF16),
            jax.ShapeDtypeStruct((4, 4, 16, 16, 128), F32),
            jax.ShapeDtypeStruct((64, 128, 128), BF16),
        ),
        in_specs=[any_space] * 6 + [vmem] * 2,
        out_specs=[any_space] * 4,
        scratch_shapes=[
            pltpu.VMEM((4, 16, 16, 128), F32),
            pltpu.VMEM((64, 128, 128), BF16),
            pltpu.VMEM((64, 128, 128), BF16),
            pltpu.SemaphoreType.DMA((11,)),
            pltpu.SemaphoreType.DMA((63,)),
            pltpu.SemaphoreType.DMA((63,)),
        ],
        compiler_params=pltpu.CompilerParams(
            collective_id=0, has_side_effects=True, vmem_limit_bytes=VMEM_LIMIT
        ),
        name="gather",
    )(w_query, w_key, w_value, w_out, acts, pair_tile, pair_gain, pair_weight)


def transposed_product(left, right):
    return lax.dot_general(left, right, (((0,), (0,)), ((), ())), preferred_element_type=F32)


WINDOWS = ((0, 0, 5), (128, 5, 3), (384, 8, 5), (512, 13, 3))


def head_mask(start, head):
    lanes = lax.broadcasted_iota(jnp.int32, (64, 256), 1) + start
    return (lanes >= head * 48) & (lanes < head * 48 + 48)


def attention_kernel(
    own_ref, cot_ref, valid_ref, acts_hbm, w_hbm, bias_hbm, normed_hbm,
    attended_ref, gq_ref, gk_ref, gv_ref, go_ref, bias_out_ref,
    acts_ref, w_ref, bias_ref, normed_ref,
    query, key, value, grad, attention, query_grad, key_grad, value_grad, bias_total,
    scores, pulled, weights, probs_low, score_grad, joint, bias_grad,
    g_ref, from_core, to_far, from_far, to_y, from_y, to_x, from_x, x_halves, to_z, from_z,
    own_sum, last, from_last, results,
    bias_halves, bias_sent, bias_in, bias_sum, partial, partial_in,
    local_sem, send_sem, recv_sem,
):
    y, z_lo, z_hi, core, x = place()
    z = z_hi * 2 + z_lo
    y_peers = [device((y + d) % 4, z_lo, z_hi, core, x) for d in (1, 2, 3)]
    x_peers = [device(y, z_lo, z_hi, core, (x + d) % 4) for d in (1, 2, 3)]
    z_peers = [device(y, (z + d) % 2, ((z + d) % 8) // 2, core, x) for d in range(1, 8)]
    partner = device(y, z_lo, z_hi, 1 - core, x)
    y_next, y_back, x_next, x_back = y_peers[0], y_peers[2], x_peers[0], x_peers[2]
    peers = y_peers + x_peers + z_peers + [partner]
    greet(peers)

    load_acts = pltpu.make_async_copy(acts_hbm, acts_ref, local_sem.at[0])
    load_w = [
        pltpu.make_async_copy(w_hbm.at[n], w_ref.at[n], local_sem.at[1 + n]) for n in range(4)
    ]
    load_bias = pltpu.make_async_copy(bias_hbm, bias_ref, local_sem.at[5])
    load_normed = pltpu.make_async_copy(normed_hbm, normed_ref, local_sem.at[6])
    load_w[3].start()
    load_w[0].start()
    load_acts.start()
    load_w[1].start()
    load_w[2].start()
    load_bias.start()
    load_normed.start()

    scaling = 1.0 / math.sqrt(48)
    own = own_ref[...]
    cot = cot_ref[...]
    bias_total[...] = jnp.zeros_like(bias_total)
    attention[...] = jnp.zeros_like(attention)
    query_grad[...] = jnp.zeros_like(query_grad)
    key_grad[...] = jnp.zeros_like(key_grad)
    value_grad[...] = jnp.zeros_like(value_grad)
    load_w[3].wait()
    grad[...] = lax.dot_general(
        cot, w_ref[3], (((1,), (1,)), ((), ())), preferred_element_type=F32
    ).astype(BF16)
    load_w[0].wait()
    query[...] = jnp.dot(own, w_ref[0], preferred_element_type=F32).astype(BF16)
    load_acts.wait()
    load_w[1].wait()
    load_w[2].wait()

    def project_rows(block, _):
        rows = pl.ds(pl.multiple_of(block * 256, 256), 256)
        part = acts_ref[rows, :]
        key[rows, :] = jnp.dot(part, w_ref[1], preferred_element_type=F32).astype(BF16)
        value[rows, :] = jnp.dot(part, w_ref[2], preferred_element_type=F32).astype(BF16)
        return 0

    lax.fori_loop(0, 4, project_rows, 0)
    load_bias.wait()
    keep = valid_ref[...] == 1

    def head_bias(head):
        return jnp.concatenate(
            [
                jnp.concatenate([bias_ref[r, c, head] for c in range(4)], axis=1)
                for r in range(4)
            ],
            axis=0,
        )

    def one_copy(s, _):
        q_rows = pl.ds(pl.multiple_of(s * 64, 64), 64)
        k_rows = pl.ds(pl.multiple_of(s * 512, 512), 512)
        for start, first, count in WINDOWS:
            lanes = slice(start, start + 256)
            stacked = slice(0, count * 64)
            k_win = key[k_rows, lanes]
            v_win = value[k_rows, lanes]
            q_win = query[q_rows, lanes]
            g_win = grad[q_rows, lanes]
            masks = [head_mask(start, first + n) for n in range(count)]
            zero = jnp.zeros_like(q_win)
            q_stack = jnp.concatenate([jnp.where(m, q_win, zero) for m in masks], axis=0)
            g_stack = jnp.concatenate([jnp.where(m, g_win, zero) for m in masks], axis=0)
            scores[stacked, :] = lax.dot_general(
                q_stack, k_win, (((1,), (1,)), ((), ())), preferred_element_type=F32
            )
            pulled[stacked, :] = lax.dot_general(
                g_stack, v_win, (((1,), (1,)), ((), ())), preferred_element_type=F32
            )
            inverses = []
            for n in range(count):
                rows = slice(n * 64, n * 64 + 64)
                block = scores[rows, :] * scaling + head_bias(first + n)
                block = jnp.where(keep, block, MASKED)
                shifted = jnp.exp(block - jnp.max(block, axis=1, keepdims=True))
                inverses.append(1.0 / jnp.sum(shifted, axis=1, keepdims=True))
                scores[rows, :] = shifted
                weights[rows, :] = shifted.astype(BF16)
            merged = jnp.dot(weights[stacked, :], v_win, preferred_element_type=F32)
            attended_win = jnp.zeros((64, 256), F32)
            for n in range(count):
                attended_win = jnp.where(
                    masks[n], merged[n * 64 : n * 64 + 64] * inverses[n], attended_win
                )
            attention[q_rows, lanes] += attended_win
            product = g_win.astype(F32) * attended_win.astype(BF16).astype(F32)
            for n in range(count):
                rows = slice(n * 64, n * 64 + 64)
                delta = jnp.sum(jnp.where(masks[n], product, 0.0), axis=1, keepdims=True)
                probs = scores[rows, :] * inverses[n]
                probs_low[rows, :] = probs.astype(BF16)
                change = (probs * (pulled[rows, :] - delta)).astype(BF16)
                score_grad[rows, :] = change
                bias_total[first + n] += change.astype(F32)
            back = jnp.dot(score_grad[stacked, :], k_win, preferred_element_type=F32)
            back_win = jnp.zeros((64, 256), F32)
            for n in range(count):
                back_win = jnp.where(masks[n], back[n * 64 : n * 64 + 64], back_win)
            query_grad[q_rows, lanes] += back_win
            key_grad[k_rows, lanes] += lax.dot_general(
                score_grad[stacked, :], q_stack, (((0,), (0,)), ((), ())),
                preferred_element_type=F32,
            )
            value_grad[k_rows, lanes] += lax.dot_general(
                probs_low[stacked, :], g_stack, (((0,), (0,)), ((), ())),
                preferred_element_type=F32,
            )
        return 0

    lax.fori_loop(0, 2, one_copy, 0)
    await_greetings(peers)
    out = Sender(send_sem, recv_sem)
    send = out.send

    for column in range(4):
        bias_grad[column] = bias_total[:, :, column * 128 : column * 128 + 128].astype(BF16)
    far_block = bias_grad.at[(x + 2) % 4]
    bias_far = [
        send(far_block.at[slice(0, 8)], bias_halves.at[0], x_next),
        send(far_block.at[slice(8, 16)], bias_halves.at[1], x_back),
    ]

    merged_heads = attention[...].astype(BF16)
    q_low = (query_grad[...] * scaling).astype(BF16)
    joint[:, 0:768] = (key_grad[...] * scaling).astype(BF16)
    joint[:, 768:1536] = value_grad[...].astype(BF16)
    core_copies = {}

    def store_grads(w, half, product):
        g_ref[w, 2 * half : 2 * half + 2] = product.reshape(2, 2, 4, 24, 768).astype(BF16)
        part = slice(2 * half, 2 * half + 2)
        core_copies[w, half] = send(
            g_ref.at[w, part, 1 - core], from_core.at[w, part], partner
        )

    def own_products(half):
        lanes = slice(half * 384, half * 384 + 384)
        store_grads(3, half, transposed_product(merged_heads[:, lanes], cot))
        store_grads(0, half, transposed_product(own[:, lanes], q_low))

    def all_products(half):
        lanes = slice(half * 384, half * 384 + 384)
        both = transposed_product(acts_ref[:, lanes], joint[...])
        store_grads(1, half, both[:, 0:768])
        store_grads(2, half, both[:, 768:1536])

    def both_cores(f, w, k):
        c = (x + f) % 4
        return g_ref[w, k, core, c].astype(F32) + from_core[w, k, c].astype(F32)

    far, near = {}, {}

    def start_chunk(half, f):
        if f == 2:
            for w in range(4):
                core_copies[w, half].wait_recv()
        for k in (2 * half, 2 * half + 1):
            to_far[f, k] = both_cores(f, (y + 2) % 4, k).astype(BF16)
        far[half, f] = (
            send(to_far.at[f, 2 * half], from_far.at[0, half, f], y_next),
            send(to_far.at[f, 2 * half + 1], from_far.at[1, half, f], y_back),
        )

    def pass_chunk(half, f):
        up, down = (y + 1) % 4, (y + 3) % 4
        one, two = 2 * half, 2 * half + 1
        to_y[0, half, f, 1] = both_cores(f, up, two).astype(BF16)
        to_y[1, half, f, 0] = both_cores(f, down, one).astype(BF16)
        far[half, f][0].wait_recv()
        to_y[0, half, f, 0] = (
            both_cores(f, up, one) + from_far[0, half, f].astype(F32)
        ).astype(BF16)
        up_copy = send(to_y.at[0, half, f], from_y.at[0, half, f], y_next)
        far[half, f][1].wait_recv()
        to_y[1, half, f, 1] = (
            both_cores(f, down, two) + from_far[1, half, f].astype(F32)
        ).astype(BF16)
        near[half, f] = (up_copy, send(to_y.at[1, half, f], from_y.at[1, half, f], y_back))

    own_products(0)
    all_products(0)
    own_products(1)
    start_chunk(0, 2)
    start_chunk(0, 1)
    all_products(1)
    pass_chunk(0, 2)
    start_chunk(0, 3)
    pass_chunk(0, 1)
    start_chunk(0, 0)
    for copy in bias_far:
        copy.wait_recv()

    def add_bias(h, _):
        up, down = (x + 1) % 4, (x + 3) % 4
        bias_sent[0, h] = (
            bias_grad[up, h].astype(F32) + bias_halves[0, h].astype(F32)
        ).astype(BF16)
        bias_sent[0, h + 8] = bias_grad[up, h + 8]
        bias_sent[1, h] = bias_grad[down, h]
        bias_sent[1, h + 8] = (
            bias_grad[down, h + 8].astype(F32) + bias_halves[1, h].astype(F32)
        ).astype(BF16)
        return 0

    lax.fori_loop(0, 8, add_bias, 0)
    bias_near = [
        send(bias_sent.at[0], bias_in.at[0], x_next),
        send(bias_sent.at[1], bias_in.at[1], x_back),
    ]
    pass_chunk(0, 3)
    pass_chunk(0, 0)
    attended_ref[...] = jnp.dot(merged_heads, w_ref[3], preferred_element_type=F32).astype(BF16)
    start_chunk(1, 2)
    start_chunk(1, 1)
    pass_chunk(1, 2)
    start_chunk(1, 3)
    pass_chunk(1, 1)
    start_chunk(1, 0)
    pass_chunk(1, 3)

    for copy in bias_near:
        copy.wait_recv()

    def sum_bias(h, _):
        summed = (
            bias_grad[x, h].astype(F32) + bias_in[0, h].astype(F32) + bias_in[1, h].astype(F32)
        )
        bias_sum[h] = summed.astype(BF16).astype(F32)
        return 0

    lax.fori_loop(0, 16, sum_bias, 0)
    load_normed.wait()

    def tile_rows(block, total):
        for u in range(8):
            i = block * 8 + u
            total = total + jnp.dot(
                bias_sum[:, i, :].astype(BF16), normed_ref[i], preferred_element_type=F32
            )
        return total

    early = lax.fori_loop(0, 4, tile_rows, jnp.zeros((16, 128), F32))
    pass_chunk(1, 0)
    partial[0] = lax.fori_loop(4, 8, tile_rows, early)
    stages = ([partner], y_peers, x_peers, z_peers)
    starts = (0, 1, 4, 7)
    in_flight = {}

    def start_stage(n):
        in_flight[n] = [
            send(partial.at[n], partial_in.at[starts[n] + d], peer)
            for d, peer in enumerate(stages[n])
        ]

    def end_stage(n):
        total = partial[n]
        for d, copy in enumerate(in_flight[n]):
            copy.wait_recv()
            total = total + partial_in[starts[n] + d]
        if n < 3:
            partial[n + 1] = total
            start_stage(n + 1)
        else:
            bias_out_ref[...] = total.T

    def all_planes(half, f, n):
        return (
            both_cores(f, y, 2 * half + n)
            + from_y[0, half, f, n].astype(F32)
            + from_y[1, half, f, n].astype(F32)
        )

    def wait_planes(half, f):
        near[half, f][0].wait_recv()
        near[half, f][1].wait_recv()

    x_far, x_near = {}, {}

    def start_column(half):
        wait_planes(half, 2)
        for n in range(2):
            to_x[2, half, n] = all_planes(half, 2, n).astype(BF16)
        x_far[half] = (
            send(to_x.at[2, half, 0], x_halves.at[0, half], x_next),
            send(to_x.at[2, half, 1], x_halves.at[1, half], x_back),
        )

    def pass_column(half):
        wait_planes(half, 1)
        to_x[0, half, 1] = all_planes(half, 1, 1).astype(BF16)
        x_far[half][0].wait_recv()
        to_x[0, half, 0] = (
            all_planes(half, 1, 0) + x_halves[0, half].astype(F32)
        ).astype(BF16)
        up = send(to_x.at[0, half], from_x.at[0, half], x_next)
        wait_planes(half, 3)
        to_x[1, half, 0] = all_planes(half, 3, 0).astype(BF16)
        x_far[half][1].wait_recv()
        to_x[1, half, 1] = (
            all_planes(half, 3, 1) + x_halves[1, half].astype(F32)
        ).astype(BF16)
        x_near[half] = (up, send(to_x.at[1, half], from_x.at[1, half], x_back))

    def end_column(half):
        wait_planes(half, 0)
        for copy in x_near[half]:
            copy.wait_recv()
        for n in range(2):
            total = (
                all_planes(half, 0, n)
                + from_x[0, half, n].astype(F32)
                + from_x[1, half, n].astype(F32)
            )
            own_sum[2 * half + n] = total
            to_z[2 * half + n] = total.astype(BF16)

    start_stage(0)
    start_column(0)
    end_stage(0)
    pass_column(0)
    end_stage(1)
    start_column(1)
    pass_column(1)
    end_column(0)
    end_stage(2)
    end_column(1)
    z_copies = []
    for d in range(7):
        target = ((z + 1 + d) % 8) // 2
        z_copies.append(send(to_z.at[target], from_z.at[d], z_peers[d]))
    end_stage(3)
    total = own_sum[z_hi]
    for d, copy in enumerate(z_copies):
        copy.wait_recv()
        total = total + from_z[d].astype(F32)
    last[...] = total.astype(BF16)
    last_copies = [send(last, from_last.at[d], y_peers[d]) for d in range(3)]
    results[y] = total.astype(BF16).astype(F32)
    for d, copy in enumerate(last_copies):
        copy.wait_recv()
        results[(y + 3 - d) % 4] = from_last[d].astype(F32)
    for n, ref in enumerate((gq_ref, gk_ref, gv_ref, go_ref)):
        ref[...] = results[n]
    out.finish()


def attend(own, cot, valid, acts, weights, bias, normed):
    vmem = pl.BlockSpec(memory_space=pltpu.VMEM)
    any_space = pl.BlockSpec(memory_space=pl.ANY)
    grads = jax.ShapeDtypeStruct((24, 768), F32)
    return pl.pallas_call(
        attention_kernel,
        out_shape=(
            jax.ShapeDtypeStruct((128, 768), BF16),
            grads, grads, grads, grads,
            jax.ShapeDtypeStruct((128, 16), F32),
        ),
        in_specs=[vmem] * 3 + [any_space] * 4,
        out_specs=[vmem] * 6,
        scratch_shapes=[
            pltpu.VMEM((1024, 768), BF16),
            pltpu.VMEM((4, 768, 768), BF16),
            pltpu.VMEM((4, 4, 16, 16, 128), F32),
            pltpu.VMEM((64, 128, 128), BF16),
            pltpu.VMEM((128, 768), BF16),
            pltpu.VMEM((1024, 768), BF16),
            pltpu.VMEM((1024, 768), BF16),
            pltpu.VMEM((128, 768), BF16),
            pltpu.VMEM((128, 768), F32),
            pltpu.VMEM((128, 768), F32),
            pltpu.VMEM((1024, 768), F32),
            pltpu.VMEM((1024, 768), F32),
            pltpu.VMEM((16, 64, 512), F32),
            pltpu.VMEM((320, 512), F32),
            pltpu.VMEM((320, 512), F32),
            pltpu.VMEM((320, 512), BF16),
            pltpu.VMEM((320, 512), BF16),
            pltpu.VMEM((320, 512), BF16),
            pltpu.VMEM((1024, 1536), BF16),
            pltpu.VMEM((4, 16, 64, 128), BF16),
            pltpu.VMEM((4, 4, 2, 4, 24, 768), BF16),
            pltpu.VMEM((4, 4, 4, 24, 768), BF16),
            pltpu.VMEM((4, 4, 24, 768), BF16),
            pltpu.VMEM((2, 2, 4, 24, 768), BF16),
            pltpu.VMEM((2, 2, 4, 2, 24, 768), BF16),
            pltpu.VMEM((2, 2, 4, 2, 24, 768), BF16),
            pltpu.VMEM((3, 2, 2, 24, 768), BF16),
            pltpu.VMEM((2, 2, 2, 24, 768), BF16),
            pltpu.VMEM((2, 2, 24, 768), BF16),
            pltpu.VMEM((4, 24, 768), BF16),
            pltpu.VMEM((7, 24, 768), BF16),
            pltpu.VMEM((4, 24, 768), F32),
            pltpu.VMEM((24, 768), BF16),
            pltpu.VMEM((3, 24, 768), BF16),
            pltpu.VMEM((4, 24, 768), F32),
            pltpu.VMEM((2, 8, 64, 128), BF16),
            pltpu.VMEM((2, 16, 64, 128), BF16),
            pltpu.VMEM((2, 16, 64, 128), BF16),
            pltpu.VMEM((16, 64, 128), F32),
            pltpu.VMEM((4, 16, 128), F32),
            pltpu.VMEM((14, 16, 128), F32),
            pltpu.SemaphoreType.DMA((7,)),
            pltpu.SemaphoreType.DMA((76,)),
            pltpu.SemaphoreType.DMA((76,)),
        ],
        compiler_params=pltpu.CompilerParams(
            collective_id=1, has_side_effects=True, vmem_limit_bytes=VMEM_LIMIT
        ),
        name="attend",
    )(own, cot, valid, acts, weights, bias, normed)


def per_device(
    single, pair_features, key_valid, pair_gain, w_query, w_key, w_value, w_out, pair_bias_weight,
    out_cotangent,
):
    own_acts = single[0]
    copies, own_count, features = own_acts.shape
    w_all, acts_all, bias, normed = gather(
        w_query, w_key, w_value, w_out, own_acts,
        pair_features[0],
        pair_gain[None],
        pair_bias_weight.T,
    )
    attended, grad_query, grad_key, grad_value, grad_out, grad_bias = attend(
        own_acts.reshape(copies * own_count, features),
        out_cotangent[0].reshape(copies * own_count, features),
        key_valid,
        acts_all.reshape(copies * 512, features),
        w_all.reshape(4, features, features),
        bias,
        normed,
    )
    attended = attended.reshape(1, copies, own_count, features)
    return (attended, grad_query, grad_key, grad_value, grad_out, grad_bias)


def solution(mesh):
    weight = P(("row", "col"), None)
    tokens = P("dp", "col", "row", None)
    return jax.shard_map(
        per_device,
        mesh=mesh,
        in_specs=(
            tokens, P("dp", "row", "col", None), P("dp", None), P(), weight, weight, weight, weight,
            P(), tokens,
        ),
        out_specs=(tokens, weight, weight, weight, weight, P()),
        check_vma=False,
    )
```

```python
import math

import jax
import jax.numpy as jnp
from jax import lax
from jax.experimental import pallas as pl
from jax.experimental.pallas import tpu as pltpu
from jax.sharding import PartitionSpec as P

NORM_EPSILON = 1e-05
MASKED = -1000000000.0
MESH = pl.DeviceIdType.MESH
F32 = jnp.float32
BF16 = jnp.bfloat16
VMEM_LIMIT = 56 * 1024 * 1024


def place():
    dp, row, col = lax.axis_index("dp"), lax.axis_index("row"), lax.axis_index("col")
    return dp // 2, dp % 2, row // 2, row % 2, col


def device(y, z_lo, z_hi, core, x):
    return (y * 2 + z_lo, z_hi * 2 + core, x)


def greet(peers):
    barrier = pltpu.get_barrier_semaphore()
    for peer in peers:
        pl.semaphore_signal(barrier, inc=1, device_id=peer, device_id_type=MESH)


def await_greetings(peers):
    pl.semaphore_wait(pltpu.get_barrier_semaphore(), len(peers))


class Sender:
    def __init__(self, send_sem, recv_sem):
        self.send_sem, self.recv_sem, self.started = send_sem, recv_sem, []

    def send(self, src, dst, peer):
        key = len(self.started)
        copy = pltpu.make_async_remote_copy(
            src_ref=src,
            dst_ref=dst,
            send_sem=self.send_sem.at[key],
            recv_sem=self.recv_sem.at[key],
            device_id=peer,
            device_id_type=MESH,
        )
        copy.start()
        self.started.append(copy)
        return copy

    def finish(self):
        for copy in self.started:
            copy.wait_send()


def gather_kernel(
    wq_ref, wk_ref, wv_ref, wo_ref, acts_ref, pair_ref, gain_ref, pair_weight_ref,
    w_full, acts_full, bias_full, normed_ref,
    tile_bias, pair, normed_rows, local_sem, send_sem, recv_sem,
):
    y, z_lo, z_hi, core, x = place()
    row = z_hi * 2 + core
    y_next, y_back = [device((y + d) % 4, z_lo, z_hi, core, x) for d in (1, 3)]
    x_next, x_back = [device(y, z_lo, z_hi, core, (x + d) % 4) for d in (1, 3)]
    z_peers = [device(y, z_lo, (z_hi + d) % 4, core, x) for d in (1, 2, 3)]
    z_next, z_back = z_peers[0], z_peers[2]
    partner = device(y, z_lo, z_hi, 1 - core, x)
    peers = [y_next, y_back, x_next, x_back, partner] + z_peers
    greet(peers)

    def block_rows(block):
        return slice(block * 16, block * 16 + 16)

    loads = [
        pltpu.make_async_copy(
            pair_ref.at[block_rows(b)], pair.at[block_rows(b)], local_sem.at[3 + b]
        )
        for b in range(4)
    ]
    for load in loads:
        load.start()
    stores = []
    await_greetings(peers)

    def normalize_rows(block):
        loads[block].wait()

        def one_row(k, _):
            i = block * 16 + k
            values = pair[i].astype(F32)
            center = jnp.mean(values, axis=-1, keepdims=True)
            centered = values - center
            variance = jnp.mean(centered * centered, axis=-1, keepdims=True)
            normed = (
                centered * lax.rsqrt(variance + NORM_EPSILON) * gain_ref[...]
            ).astype(BF16)
            normed_rows[i] = normed
            tile_bias[block, :, k, :] = lax.dot_general(
                pair_weight_ref[...], normed, (((1,), (1,)), ((), ())),
                preferred_element_type=F32,
            )
            return 0

        lax.fori_loop(0, 16, one_row, 0, unroll=4)
        store = pltpu.make_async_copy(
            normed_rows.at[block_rows(block)], normed_ref.at[block_rows(block)],
            local_sem.at[7 + block],
        )
        store.start()
        stores.append(store)

    def line(plane, owner, part=slice(0, 4)):
        return w_full.at[plane % 4, part, core, owner % 4]

    def rows(z_owner):
        return acts_full.at[:, (z_owner % 4) * 2 + core]

    out = Sender(send_sem, recv_sem)
    send = out.send
    first, second = slice(0, 2), slice(2, 4)
    for plane, w_ref in enumerate((wq_ref, wk_ref, wv_ref, wo_ref)):

        @pl.when(y == plane)
        def _(plane=plane, w_ref=w_ref):
            target = w_full.at[plane, z_hi, core, x]
            pltpu.make_async_copy(w_ref, target, local_sem.at[0]).start()
            for d, peer in enumerate(z_peers):
                pltpu.make_async_remote_copy(
                    src_ref=w_ref, dst_ref=target, send_sem=send_sem.at[d],
                    recv_sem=recv_sem.at[d], device_id=peer, device_id_type=MESH,
                ).start()

    own_w = pltpu.make_async_copy(wq_ref, w_full.at[y, z_hi, core, x], local_sem.at[0])
    own_acts = pltpu.make_async_copy(acts_ref, acts_full.at[:, row], local_sem.at[1])
    z_copies = [
        pltpu.make_async_remote_copy(
            src_ref=wq_ref, dst_ref=w_full.at[y, z_hi, core, x], send_sem=send_sem.at[d],
            recv_sem=recv_sem.at[d], device_id=peer, device_id_type=MESH,
        )
        for d, peer in enumerate(z_peers)
    ]
    out.started.extend(z_copies)
    own_acts.start()
    acts_up = send(acts_ref, rows(z_hi), z_next)
    acts_down = send(acts_ref, rows(z_hi), z_back)
    core_copies = [send(acts_ref, rows(z_hi), partner)]
    normalize_rows(0)

    def swap_planes(owner):
        own = line(y, owner)
        core_copies.append(send(own, own, partner))
        return send(own, own, y_next), send(own, own, y_back)

    def bias_block(owner, chunk, heads=slice(0, 16)):
        return bias_full.at[chunk, owner % 4, heads]

    bias_near, bias_far = [], []

    def send_bias(chunk):
        source = tile_bias.at[chunk]
        bias_near.append(
            (send(source, bias_block(x, chunk), x_next), send(source, bias_block(x, chunk), x_back))
        )

    def relay_bias(chunk):
        up, down = bias_near[chunk]
        up.wait_recv()
        part = bias_block(x + 3, chunk, slice(0, 8))
        bias_far.append(send(part, part, x_next))
        down.wait_recv()
        part = bias_block(x + 1, chunk, slice(8, 16))
        bias_far.append(send(part, part, x_back))

    own_w.wait()
    for copy in z_copies:
        copy.wait_recv()
    own = line(y, x)
    x_up = send(own, own, x_next)
    x_down = send(own, own, x_back)
    planes = [swap_planes(x)]
    send_bias(0)
    normalize_rows(1)
    send_bias(1)
    x_up.wait_recv()
    part = line(y, x + 3, first)
    x_far_up = send(part, part, x_next)
    x_down.wait_recv()
    part = line(y, x + 1, second)
    x_far_down = send(part, part, x_back)
    planes.append(swap_planes(x + 3))
    planes.append(swap_planes(x + 1))
    normalize_rows(2)
    send_bias(2)
    acts_up.wait_recv()
    part = acts_full.at[0, ((z_hi + 3) % 4) * 2 + core]
    acts_far_up = send(part, part, z_next)
    acts_down.wait_recv()
    part = acts_full.at[1, ((z_hi + 1) % 4) * 2 + core]
    acts_far_down = send(part, part, z_back)
    core_copies.append(send(rows(z_hi + 3), rows(z_hi + 3), partner))
    core_copies.append(send(rows(z_hi + 1), rows(z_hi + 1), partner))
    relay_bias(0)
    x_far_up.wait_recv()
    x_far_down.wait_recv()
    planes.append(swap_planes(x + 2))
    owners = (x, x + 3, x + 1, x + 2)
    far = []

    def relay_planes(n):
        up, down = planes[n]
        owner = owners[n]
        up.wait_recv()
        part = line(y + 3, owner, first)
        far_up = send(part, part, y_next)
        down.wait_recv()
        part = line(y + 1, owner, second)
        far.append((far_up, send(part, part, y_back)))
        for plane in (y + 3, y + 1):
            whole = line(plane, owner)
            core_copies.append(send(whole, whole, partner))

    relay_planes(0)
    normalize_rows(3)
    send_bias(3)
    own_bias = pltpu.make_async_copy(tile_bias, bias_full.at[:, x], local_sem.at[2])
    own_bias.start()
    relay_bias(1)
    relay_planes(1)
    relay_bias(2)
    relay_planes(2)
    relay_bias(3)
    relay_planes(3)
    acts_far_up.wait_recv()
    acts_far_down.wait_recv()
    core_copies.append(send(rows(z_hi + 2), rows(z_hi + 2), partner))
    for n in range(4):
        for copy in far[n]:
            copy.wait_recv()
        whole = line(y + 2, owners[n])
        core_copies.append(send(whole, whole, partner))
    for copy in core_copies + bias_far:
        copy.wait_recv()
    own_acts.wait()
    own_bias.wait()
    for store in stores:
        store.wait()
    out.finish()


def gather(w_query, w_key, w_value, w_out, acts, pair_tile, pair_gain, pair_weight):
    any_space = pl.BlockSpec(memory_space=pl.ANY)
    vmem = pl.BlockSpec(memory_space=pltpu.VMEM)
    return pl.pallas_call(
        gather_kernel,
        out_shape=(
            jax.ShapeDtypeStruct((4, 4, 2, 4, 24, 768), BF16),
            jax.ShapeDtypeStruct((2, 8, 64, 768), BF16),
            jax.ShapeDtypeStruct((4, 4, 16, 16, 128), F32),
            jax.ShapeDtypeStruct((64, 128, 128), BF16),
        ),
        in_specs=[any_space] * 6 + [vmem] * 2,
        out_specs=[any_space] * 4,
        scratch_shapes=[
            pltpu.VMEM((4, 16, 16, 128), F32),
            pltpu.VMEM((64, 128, 128), BF16),
            pltpu.VMEM((64, 128, 128), BF16),
            pltpu.SemaphoreType.DMA((11,)),
            pltpu.SemaphoreType.DMA((63,)),
            pltpu.SemaphoreType.DMA((63,)),
        ],
        compiler_params=pltpu.CompilerParams(
            collective_id=0, has_side_effects=True, vmem_limit_bytes=VMEM_LIMIT
        ),
        name="gather",
    )(w_query, w_key, w_value, w_out, acts, pair_tile, pair_gain, pair_weight)


def transposed_product(left, right):
    return lax.dot_general(left, right, (((0,), (0,)), ((), ())), preferred_element_type=F32)


WINDOWS = ((0, 0, 5), (128, 5, 3), (384, 8, 5), (512, 13, 3))


def head_mask(start, head):
    lanes = lax.broadcasted_iota(jnp.int32, (64, 256), 1) + start
    return (lanes >= head * 48) & (lanes < head * 48 + 48)


def attention_kernel(
    own_ref, cot_ref, valid_ref, acts_hbm, w_hbm, bias_hbm, normed_hbm,
    attended_ref, results, bias_out_ref,
    acts_ref, w_ref, bias_ref, normed_ref,
    query, key, value, grad, attention, query_grad, key_grad, value_grad, bias_total,
    scores, pulled, weights, probs_low, score_grad, joint, bias_grad,
    g_ref, from_core, to_far, from_far, to_y, from_y, to_x, from_x, x_halves,
    own_sum, to_pair, from_pair, to_z, from_z, last, from_last,
    bias_halves, bias_sent, bias_in, bias_sum, partial, partial_in,
    local_sem, send_sem, recv_sem,
):
    y, z_lo, z_hi, core, x = place()
    y_peers = [device((y + d) % 4, z_lo, z_hi, core, x) for d in (1, 2, 3)]
    x_peers = [device(y, z_lo, z_hi, core, (x + d) % 4) for d in (1, 2, 3)]
    z_peers = [device(y, z_lo, (z_hi + d) % 4, core, x) for d in (1, 2, 3)]
    pair_peers = [device((y + d) % 4, 1 - z_lo, z_hi, core, x) for d in range(4)]
    partner = device(y, z_lo, z_hi, 1 - core, x)
    y_next, y_back, x_next, x_back = y_peers[0], y_peers[2], x_peers[0], x_peers[2]
    peers = y_peers + x_peers + z_peers + pair_peers + [partner]
    greet(peers)

    load_acts = pltpu.make_async_copy(acts_hbm, acts_ref, local_sem.at[0])
    load_w = [
        pltpu.make_async_copy(w_hbm.at[n], w_ref.at[n], local_sem.at[1 + n]) for n in range(4)
    ]
    load_bias = pltpu.make_async_copy(bias_hbm, bias_ref, local_sem.at[5])
    load_normed = pltpu.make_async_copy(normed_hbm, normed_ref, local_sem.at[6])
    load_w[3].start()
    load_w[0].start()
    load_acts.start()
    load_w[1].start()
    load_w[2].start()
    load_bias.start()
    load_normed.start()

    scaling = 1.0 / math.sqrt(48)
    own = own_ref[...]
    cot = cot_ref[...]
    bias_total[...] = jnp.zeros_like(bias_total)
    attention[...] = jnp.zeros_like(attention)
    query_grad[...] = jnp.zeros_like(query_grad)
    key_grad[...] = jnp.zeros_like(key_grad)
    value_grad[...] = jnp.zeros_like(value_grad)
    load_w[3].wait()
    grad[...] = lax.dot_general(
        cot, w_ref[3], (((1,), (1,)), ((), ())), preferred_element_type=F32
    ).astype(BF16)
    load_w[0].wait()
    query[...] = jnp.dot(own, w_ref[0], preferred_element_type=F32).astype(BF16)
    load_acts.wait()
    load_w[1].wait()
    load_w[2].wait()

    def project_rows(block, _):
        rows = pl.ds(pl.multiple_of(block * 256, 256), 256)
        part = acts_ref[rows, :]
        key[rows, :] = jnp.dot(part, w_ref[1], preferred_element_type=F32).astype(BF16)
        value[rows, :] = jnp.dot(part, w_ref[2], preferred_element_type=F32).astype(BF16)
        return 0

    lax.fori_loop(0, 4, project_rows, 0)
    load_bias.wait()
    keep = valid_ref[...] == 1

    def head_bias(head):
        return jnp.concatenate(
            [
                jnp.concatenate([bias_ref[r, c, head] for c in range(4)], axis=1)
                for r in range(4)
            ],
            axis=0,
        )

    def one_copy(s, _):
        q_rows = pl.ds(pl.multiple_of(s * 64, 64), 64)
        k_rows = pl.ds(pl.multiple_of(s * 512, 512), 512)
        for start, first, count in WINDOWS:
            lanes = slice(start, start + 256)
            stacked = slice(0, count * 64)
            k_win = key[k_rows, lanes]
            v_win = value[k_rows, lanes]
            q_win = query[q_rows, lanes]
            g_win = grad[q_rows, lanes]
            masks = [head_mask(start, first + n) for n in range(count)]
            zero = jnp.zeros_like(q_win)
            q_stack = jnp.concatenate([jnp.where(m, q_win, zero) for m in masks], axis=0)
            g_stack = jnp.concatenate([jnp.where(m, g_win, zero) for m in masks], axis=0)
            scores[stacked, :] = lax.dot_general(
                q_stack, k_win, (((1,), (1,)), ((), ())), preferred_element_type=F32
            )
            pulled[stacked, :] = lax.dot_general(
                g_stack, v_win, (((1,), (1,)), ((), ())), preferred_element_type=F32
            )
            inverses = []
            for n in range(count):
                rows = slice(n * 64, n * 64 + 64)
                block = scores[rows, :] * scaling + head_bias(first + n)
                block = jnp.where(keep, block, MASKED)
                shifted = jnp.exp(block - jnp.max(block, axis=1, keepdims=True))
                inverses.append(1.0 / jnp.sum(shifted, axis=1, keepdims=True))
                scores[rows, :] = shifted
                weights[rows, :] = shifted.astype(BF16)
            merged = jnp.dot(weights[stacked, :], v_win, preferred_element_type=F32)
            attended_win = jnp.zeros((64, 256), F32)
            for n in range(count):
                attended_win = jnp.where(
                    masks[n], merged[n * 64 : n * 64 + 64] * inverses[n], attended_win
                )
            attention[q_rows, lanes] += attended_win
            product = g_win.astype(F32) * attended_win.astype(BF16).astype(F32)
            for n in range(count):
                rows = slice(n * 64, n * 64 + 64)
                delta = jnp.sum(jnp.where(masks[n], product, 0.0), axis=1, keepdims=True)
                probs = scores[rows, :] * inverses[n]
                probs_low[rows, :] = probs.astype(BF16)
                change = (probs * (pulled[rows, :] - delta)).astype(BF16)
                score_grad[rows, :] = change
                bias_total[first + n] += change.astype(F32)
            back = jnp.dot(score_grad[stacked, :], k_win, preferred_element_type=F32)
            back_win = jnp.zeros((64, 256), F32)
            for n in range(count):
                back_win = jnp.where(masks[n], back[n * 64 : n * 64 + 64], back_win)
            query_grad[q_rows, lanes] += back_win
            key_grad[k_rows, lanes] += lax.dot_general(
                score_grad[stacked, :], q_stack, (((0,), (0,)), ((), ())),
                preferred_element_type=F32,
            )
            value_grad[k_rows, lanes] += lax.dot_general(
                probs_low[stacked, :], g_stack, (((0,), (0,)), ((), ())),
                preferred_element_type=F32,
            )
        return 0

    lax.fori_loop(0, 2, one_copy, 0)
    await_greetings(peers)
    out = Sender(send_sem, recv_sem)
    send = out.send

    for column in range(4):
        bias_grad[column] = bias_total[:, :, column * 128 : column * 128 + 128].astype(BF16)
    far_block = bias_grad.at[(x + 2) % 4]
    bias_far = [
        send(far_block.at[slice(0, 8)], bias_halves.at[0], x_next),
        send(far_block.at[slice(8, 16)], bias_halves.at[1], x_back),
    ]

    merged_heads = attention[...].astype(BF16)
    q_low = (query_grad[...] * scaling).astype(BF16)
    joint[:, 0:768] = (key_grad[...] * scaling).astype(BF16)
    joint[:, 768:1536] = value_grad[...].astype(BF16)
    core_copies = {}

    def store_grads(w, half, product):
        g_ref[w, 2 * half : 2 * half + 2] = product.reshape(2, 2, 4, 24, 768).astype(BF16)
        part = slice(2 * half, 2 * half + 2)
        core_copies[w, half] = send(
            g_ref.at[w, part, 1 - core], from_core.at[w, part], partner
        )

    def own_products(half):
        lanes = slice(half * 384, half * 384 + 384)
        store_grads(3, half, transposed_product(merged_heads[:, lanes], cot))
        store_grads(0, half, transposed_product(own[:, lanes], q_low))

    def all_products(half):
        lanes = slice(half * 384, half * 384 + 384)
        both = transposed_product(acts_ref[:, lanes], joint[...])
        store_grads(1, half, both[:, 0:768])
        store_grads(2, half, both[:, 768:1536])

    first_next, first_back = (y_next, x_next), (y_back, x_back)
    second_next, second_back = (x_next, y_next), (x_back, y_back)

    def both_cores(half, a, b, n):
        w = (y + (a, b)[half]) % 4
        c = (x + (b, a)[half]) % 4
        k = 2 * half + n
        return g_ref[w, k, core, c].astype(F32) + from_core[w, k, c].astype(F32)

    far, near = {}, {}

    def start_chunk(half, b):
        if b == 2:
            for w in range(4):
                core_copies[w, half].wait_recv()
        for n in range(2):
            to_far[b, 2 * half + n] = both_cores(half, 2, b, n).astype(BF16)
        far[half, b] = (
            send(to_far.at[b, 2 * half], from_far.at[0, half, b], first_next[half]),
            send(to_far.at[b, 2 * half + 1], from_far.at[1, half, b], first_back[half]),
        )

    def pass_chunk(half, b):
        to_y[0, half, b, 1] = both_cores(half, 1, b, 1).astype(BF16)
        to_y[1, half, b, 0] = both_cores(half, 3, b, 0).astype(BF16)
        far[half, b][0].wait_recv()
        to_y[0, half, b, 0] = (
            both_cores(half, 1, b, 0) + from_far[0, half, b].astype(F32)
        ).astype(BF16)
        up = send(to_y.at[0, half, b], from_y.at[0, half, b], first_next[half])
        far[half, b][1].wait_recv()
        to_y[1, half, b, 1] = (
            both_cores(half, 3, b, 1) + from_far[1, half, b].astype(F32)
        ).astype(BF16)
        down = send(to_y.at[1, half, b], from_y.at[1, half, b], first_back[half])
        near[half, b] = (up, down)

    own_products(0)
    all_products(0)
    own_products(1)
    start_chunk(0, 2)
    start_chunk(0, 1)
    for copy in bias_far:
        copy.wait_recv()

    def add_bias(h, _):
        up, down = (x + 1) % 4, (x + 3) % 4
        bias_sent[0, h] = (
            bias_grad[up, h].astype(F32) + bias_halves[0, h].astype(F32)
        ).astype(BF16)
        bias_sent[0, h + 8] = bias_grad[up, h + 8]
        bias_sent[1, h] = bias_grad[down, h]
        bias_sent[1, h + 8] = (
            bias_grad[down, h + 8].astype(F32) + bias_halves[1, h].astype(F32)
        ).astype(BF16)
        return 0

    lax.fori_loop(0, 8, add_bias, 0)
    bias_near = [
        send(bias_sent.at[0], bias_in.at[0], x_next),
        send(bias_sent.at[1], bias_in.at[1], x_back),
    ]
    all_products(1)
    pass_chunk(0, 2)
    start_chunk(1, 2)
    start_chunk(0, 3)
    pass_chunk(0, 1)
    start_chunk(1, 1)
    start_chunk(0, 0)
    pass_chunk(1, 2)
    pass_chunk(0, 3)
    start_chunk(1, 3)
    pass_chunk(1, 1)
    pass_chunk(0, 0)
    start_chunk(1, 0)
    attended_ref[...] = jnp.dot(merged_heads, w_ref[3], preferred_element_type=F32).astype(BF16)
    pass_chunk(1, 3)

    for copy in bias_near:
        copy.wait_recv()

    def sum_bias(h, _):
        summed = (
            bias_grad[x, h].astype(F32) + bias_in[0, h].astype(F32) + bias_in[1, h].astype(F32)
        )
        bias_sum[h] = summed.astype(BF16).astype(F32)
        return 0

    lax.fori_loop(0, 16, sum_bias, 0)
    load_normed.wait()

    def tile_rows(block, total):
        for u in range(8):
            i = block * 8 + u
            total = total + jnp.dot(
                bias_sum[:, i, :].astype(BF16), normed_ref[i], preferred_element_type=F32
            )
        return total

    early = lax.fori_loop(0, 4, tile_rows, jnp.zeros((16, 128), F32))
    pass_chunk(1, 0)
    partial[0] = lax.fori_loop(4, 8, tile_rows, early)
    stages = ([partner], y_peers, x_peers, z_peers, pair_peers[0:1])
    starts = (0, 1, 4, 7, 10)
    in_flight = {}

    def start_stage(n):
        in_flight[n] = [
            send(partial.at[n], partial_in.at[starts[n] + d], peer)
            for d, peer in enumerate(stages[n])
        ]

    def end_stage(n):
        total = partial[n]
        for d, copy in enumerate(in_flight[n]):
            copy.wait_recv()
            total = total + partial_in[starts[n] + d]
        if n < 4:
            partial[n + 1] = total
            start_stage(n + 1)
        else:
            bias_out_ref[...] = total.T

    def first_sum(half, b, n):
        return (
            both_cores(half, 0, b, n)
            + from_y[0, half, b, n].astype(F32)
            + from_y[1, half, b, n].astype(F32)
        )

    def wait_first(half, b):
        near[half, b][0].wait_recv()
        near[half, b][1].wait_recv()

    x_far, x_near, pair_copies = {}, {}, {}

    def start_second(half):
        wait_first(half, 2)
        for n in range(2):
            to_x[2, half, n] = first_sum(half, 2, n).astype(BF16)
        x_far[half] = (
            send(to_x.at[2, half, 0], x_halves.at[0, half], second_next[half]),
            send(to_x.at[2, half, 1], x_halves.at[1, half], second_back[half]),
        )

    def pass_second(half):
        wait_first(half, 1)
        to_x[0, half, 1] = first_sum(half, 1, 1).astype(BF16)
        x_far[half][0].wait_recv()
        to_x[0, half, 0] = (
            first_sum(half, 1, 0) + x_halves[0, half].astype(F32)
        ).astype(BF16)
        up = send(to_x.at[0, half], from_x.at[0, half], second_next[half])
        wait_first(half, 3)
        to_x[1, half, 0] = first_sum(half, 3, 0).astype(BF16)
        x_far[half][1].wait_recv()
        to_x[1, half, 1] = (
            first_sum(half, 3, 1) + x_halves[1, half].astype(F32)
        ).astype(BF16)
        down = send(to_x.at[1, half], from_x.at[1, half], second_back[half])
        x_near[half] = (up, down)

    def end_second(half):
        wait_first(half, 0)
        for copy in x_near[half]:
            copy.wait_recv()
        for n in range(2):
            total = (
                first_sum(half, 0, n)
                + from_x[0, half, n].astype(F32)
                + from_x[1, half, n].astype(F32)
            )
            for side in range(2):
                lanes = total[:, side * 384 : side * 384 + 384]
                own_sum[side, 2 * half + n] = lanes
                to_pair[side, 2 * half + n] = lanes.astype(BF16)
        part = slice(2 * half, 2 * half + 2)
        pair_copies[half] = send(
            to_pair.at[1 - z_lo, part], from_pair.at[part], pair_peers[0]
        )

    start_stage(0)
    start_second(0)
    start_second(1)
    end_stage(0)
    pass_second(0)
    pass_second(1)
    end_stage(1)
    end_second(0)
    end_second(1)
    end_stage(2)
    for half in range(2):
        pair_copies[half].wait_recv()
        for k in (2 * half, 2 * half + 1):
            total = own_sum[z_lo, k] + from_pair[k].astype(F32)
            own_sum[z_lo, k] = total
            to_z[k] = total.astype(BF16)
    z_copies = [
        send(to_z.at[(z_hi + 1 + d) % 4], from_z.at[d], z_peers[d]) for d in range(3)
    ]
    end_stage(3)
    total = own_sum[z_lo, z_hi]
    for d, copy in enumerate(z_copies):
        copy.wait_recv()
        total = total + from_z[d].astype(F32)
    last[...] = total.astype(BF16)
    last_copies = [
        send(last, from_last.at[d], peer) for d, peer in enumerate(y_peers + pair_peers)
    ]
    results[y, z_lo] = total.astype(BF16).astype(F32)
    end_stage(4)
    for d, copy in enumerate(last_copies):
        copy.wait_recv()
        if d < 3:
            results[(y + 3 - d) % 4, z_lo] = from_last[d].astype(F32)
        else:
            results[(y + 7 - d) % 4, 1 - z_lo] = from_last[d].astype(F32)
    out.finish()


def attend(own, cot, valid, acts, weights, bias, normed):
    vmem = pl.BlockSpec(memory_space=pltpu.VMEM)
    any_space = pl.BlockSpec(memory_space=pl.ANY)
    return pl.pallas_call(
        attention_kernel,
        out_shape=(
            jax.ShapeDtypeStruct((128, 768), BF16),
            jax.ShapeDtypeStruct((4, 2, 24, 384), F32),
            jax.ShapeDtypeStruct((128, 16), F32),
        ),
        in_specs=[vmem] * 3 + [any_space] * 4,
        out_specs=[vmem] * 3,
        scratch_shapes=[
            pltpu.VMEM((1024, 768), BF16),
            pltpu.VMEM((4, 768, 768), BF16),
            pltpu.VMEM((4, 4, 16, 16, 128), F32),
            pltpu.VMEM((64, 128, 128), BF16),
            pltpu.VMEM((128, 768), BF16),
            pltpu.VMEM((1024, 768), BF16),
            pltpu.VMEM((1024, 768), BF16),
            pltpu.VMEM((128, 768), BF16),
            pltpu.VMEM((128, 768), F32),
            pltpu.VMEM((128, 768), F32),
            pltpu.VMEM((1024, 768), F32),
            pltpu.VMEM((1024, 768), F32),
            pltpu.VMEM((16, 64, 512), F32),
            pltpu.VMEM((320, 512), F32),
            pltpu.VMEM((320, 512), F32),
            pltpu.VMEM((320, 512), BF16),
            pltpu.VMEM((320, 512), BF16),
            pltpu.VMEM((320, 512), BF16),
            pltpu.VMEM((1024, 1536), BF16),
            pltpu.VMEM((4, 16, 64, 128), BF16),
            pltpu.VMEM((4, 4, 2, 4, 24, 768), BF16),
            pltpu.VMEM((4, 4, 4, 24, 768), BF16),
            pltpu.VMEM((4, 4, 24, 768), BF16),
            pltpu.VMEM((2, 2, 4, 24, 768), BF16),
            pltpu.VMEM((2, 2, 4, 2, 24, 768), BF16),
            pltpu.VMEM((2, 2, 4, 2, 24, 768), BF16),
            pltpu.VMEM((3, 2, 2, 24, 768), BF16),
            pltpu.VMEM((2, 2, 2, 24, 768), BF16),
            pltpu.VMEM((2, 2, 24, 768), BF16),
            pltpu.VMEM((2, 4, 24, 384), F32),
            pltpu.VMEM((2, 4, 24, 384), BF16),
            pltpu.VMEM((4, 24, 384), BF16),
            pltpu.VMEM((4, 24, 384), BF16),
            pltpu.VMEM((3, 24, 384), BF16),
            pltpu.VMEM((24, 384), BF16),
            pltpu.VMEM((7, 24, 384), BF16),
            pltpu.VMEM((2, 8, 64, 128), BF16),
            pltpu.VMEM((2, 16, 64, 128), BF16),
            pltpu.VMEM((2, 16, 64, 128), BF16),
            pltpu.VMEM((16, 64, 128), F32),
            pltpu.VMEM((5, 16, 128), F32),
            pltpu.VMEM((11, 16, 128), F32),
            pltpu.SemaphoreType.DMA((7,)),
            pltpu.SemaphoreType.DMA((76,)),
            pltpu.SemaphoreType.DMA((76,)),
        ],
        compiler_params=pltpu.CompilerParams(
            collective_id=1, has_side_effects=True, vmem_limit_bytes=VMEM_LIMIT
        ),
        name="attend",
    )(own, cot, valid, acts, weights, bias, normed)


def finish_kernel(
    attended_in, results_in, bias_in, attended_ref, gq_ref, gk_ref, gv_ref, go_ref, bias_ref
):
    attended_ref[...] = attended_in[...]
    for n, ref in enumerate((gq_ref, gk_ref, gv_ref, go_ref)):
        ref[:, 0:384] = results_in[n, 0]
        ref[:, 384:768] = results_in[n, 1]
    bias_ref[...] = bias_in[...]


def finish(attended, results, grad_bias):
    vmem = pl.BlockSpec(memory_space=pltpu.VMEM)
    grads = jax.ShapeDtypeStruct((24, 768), F32)
    return pl.pallas_call(
        finish_kernel,
        out_shape=(
            jax.ShapeDtypeStruct((128, 768), BF16),
            grads, grads, grads, grads,
            jax.ShapeDtypeStruct((128, 16), F32),
        ),
        in_specs=[vmem] * 3,
        out_specs=[vmem] * 6,
        name="finish",
    )(attended, results, grad_bias)


def per_device(
    single, pair_features, key_valid, pair_gain, w_query, w_key, w_value, w_out, pair_bias_weight,
    out_cotangent,
):
    own_acts = single[0]
    copies, own_count, features = own_acts.shape
    w_all, acts_all, bias, normed = gather(
        w_query, w_key, w_value, w_out, own_acts,
        pair_features[0],
        pair_gain[None],
        pair_bias_weight.T,
    )
    summed = attend(
        own_acts.reshape(copies * own_count, features),
        out_cotangent[0].reshape(copies * own_count, features),
        key_valid,
        acts_all.reshape(copies * 512, features),
        w_all.reshape(4, features, features),
        bias,
        normed,
    )
    attended, grad_query, grad_key, grad_value, grad_out, grad_bias = finish(*summed)
    attended = attended.reshape(1, copies, own_count, features)
    return (attended, grad_query, grad_key, grad_value, grad_out, grad_bias)


def solution(mesh):
    weight = P(("row", "col"), None)
    tokens = P("dp", "col", "row", None)
    return jax.shard_map(
        per_device,
        mesh=mesh,
        in_specs=(
            tokens, P("dp", "row", "col", None), P("dp", None), P(), weight, weight, weight, weight,
            P(), tokens,
        ),
        out_specs=(tokens, weight, weight, weight, weight, P()),
        check_vma=False,
    )
```

```python
import math

import jax
import jax.numpy as jnp
from jax import lax
from jax.experimental import pallas as pl
from jax.experimental.pallas import tpu as pltpu
from jax.sharding import PartitionSpec as P

NORM_EPSILON = 1e-05
MASKED = -1000000000.0
MESH = pl.DeviceIdType.MESH
F32 = jnp.float32
BF16 = jnp.bfloat16
VMEM_LIMIT = 56 * 1024 * 1024


def place():
    dp, row, col = lax.axis_index("dp"), lax.axis_index("row"), lax.axis_index("col")
    return dp // 2, dp % 2, row // 2, row % 2, col


def device(y, z_lo, z_hi, core, x):
    return (y * 2 + z_lo, z_hi * 2 + core, x)


def greet(peers):
    barrier = pltpu.get_barrier_semaphore()
    for peer in peers:
        pl.semaphore_signal(barrier, inc=1, device_id=peer, device_id_type=MESH)


def await_greetings(peers):
    pl.semaphore_wait(pltpu.get_barrier_semaphore(), len(peers))


class Sender:
    def __init__(self, send_sem, recv_sem):
        self.send_sem, self.recv_sem, self.started = send_sem, recv_sem, []

    def send(self, src, dst, peer):
        key = len(self.started)
        copy = pltpu.make_async_remote_copy(
            src_ref=src,
            dst_ref=dst,
            send_sem=self.send_sem.at[key],
            recv_sem=self.recv_sem.at[key],
            device_id=peer,
            device_id_type=MESH,
        )
        copy.start()
        self.started.append(copy)
        return copy

    def finish(self):
        for copy in self.started:
            copy.wait_send()


def gather_kernel(
    wq_ref, wk_ref, wv_ref, wo_ref, acts_ref, pair_ref, gain_ref, pair_weight_ref,
    w_full, acts_full, bias_full, normed_ref,
    tile_bias, pair, normed_rows, local_sem, send_sem, recv_sem,
):
    y, z_lo, z_hi, core, x = place()
    row = z_hi * 2 + core
    y_next, y_back = [device((y + d) % 4, z_lo, z_hi, core, x) for d in (1, 3)]
    x_next, x_back = [device(y, z_lo, z_hi, core, (x + d) % 4) for d in (1, 3)]
    z_peers = [device(y, z_lo, (z_hi + d) % 4, core, x) for d in (1, 2, 3)]
    z_next, z_back = z_peers[0], z_peers[2]
    partner = device(y, z_lo, z_hi, 1 - core, x)
    peers = [y_next, y_back, x_next, x_back, partner] + z_peers
    greet(peers)

    def block_rows(block):
        return slice(block * 16, block * 16 + 16)

    loads = [
        pltpu.make_async_copy(
            pair_ref.at[block_rows(b)], pair.at[block_rows(b)], local_sem.at[3 + b]
        )
        for b in range(4)
    ]
    for load in loads:
        load.start()
    stores = []

    def normalize_rows(block):
        loads[block].wait()

        def one_row(k, _):
            i = block * 16 + k
            values = pair[i].astype(F32)
            center = jnp.mean(values, axis=-1, keepdims=True)
            centered = values - center
            variance = jnp.mean(centered * centered, axis=-1, keepdims=True)
            normed = (
                centered * lax.rsqrt(variance + NORM_EPSILON) * gain_ref[...]
            ).astype(BF16)
            normed_rows[i] = normed
            tile_bias[block, :, k, :] = lax.dot_general(
                pair_weight_ref[...], normed, (((1,), (1,)), ((), ())),
                preferred_element_type=F32,
            )
            return 0

        lax.fori_loop(0, 16, one_row, 0, unroll=4)
        store = pltpu.make_async_copy(
            normed_rows.at[block_rows(block)], normed_ref.at[block_rows(block)],
            local_sem.at[7 + block],
        )
        store.start()
        stores.append(store)

    def line(plane, owner, part=slice(0, 4)):
        return w_full.at[plane % 4, part, core, owner % 4]

    def rows(z_owner):
        return acts_full.at[:, (z_owner % 4) * 2 + core]

    normalize_rows(0)
    await_greetings(peers)
    out = Sender(send_sem, recv_sem)
    send = out.send
    first, second = slice(0, 2), slice(2, 4)
    for plane, w_ref in enumerate((wq_ref, wk_ref, wv_ref, wo_ref)):

        @pl.when(y == plane)
        def _(plane=plane, w_ref=w_ref):
            target = w_full.at[plane, z_hi, core, x]
            pltpu.make_async_copy(w_ref, target, local_sem.at[0]).start()
            for d, peer in enumerate(z_peers):
                pltpu.make_async_remote_copy(
                    src_ref=w_ref, dst_ref=target, send_sem=send_sem.at[d],
                    recv_sem=recv_sem.at[d], device_id=peer, device_id_type=MESH,
                ).start()

    own_w = pltpu.make_async_copy(wq_ref, w_full.at[y, z_hi, core, x], local_sem.at[0])
    own_acts = pltpu.make_async_copy(acts_ref, acts_full.at[:, row], local_sem.at[1])
    z_copies = [
        pltpu.make_async_remote_copy(
            src_ref=wq_ref, dst_ref=w_full.at[y, z_hi, core, x], send_sem=send_sem.at[d],
            recv_sem=recv_sem.at[d], device_id=peer, device_id_type=MESH,
        )
        for d, peer in enumerate(z_peers)
    ]
    out.started.extend(z_copies)
    own_acts.start()
    acts_up = send(acts_ref, rows(z_hi), z_next)
    acts_down = send(acts_ref, rows(z_hi), z_back)
    core_copies = [send(acts_ref, rows(z_hi), partner)]

    def swap_planes(owner):
        own = line(y, owner)
        core_copies.append(send(own, own, partner))
        return send(own, own, y_next), send(own, own, y_back)

    def bias_block(owner, chunk, heads=slice(0, 16)):
        return bias_full.at[chunk, owner % 4, heads]

    bias_near, bias_far = [], []

    def send_bias(chunk):
        source = tile_bias.at[chunk]
        bias_near.append(
            (send(source, bias_block(x, chunk), x_next), send(source, bias_block(x, chunk), x_back))
        )

    def relay_bias(chunk):
        up, down = bias_near[chunk]
        up.wait_recv()
        part = bias_block(x + 3, chunk, slice(0, 8))
        bias_far.append(send(part, part, x_next))
        down.wait_recv()
        part = bias_block(x + 1, chunk, slice(8, 16))
        bias_far.append(send(part, part, x_back))

    send_bias(0)
    normalize_rows(1)
    own_w.wait()
    for copy in z_copies:
        copy.wait_recv()
    own = line(y, x)
    x_up = send(own, own, x_next)
    x_down = send(own, own, x_back)
    planes = [swap_planes(x)]
    send_bias(1)
    normalize_rows(2)
    x_up.wait_recv()
    part = line(y, x + 3, first)
    x_far_up = send(part, part, x_next)
    x_down.wait_recv()
    part = line(y, x + 1, second)
    x_far_down = send(part, part, x_back)
    planes.append(swap_planes(x + 3))
    planes.append(swap_planes(x + 1))
    send_bias(2)
    acts_up.wait_recv()
    part = acts_full.at[0, ((z_hi + 3) % 4) * 2 + core]
    acts_far_up = send(part, part, z_next)
    acts_down.wait_recv()
    part = acts_full.at[1, ((z_hi + 1) % 4) * 2 + core]
    acts_far_down = send(part, part, z_back)
    core_copies.append(send(rows(z_hi + 3), rows(z_hi + 3), partner))
    core_copies.append(send(rows(z_hi + 1), rows(z_hi + 1), partner))
    relay_bias(0)
    normalize_rows(3)
    send_bias(3)
    x_far_up.wait_recv()
    x_far_down.wait_recv()
    planes.append(swap_planes(x + 2))
    owners = (x, x + 3, x + 1, x + 2)
    far = []

    def relay_planes(n):
        up, down = planes[n]
        owner = owners[n]
        up.wait_recv()
        part = line(y + 3, owner, first)
        far_up = send(part, part, y_next)
        down.wait_recv()
        part = line(y + 1, owner, second)
        far.append((far_up, send(part, part, y_back)))
        for plane in (y + 3, y + 1):
            whole = line(plane, owner)
            core_copies.append(send(whole, whole, partner))

    relay_planes(0)
    own_bias = pltpu.make_async_copy(tile_bias, bias_full.at[:, x], local_sem.at[2])
    own_bias.start()
    relay_bias(1)
    relay_planes(1)
    relay_bias(2)
    relay_planes(2)
    relay_bias(3)
    relay_planes(3)
    acts_far_up.wait_recv()
    acts_far_down.wait_recv()
    core_copies.append(send(rows(z_hi + 2), rows(z_hi + 2), partner))
    for n in range(4):
        for copy in far[n]:
            copy.wait_recv()
        whole = line(y + 2, owners[n])
        core_copies.append(send(whole, whole, partner))
    for copy in core_copies + bias_far:
        copy.wait_recv()
    own_acts.wait()
    own_bias.wait()
    for store in stores:
        store.wait()
    out.finish()


def gather(w_query, w_key, w_value, w_out, acts, pair_tile, pair_gain, pair_weight):
    any_space = pl.BlockSpec(memory_space=pl.ANY)
    vmem = pl.BlockSpec(memory_space=pltpu.VMEM)
    return pl.pallas_call(
        gather_kernel,
        out_shape=(
            jax.ShapeDtypeStruct((4, 4, 2, 4, 24, 768), BF16),
            jax.ShapeDtypeStruct((2, 8, 64, 768), BF16),
            jax.ShapeDtypeStruct((4, 4, 16, 16, 128), F32),
            jax.ShapeDtypeStruct((64, 128, 128), BF16),
        ),
        in_specs=[any_space] * 6 + [vmem] * 2,
        out_specs=[any_space] * 4,
        scratch_shapes=[
            pltpu.VMEM((4, 16, 16, 128), F32),
            pltpu.VMEM((64, 128, 128), BF16),
            pltpu.VMEM((64, 128, 128), BF16),
            pltpu.SemaphoreType.DMA((11,)),
            pltpu.SemaphoreType.DMA((63,)),
            pltpu.SemaphoreType.DMA((63,)),
        ],
        compiler_params=pltpu.CompilerParams(
            collective_id=0, has_side_effects=True, vmem_limit_bytes=VMEM_LIMIT
        ),
        name="gather",
    )(w_query, w_key, w_value, w_out, acts, pair_tile, pair_gain, pair_weight)


def transposed_product(left, right):
    return lax.dot_general(left, right, (((0,), (0,)), ((), ())), preferred_element_type=F32)


WINDOWS = ((0, 0, 5), (128, 5, 3), (384, 8, 5), (512, 13, 3))


def head_mask(start, head):
    lanes = lax.broadcasted_iota(jnp.int32, (64, 256), 1) + start
    return (lanes >= head * 48) & (lanes < head * 48 + 48)


def attention_kernel(
    own_ref, cot_ref, valid_ref, acts_hbm, w_hbm, bias_hbm, normed_hbm,
    attended_ref, results, bias_out_ref,
    acts_ref, w_ref, bias_ref, normed_ref,
    query, key, value, grad, attention, query_grad, key_grad, value_grad, bias_total,
    scores, pulled, weights, probs_low, score_grad, joint, bias_grad,
    g_ref, from_core, to_far, from_far, to_y, from_y, to_x, from_x, x_halves,
    own_sum, to_pair, from_pair, to_z, from_z, last, from_last,
    bias_halves, bias_sent, bias_in, bias_sum, partial, partial_in,
    local_sem, send_sem, recv_sem,
):
    y, z_lo, z_hi, core, x = place()
    y_peers = [device((y + d) % 4, z_lo, z_hi, core, x) for d in (1, 2, 3)]
    x_peers = [device(y, z_lo, z_hi, core, (x + d) % 4) for d in (1, 2, 3)]
    z_peers = [device(y, z_lo, (z_hi + d) % 4, core, x) for d in (1, 2, 3)]
    pair_peers = [device((y + d) % 4, 1 - z_lo, z_hi, core, x) for d in range(4)]
    partner = device(y, z_lo, z_hi, 1 - core, x)
    y_next, y_back, x_next, x_back = y_peers[0], y_peers[2], x_peers[0], x_peers[2]
    peers = y_peers + x_peers + z_peers + pair_peers + [partner]
    greet(peers)

    load_acts = pltpu.make_async_copy(acts_hbm, acts_ref, local_sem.at[0])
    load_w = [
        pltpu.make_async_copy(w_hbm.at[n], w_ref.at[n], local_sem.at[1 + n]) for n in range(4)
    ]
    load_bias = pltpu.make_async_copy(bias_hbm, bias_ref, local_sem.at[5])
    load_normed = pltpu.make_async_copy(normed_hbm, normed_ref, local_sem.at[6])
    load_w[3].start()
    load_w[0].start()
    load_acts.start()
    load_w[1].start()
    load_w[2].start()
    load_bias.start()
    load_normed.start()

    scaling = 1.0 / math.sqrt(48)
    own = own_ref[...]
    cot = cot_ref[...]
    bias_total[...] = jnp.zeros_like(bias_total)
    attention[...] = jnp.zeros_like(attention)
    query_grad[...] = jnp.zeros_like(query_grad)
    key_grad[...] = jnp.zeros_like(key_grad)
    value_grad[...] = jnp.zeros_like(value_grad)
    load_w[3].wait()
    grad[...] = lax.dot_general(
        cot, w_ref[3], (((1,), (1,)), ((), ())), preferred_element_type=F32
    ).astype(BF16)
    load_w[0].wait()
    query[...] = jnp.dot(own, w_ref[0], preferred_element_type=F32).astype(BF16)
    load_acts.wait()
    load_w[1].wait()
    load_w[2].wait()

    def project_rows(block, _):
        rows = pl.ds(pl.multiple_of(block * 256, 256), 256)
        part = acts_ref[rows, :]
        key[rows, :] = jnp.dot(part, w_ref[1], preferred_element_type=F32).astype(BF16)
        value[rows, :] = jnp.dot(part, w_ref[2], preferred_element_type=F32).astype(BF16)
        return 0

    lax.fori_loop(0, 4, project_rows, 0)
    load_bias.wait()
    keep = valid_ref[...] == 1

    def head_bias(head):
        return jnp.concatenate(
            [
                jnp.concatenate([bias_ref[r, c, head] for c in range(4)], axis=1)
                for r in range(4)
            ],
            axis=0,
        )

    def one_copy(s, _):
        q_rows = pl.ds(pl.multiple_of(s * 64, 64), 64)
        k_rows = pl.ds(pl.multiple_of(s * 512, 512), 512)
        for start, first, count in WINDOWS:
            lanes = slice(start, start + 256)
            stacked = slice(0, count * 64)
            k_win = key[k_rows, lanes]
            v_win = value[k_rows, lanes]
            q_win = query[q_rows, lanes]
            g_win = grad[q_rows, lanes]
            masks = [head_mask(start, first + n) for n in range(count)]
            zero = jnp.zeros_like(q_win)
            q_stack = jnp.concatenate([jnp.where(m, q_win, zero) for m in masks], axis=0)
            g_stack = jnp.concatenate([jnp.where(m, g_win, zero) for m in masks], axis=0)
            scores[stacked, :] = lax.dot_general(
                q_stack, k_win, (((1,), (1,)), ((), ())), preferred_element_type=F32
            )
            pulled[stacked, :] = lax.dot_general(
                g_stack, v_win, (((1,), (1,)), ((), ())), preferred_element_type=F32
            )
            inverses = []
            for n in range(count):
                rows = slice(n * 64, n * 64 + 64)
                block = scores[rows, :] * scaling + head_bias(first + n)
                block = jnp.where(keep, block, MASKED)
                shifted = jnp.exp(block - jnp.max(block, axis=1, keepdims=True))
                inverses.append(1.0 / jnp.sum(shifted, axis=1, keepdims=True))
                scores[rows, :] = shifted
                weights[rows, :] = shifted.astype(BF16)
            merged = jnp.dot(weights[stacked, :], v_win, preferred_element_type=F32)
            attended_win = jnp.zeros((64, 256), F32)
            for n in range(count):
                attended_win = jnp.where(
                    masks[n], merged[n * 64 : n * 64 + 64] * inverses[n], attended_win
                )
            attention[q_rows, lanes] += attended_win
            product = g_win.astype(F32) * attended_win.astype(BF16).astype(F32)
            for n in range(count):
                rows = slice(n * 64, n * 64 + 64)
                delta = jnp.sum(jnp.where(masks[n], product, 0.0), axis=1, keepdims=True)
                probs = scores[rows, :] * inverses[n]
                probs_low[rows, :] = probs.astype(BF16)
                change = (probs * (pulled[rows, :] - delta)).astype(BF16)
                score_grad[rows, :] = change
                bias_total[first + n] += change.astype(F32)
            back = jnp.dot(score_grad[stacked, :], k_win, preferred_element_type=F32)
            back_win = jnp.zeros((64, 256), F32)
            for n in range(count):
                back_win = jnp.where(masks[n], back[n * 64 : n * 64 + 64], back_win)
            query_grad[q_rows, lanes] += back_win
            key_grad[k_rows, lanes] += lax.dot_general(
                score_grad[stacked, :], q_stack, (((0,), (0,)), ((), ())),
                preferred_element_type=F32,
            )
            value_grad[k_rows, lanes] += lax.dot_general(
                probs_low[stacked, :], g_stack, (((0,), (0,)), ((), ())),
                preferred_element_type=F32,
            )
        return 0

    lax.fori_loop(0, 2, one_copy, 0)
    await_greetings(peers)
    out = Sender(send_sem, recv_sem)
    send = out.send

    for column in range(4):
        bias_grad[column] = bias_total[:, :, column * 128 : column * 128 + 128].astype(BF16)
    far_block = bias_grad.at[(x + 2) % 4]
    bias_far = [
        send(far_block.at[slice(0, 8)], bias_halves.at[0], x_next),
        send(far_block.at[slice(8, 16)], bias_halves.at[1], x_back),
    ]

    merged_heads = attention[...].astype(BF16)
    q_low = (query_grad[...] * scaling).astype(BF16)
    joint[:, 0:768] = (key_grad[...] * scaling).astype(BF16)
    joint[:, 768:1536] = value_grad[...].astype(BF16)
    core_copies = {}

    def store_grads(w, half, product):
        g_ref[w, 2 * half : 2 * half + 2] = product.reshape(2, 2, 4, 24, 768).astype(BF16)
        part = slice(2 * half, 2 * half + 2)
        core_copies[w, half] = send(
            g_ref.at[w, part, 1 - core], from_core.at[w, part], partner
        )

    def own_products(half):
        lanes = slice(half * 384, half * 384 + 384)
        store_grads(3, half, transposed_product(merged_heads[:, lanes], cot))
        store_grads(0, half, transposed_product(own[:, lanes], q_low))

    def all_products(half):
        lanes = slice(half * 384, half * 384 + 384)
        both = transposed_product(acts_ref[:, lanes], joint[...])
        store_grads(1, half, both[:, 0:768])
        store_grads(2, half, both[:, 768:1536])

    first_next, first_back = (y_next, x_next), (y_back, x_back)
    second_next, second_back = (x_next, y_next), (x_back, y_back)

    def both_cores(half, a, b, n):
        w = (y + (a, b)[half]) % 4
        c = (x + (b, a)[half]) % 4
        k = 2 * half + n
        return g_ref[w, k, core, c].astype(F32) + from_core[w, k, c].astype(F32)

    far, near = {}, {}

    def start_chunk(half, b):
        if b == 2:
            for w in range(4):
                core_copies[w, half].wait_recv()
        for n in range(2):
            to_far[b, 2 * half + n] = both_cores(half, 2, b, n).astype(BF16)
        far[half, b] = (
            send(to_far.at[b, 2 * half], from_far.at[0, half, b], first_next[half]),
            send(to_far.at[b, 2 * half + 1], from_far.at[1, half, b], first_back[half]),
        )

    def pass_chunk(half, b):
        to_y[0, half, b, 1] = both_cores(half, 1, b, 1).astype(BF16)
        to_y[1, half, b, 0] = both_cores(half, 3, b, 0).astype(BF16)
        far[half, b][0].wait_recv()
        to_y[0, half, b, 0] = (
            both_cores(half, 1, b, 0) + from_far[0, half, b].astype(F32)
        ).astype(BF16)
        up = send(to_y.at[0, half, b], from_y.at[0, half, b], first_next[half])
        far[half, b][1].wait_recv()
        to_y[1, half, b, 1] = (
            both_cores(half, 3, b, 1) + from_far[1, half, b].astype(F32)
        ).astype(BF16)
        down = send(to_y.at[1, half, b], from_y.at[1, half, b], first_back[half])
        near[half, b] = (up, down)

    own_products(0)
    all_products(0)
    own_products(1)
    start_chunk(0, 2)
    start_chunk(0, 1)
    for copy in bias_far:
        copy.wait_recv()

    def add_bias(h, _):
        up, down = (x + 1) % 4, (x + 3) % 4
        bias_sent[0, h] = (
            bias_grad[up, h].astype(F32) + bias_halves[0, h].astype(F32)
        ).astype(BF16)
        bias_sent[0, h + 8] = bias_grad[up, h + 8]
        bias_sent[1, h] = bias_grad[down, h]
        bias_sent[1, h + 8] = (
            bias_grad[down, h + 8].astype(F32) + bias_halves[1, h].astype(F32)
        ).astype(BF16)
        return 0

    lax.fori_loop(0, 8, add_bias, 0)
    bias_near = [
        send(bias_sent.at[0], bias_in.at[0], x_next),
        send(bias_sent.at[1], bias_in.at[1], x_back),
    ]
    all_products(1)
    pass_chunk(0, 2)
    start_chunk(1, 2)
    start_chunk(0, 3)
    pass_chunk(0, 1)
    start_chunk(1, 1)
    start_chunk(0, 0)
    pass_chunk(1, 2)
    pass_chunk(0, 3)
    start_chunk(1, 3)
    pass_chunk(1, 1)
    pass_chunk(0, 0)
    start_chunk(1, 0)
    attended_ref[...] = jnp.dot(merged_heads, w_ref[3], preferred_element_type=F32).astype(BF16)
    pass_chunk(1, 3)

    for copy in bias_near:
        copy.wait_recv()

    def sum_bias(h, _):
        summed = (
            bias_grad[x, h].astype(F32) + bias_in[0, h].astype(F32) + bias_in[1, h].astype(F32)
        )
        bias_sum[h] = summed.astype(BF16).astype(F32)
        return 0

    lax.fori_loop(0, 16, sum_bias, 0)
    load_normed.wait()

    def tile_rows(block, total):
        rows = [bias_sum[:, block * 8 + u, :].astype(BF16) for u in range(8)]
        tile = normed_ref[block * 8 : block * 8 + 8].reshape(1024, 128)
        return total + jnp.dot(
            jnp.concatenate(rows, axis=1), tile, preferred_element_type=F32
        )

    early = jnp.zeros((16, 128), F32)
    for block in range(4):
        early = tile_rows(block, early)
    partial[0] = early
    pass_chunk(1, 0)
    late = partial[0]
    for block in range(4, 8):
        late = tile_rows(block, late)
    partial[0] = late
    stages = ([partner], y_peers, x_peers, z_peers, pair_peers[0:1])
    starts = (0, 1, 4, 7, 10)
    in_flight = {}

    def start_stage(n):
        in_flight[n] = [
            send(partial.at[n], partial_in.at[starts[n] + d], peer)
            for d, peer in enumerate(stages[n])
        ]

    def end_stage(n):
        total = partial[n]
        for d, copy in enumerate(in_flight[n]):
            copy.wait_recv()
            total = total + partial_in[starts[n] + d]
        if n < 4:
            partial[n + 1] = total
            start_stage(n + 1)
        else:
            bias_out_ref[...] = total

    def first_sum(half, b, n):
        return (
            both_cores(half, 0, b, n)
            + from_y[0, half, b, n].astype(F32)
            + from_y[1, half, b, n].astype(F32)
        )

    def wait_first(half, b):
        near[half, b][0].wait_recv()
        near[half, b][1].wait_recv()

    x_far, x_near, pair_copies = {}, {}, {}

    def start_second(half):
        wait_first(half, 2)
        for n in range(2):
            to_x[2, half, n] = first_sum(half, 2, n).astype(BF16)
        x_far[half] = (
            send(to_x.at[2, half, 0], x_halves.at[0, half], second_next[half]),
            send(to_x.at[2, half, 1], x_halves.at[1, half], second_back[half]),
        )

    def pass_second(half):
        wait_first(half, 1)
        to_x[0, half, 1] = first_sum(half, 1, 1).astype(BF16)
        x_far[half][0].wait_recv()
        to_x[0, half, 0] = (
            first_sum(half, 1, 0) + x_halves[0, half].astype(F32)
        ).astype(BF16)
        up = send(to_x.at[0, half], from_x.at[0, half], second_next[half])
        wait_first(half, 3)
        to_x[1, half, 0] = first_sum(half, 3, 0).astype(BF16)
        x_far[half][1].wait_recv()
        to_x[1, half, 1] = (
            first_sum(half, 3, 1) + x_halves[1, half].astype(F32)
        ).astype(BF16)
        down = send(to_x.at[1, half], from_x.at[1, half], second_back[half])
        x_near[half] = (up, down)

    def end_second(half):
        wait_first(half, 0)
        for copy in x_near[half]:
            copy.wait_recv()
        for n in range(2):
            total = (
                first_sum(half, 0, n)
                + from_x[0, half, n].astype(F32)
                + from_x[1, half, n].astype(F32)
            )
            for side in range(2):
                lanes = total[:, side * 384 : side * 384 + 384]
                own_sum[side, 2 * half + n] = lanes
                to_pair[side, 2 * half + n] = lanes.astype(BF16)
        part = slice(2 * half, 2 * half + 2)
        pair_copies[half] = send(
            to_pair.at[1 - z_lo, part], from_pair.at[part], pair_peers[0]
        )

    start_stage(0)
    start_second(0)
    start_second(1)
    end_stage(0)
    pass_second(0)
    pass_second(1)
    end_stage(1)
    end_second(0)
    end_second(1)
    end_stage(2)
    for half in range(2):
        pair_copies[half].wait_recv()
        for k in (2 * half, 2 * half + 1):
            total = own_sum[z_lo, k] + from_pair[k].astype(F32)
            own_sum[z_lo, k] = total
            to_z[k] = total.astype(BF16)
    z_copies = [
        send(to_z.at[(z_hi + 1 + d) % 4], from_z.at[d], z_peers[d]) for d in range(3)
    ]
    end_stage(3)
    total = own_sum[z_lo, z_hi]
    for d, copy in enumerate(z_copies):
        copy.wait_recv()
        total = total + from_z[d].astype(F32)
    last[...] = total.astype(BF16)
    last_copies = [
        send(last, from_last.at[d], peer) for d, peer in enumerate(y_peers + pair_peers)
    ]
    results[y, z_lo] = total.astype(BF16).astype(F32)
    end_stage(4)
    for d, copy in enumerate(last_copies):
        copy.wait_recv()
        if d < 3:
            results[(y + 3 - d) % 4, z_lo] = from_last[d].astype(F32)
        else:
            results[(y + 7 - d) % 4, 1 - z_lo] = from_last[d].astype(F32)
    out.finish()


def attend(own, cot, valid, acts, weights, bias, normed):
    vmem = pl.BlockSpec(memory_space=pltpu.VMEM)
    any_space = pl.BlockSpec(memory_space=pl.ANY)
    return pl.pallas_call(
        attention_kernel,
        out_shape=(
            jax.ShapeDtypeStruct((128, 768), BF16),
            jax.ShapeDtypeStruct((4, 2, 24, 384), F32),
            jax.ShapeDtypeStruct((16, 128), F32),
        ),
        in_specs=[vmem] * 3 + [any_space] * 4,
        out_specs=[vmem] * 3,
        scratch_shapes=[
            pltpu.VMEM((1024, 768), BF16),
            pltpu.VMEM((4, 768, 768), BF16),
            pltpu.VMEM((4, 4, 16, 16, 128), F32),
            pltpu.VMEM((64, 128, 128), BF16),
            pltpu.VMEM((128, 768), BF16),
            pltpu.VMEM((1024, 768), BF16),
            pltpu.VMEM((1024, 768), BF16),
            pltpu.VMEM((128, 768), BF16),
            pltpu.VMEM((128, 768), F32),
            pltpu.VMEM((128, 768), F32),
            pltpu.VMEM((1024, 768), F32),
            pltpu.VMEM((1024, 768), F32),
            pltpu.VMEM((16, 64, 512), F32),
            pltpu.VMEM((320, 512), F32),
            pltpu.VMEM((320, 512), F32),
            pltpu.VMEM((320, 512), BF16),
            pltpu.VMEM((320, 512), BF16),
            pltpu.VMEM((320, 512), BF16),
            pltpu.VMEM((1024, 1536), BF16),
            pltpu.VMEM((4, 16, 64, 128), BF16),
            pltpu.VMEM((4, 4, 2, 4, 24, 768), BF16),
            pltpu.VMEM((4, 4, 4, 24, 768), BF16),
            pltpu.VMEM((4, 4, 24, 768), BF16),
            pltpu.VMEM((2, 2, 4, 24, 768), BF16),
            pltpu.VMEM((2, 2, 4, 2, 24, 768), BF16),
            pltpu.VMEM((2, 2, 4, 2, 24, 768), BF16),
            pltpu.VMEM((3, 2, 2, 24, 768), BF16),
            pltpu.VMEM((2, 2, 2, 24, 768), BF16),
            pltpu.VMEM((2, 2, 24, 768), BF16),
            pltpu.VMEM((2, 4, 24, 384), F32),
            pltpu.VMEM((2, 4, 24, 384), BF16),
            pltpu.VMEM((4, 24, 384), BF16),
            pltpu.VMEM((4, 24, 384), BF16),
            pltpu.VMEM((3, 24, 384), BF16),
            pltpu.VMEM((24, 384), BF16),
            pltpu.VMEM((7, 24, 384), BF16),
            pltpu.VMEM((2, 8, 64, 128), BF16),
            pltpu.VMEM((2, 16, 64, 128), BF16),
            pltpu.VMEM((2, 16, 64, 128), BF16),
            pltpu.VMEM((16, 64, 128), F32),
            pltpu.VMEM((5, 16, 128), F32),
            pltpu.VMEM((11, 16, 128), F32),
            pltpu.SemaphoreType.DMA((7,)),
            pltpu.SemaphoreType.DMA((76,)),
            pltpu.SemaphoreType.DMA((76,)),
        ],
        compiler_params=pltpu.CompilerParams(
            collective_id=1, has_side_effects=True, vmem_limit_bytes=VMEM_LIMIT
        ),
        name="attend",
    )(own, cot, valid, acts, weights, bias, normed)


def finish_kernel(
    attended_in, results_in, bias_in, attended_ref, gq_ref, gk_ref, gv_ref, go_ref, bias_ref
):
    attended_ref[...] = attended_in[...]
    for n, ref in enumerate((gq_ref, gk_ref, gv_ref, go_ref)):
        ref[:, 0:384] = results_in[n, 0]
        ref[:, 384:768] = results_in[n, 1]
    bias_ref[...] = bias_in[...]


def finish(attended, results, grad_bias):
    vmem = pl.BlockSpec(memory_space=pltpu.VMEM)
    grads = jax.ShapeDtypeStruct((24, 768), F32)
    return pl.pallas_call(
        finish_kernel,
        out_shape=(
            jax.ShapeDtypeStruct((128, 768), BF16),
            grads, grads, grads, grads,
            jax.ShapeDtypeStruct((16, 128), F32),
        ),
        in_specs=[vmem] * 3,
        out_specs=[vmem] * 6,
        name="finish",
    )(attended, results, grad_bias)


def per_device(
    single, pair_features, key_valid, pair_gain, w_query, w_key, w_value, w_out, pair_bias_weight,
    out_cotangent,
):
    own_acts = single[0]
    copies, own_count, features = own_acts.shape
    w_all, acts_all, bias, normed = gather(
        w_query, w_key, w_value, w_out, own_acts,
        pair_features[0],
        pair_gain[None],
        pair_bias_weight.T,
    )
    summed = attend(
        own_acts.reshape(copies * own_count, features),
        out_cotangent[0].reshape(copies * own_count, features),
        key_valid,
        acts_all.reshape(copies * 512, features),
        w_all.reshape(4, features, features),
        bias,
        normed,
    )
    attended, grad_query, grad_key, grad_value, grad_out, grad_bias = finish(*summed)
    attended = attended.reshape(1, copies, own_count, features)
    return (attended, grad_query, grad_key, grad_value, grad_out, grad_bias.T)


def solution(mesh):
    weight = P(("row", "col"), None)
    tokens = P("dp", "col", "row", None)
    return jax.shard_map(
        per_device,
        mesh=mesh,
        in_specs=(
            tokens, P("dp", "row", "col", None), P("dp", None), P(), weight, weight, weight, weight,
            P(), tokens,
        ),
        out_specs=(tokens, weight, weight, weight, weight, P()),
        check_vma=False,
    )
```

```python
import math

import jax
import jax.numpy as jnp
from jax import lax
from jax.experimental import pallas as pl
from jax.experimental.pallas import tpu as pltpu
from jax.sharding import PartitionSpec as P

NORM_EPSILON = 1e-05
MASKED = -1000000000.0
MESH = pl.DeviceIdType.MESH
F32 = jnp.float32
BF16 = jnp.bfloat16
VMEM_LIMIT = 56 * 1024 * 1024


def place():
    dp, row, col = lax.axis_index("dp"), lax.axis_index("row"), lax.axis_index("col")
    return dp // 2, dp % 2, row // 2, row % 2, col


def device(y, z_lo, z_hi, core, x):
    return (y * 2 + z_lo, z_hi * 2 + core, x)


def greet(peers):
    barrier = pltpu.get_barrier_semaphore()
    for peer in peers:
        pl.semaphore_signal(barrier, inc=1, device_id=peer, device_id_type=MESH)


def await_greetings(peers):
    pl.semaphore_wait(pltpu.get_barrier_semaphore(), len(peers))


class Sender:
    def __init__(self, send_sem, recv_sem):
        self.send_sem, self.recv_sem, self.started = send_sem, recv_sem, []

    def send(self, src, dst, peer):
        key = len(self.started)
        copy = pltpu.make_async_remote_copy(
            src_ref=src,
            dst_ref=dst,
            send_sem=self.send_sem.at[key],
            recv_sem=self.recv_sem.at[key],
            device_id=peer,
            device_id_type=MESH,
        )
        copy.start()
        self.started.append(copy)
        return copy

    def finish(self):
        for copy in self.started:
            copy.wait_send()


def gather_kernel(
    wq_ref, wk_ref, wv_ref, wo_ref, acts_ref, pair_ref, gain_ref, pair_weight_ref,
    w_full, acts_full, bias_full, normed_ref,
    tile_bias, pair, normed_rows, local_sem, send_sem, recv_sem,
):
    y, z_lo, z_hi, core, x = place()
    row = z_hi * 2 + core
    y_next, y_back = [device((y + d) % 4, z_lo, z_hi, core, x) for d in (1, 3)]
    x_next, x_back = [device(y, z_lo, z_hi, core, (x + d) % 4) for d in (1, 3)]
    z_peers = [device(y, z_lo, (z_hi + d) % 4, core, x) for d in (1, 2, 3)]
    z_next, z_back = z_peers[0], z_peers[2]
    partner = device(y, z_lo, z_hi, 1 - core, x)
    peers = [y_next, y_back, x_next, x_back, partner] + z_peers
    greet(peers)

    def block_rows(block):
        return slice(block * 16, block * 16 + 16)

    loads = [
        pltpu.make_async_copy(
            pair_ref.at[block_rows(b)], pair.at[block_rows(b)], local_sem.at[3 + b]
        )
        for b in range(4)
    ]
    for load in loads:
        load.start()
    stores = []

    def normalize_rows(block):
        loads[block].wait()

        def one_row(k, _):
            i = block * 16 + k
            values = pair[i].astype(F32)
            center = jnp.mean(values, axis=-1, keepdims=True)
            centered = values - center
            variance = jnp.mean(centered * centered, axis=-1, keepdims=True)
            normed = (
                centered * lax.rsqrt(variance + NORM_EPSILON) * gain_ref[...]
            ).astype(BF16)
            normed_rows[i] = normed
            tile_bias[block, :, k, :] = lax.dot_general(
                pair_weight_ref[...], normed, (((1,), (1,)), ((), ())),
                preferred_element_type=F32,
            )
            return 0

        lax.fori_loop(0, 16, one_row, 0, unroll=4)
        store = pltpu.make_async_copy(
            normed_rows.at[block_rows(block)], normed_ref.at[block_rows(block)],
            local_sem.at[7 + block],
        )
        store.start()
        stores.append(store)

    def line(plane, owner, part=slice(0, 4)):
        return w_full.at[plane % 4, part, core, owner % 4]

    def rows(z_owner):
        return acts_full.at[:, (z_owner % 4) * 2 + core]

    normalize_rows(0)
    await_greetings(peers)
    out = Sender(send_sem, recv_sem)
    send = out.send
    first, second = slice(0, 2), slice(2, 4)
    for plane, w_ref in enumerate((wq_ref, wk_ref, wv_ref, wo_ref)):

        @pl.when(y == plane)
        def _(plane=plane, w_ref=w_ref):
            target = w_full.at[plane, z_hi, core, x]
            pltpu.make_async_copy(w_ref, target, local_sem.at[0]).start()
            for d, peer in enumerate(z_peers):
                pltpu.make_async_remote_copy(
                    src_ref=w_ref, dst_ref=target, send_sem=send_sem.at[d],
                    recv_sem=recv_sem.at[d], device_id=peer, device_id_type=MESH,
                ).start()

    own_w = pltpu.make_async_copy(wq_ref, w_full.at[y, z_hi, core, x], local_sem.at[0])
    own_acts = pltpu.make_async_copy(acts_ref, acts_full.at[:, row], local_sem.at[1])
    z_copies = [
        pltpu.make_async_remote_copy(
            src_ref=wq_ref, dst_ref=w_full.at[y, z_hi, core, x], send_sem=send_sem.at[d],
            recv_sem=recv_sem.at[d], device_id=peer, device_id_type=MESH,
        )
        for d, peer in enumerate(z_peers)
    ]
    out.started.extend(z_copies)
    own_acts.start()
    core_copies = [send(acts_ref, rows(z_hi), partner)]

    def swap_planes(owner):
        own = line(y, owner)
        core_copies.append(send(own, own, partner))
        return send(own, own, y_next), send(own, own, y_back)

    def bias_block(owner, chunk, heads=slice(0, 16)):
        return bias_full.at[chunk, owner % 4, heads]

    bias_near, bias_far = [], []

    def send_bias(chunk):
        source = tile_bias.at[chunk]
        bias_near.append(
            (send(source, bias_block(x, chunk), x_next), send(source, bias_block(x, chunk), x_back))
        )

    def relay_bias(chunk):
        up, down = bias_near[chunk]
        up.wait_recv()
        part = bias_block(x + 3, chunk, slice(0, 8))
        bias_far.append(send(part, part, x_next))
        down.wait_recv()
        part = bias_block(x + 1, chunk, slice(8, 16))
        bias_far.append(send(part, part, x_back))

    send_bias(0)
    normalize_rows(1)
    own_w.wait()
    for copy in z_copies:
        copy.wait_recv()
    own = line(y, x)
    x_up = send(own, own, x_next)
    x_down = send(own, own, x_back)
    planes = [swap_planes(x)]
    acts_up = send(acts_ref, rows(z_hi), z_next)
    acts_down = send(acts_ref, rows(z_hi), z_back)
    send_bias(1)
    normalize_rows(2)
    x_up.wait_recv()
    part = line(y, x + 3, first)
    x_far_up = send(part, part, x_next)
    x_down.wait_recv()
    part = line(y, x + 1, second)
    x_far_down = send(part, part, x_back)
    planes.append(swap_planes(x + 3))
    planes.append(swap_planes(x + 1))
    send_bias(2)
    acts_up.wait_recv()
    part = acts_full.at[0, ((z_hi + 3) % 4) * 2 + core]
    acts_far_up = send(part, part, z_next)
    acts_down.wait_recv()
    part = acts_full.at[1, ((z_hi + 1) % 4) * 2 + core]
    acts_far_down = send(part, part, z_back)
    core_copies.append(send(rows(z_hi + 3), rows(z_hi + 3), partner))
    core_copies.append(send(rows(z_hi + 1), rows(z_hi + 1), partner))
    relay_bias(0)
    normalize_rows(3)
    send_bias(3)
    x_far_up.wait_recv()
    x_far_down.wait_recv()
    planes.append(swap_planes(x + 2))
    owners = (x, x + 3, x + 1, x + 2)
    far = []

    def relay_planes(n):
        up, down = planes[n]
        owner = owners[n]
        up.wait_recv()
        part = line(y + 3, owner, first)
        far_up = send(part, part, y_next)
        down.wait_recv()
        part = line(y + 1, owner, second)
        far.append((far_up, send(part, part, y_back)))
        for plane in (y + 3, y + 1):
            whole = line(plane, owner)
            core_copies.append(send(whole, whole, partner))

    relay_planes(0)
    own_bias = pltpu.make_async_copy(tile_bias, bias_full.at[:, x], local_sem.at[2])
    own_bias.start()
    relay_bias(1)
    relay_planes(1)
    relay_bias(2)
    relay_planes(2)
    relay_bias(3)
    relay_planes(3)
    acts_far_up.wait_recv()
    acts_far_down.wait_recv()
    core_copies.append(send(rows(z_hi + 2), rows(z_hi + 2), partner))
    for n in range(4):
        for copy in far[n]:
            copy.wait_recv()
        whole = line(y + 2, owners[n])
        core_copies.append(send(whole, whole, partner))
    for copy in core_copies + bias_far:
        copy.wait_recv()
    own_acts.wait()
    own_bias.wait()
    for store in stores:
        store.wait()
    out.finish()


def gather(w_query, w_key, w_value, w_out, acts, pair_tile, pair_gain, pair_weight):
    any_space = pl.BlockSpec(memory_space=pl.ANY)
    vmem = pl.BlockSpec(memory_space=pltpu.VMEM)
    return pl.pallas_call(
        gather_kernel,
        out_shape=(
            jax.ShapeDtypeStruct((4, 4, 2, 4, 24, 768), BF16),
            jax.ShapeDtypeStruct((2, 8, 64, 768), BF16),
            jax.ShapeDtypeStruct((4, 4, 16, 16, 128), F32),
            jax.ShapeDtypeStruct((64, 128, 128), BF16),
        ),
        in_specs=[any_space] * 6 + [vmem] * 2,
        out_specs=[any_space] * 4,
        scratch_shapes=[
            pltpu.VMEM((4, 16, 16, 128), F32),
            pltpu.VMEM((64, 128, 128), BF16),
            pltpu.VMEM((64, 128, 128), BF16),
            pltpu.SemaphoreType.DMA((11,)),
            pltpu.SemaphoreType.DMA((63,)),
            pltpu.SemaphoreType.DMA((63,)),
        ],
        compiler_params=pltpu.CompilerParams(
            collective_id=0, has_side_effects=True, vmem_limit_bytes=VMEM_LIMIT
        ),
        name="gather",
    )(w_query, w_key, w_value, w_out, acts, pair_tile, pair_gain, pair_weight)


def transposed_product(left, right):
    return lax.dot_general(left, right, (((0,), (0,)), ((), ())), preferred_element_type=F32)


WINDOWS = ((0, 0, 5), (128, 5, 3), (384, 8, 5), (512, 13, 3))


def head_mask(start, head):
    lanes = lax.broadcasted_iota(jnp.int32, (64, 256), 1) + start
    return (lanes >= head * 48) & (lanes < head * 48 + 48)


def attention_kernel(
    own_ref, cot_ref, valid_ref, acts_hbm, w_hbm, bias_hbm, normed_hbm,
    attended_ref, results, bias_out_ref,
    acts_ref, w_ref, bias_ref, normed_ref,
    query, key, value, grad, attention, query_grad, key_carry, value_carry, bias_total,
    scores, pulled, weights, probs_low, score_grad, joint, bias_grad,
    g_ref, from_core, to_far, from_far, to_y, from_y, to_x, from_x, x_halves,
    own_sum, to_pair, from_pair, to_z, from_z, last, from_last,
    bias_halves, bias_sent, bias_in, bias_sum, partial, partial_in,
    local_sem, send_sem, recv_sem,
):
    y, z_lo, z_hi, core, x = place()
    y_peers = [device((y + d) % 4, z_lo, z_hi, core, x) for d in (1, 2, 3)]
    x_peers = [device(y, z_lo, z_hi, core, (x + d) % 4) for d in (1, 2, 3)]
    z_peers = [device(y, z_lo, (z_hi + d) % 4, core, x) for d in (1, 2, 3)]
    pair_peers = [device((y + d) % 4, 1 - z_lo, z_hi, core, x) for d in range(4)]
    partner = device(y, z_lo, z_hi, 1 - core, x)
    y_next, y_back, x_next, x_back = y_peers[0], y_peers[2], x_peers[0], x_peers[2]
    peers = y_peers + x_peers + z_peers + pair_peers + [partner]
    greet(peers)

    load_acts = pltpu.make_async_copy(acts_hbm, acts_ref, local_sem.at[0])
    load_w = [
        pltpu.make_async_copy(w_hbm.at[n], w_ref.at[n], local_sem.at[1 + n]) for n in range(4)
    ]
    load_bias = pltpu.make_async_copy(bias_hbm, bias_ref, local_sem.at[5])
    load_normed = pltpu.make_async_copy(normed_hbm, normed_ref, local_sem.at[6])
    load_w[3].start()
    load_w[0].start()
    load_acts.start()
    load_w[1].start()
    load_w[2].start()
    load_bias.start()
    load_normed.start()

    scaling = 1.0 / math.sqrt(48)
    own = own_ref[...]
    cot = cot_ref[...]
    bias_total[...] = jnp.zeros_like(bias_total)
    attention[...] = jnp.zeros_like(attention)
    query_grad[...] = jnp.zeros_like(query_grad)
    load_w[3].wait()
    grad[...] = lax.dot_general(
        cot, w_ref[3], (((1,), (1,)), ((), ())), preferred_element_type=F32
    ).astype(BF16)
    load_w[0].wait()
    query[...] = jnp.dot(own, w_ref[0], preferred_element_type=F32).astype(BF16)
    load_acts.wait()
    for w, target in ((1, key), (2, value)):
        load_w[w].wait()

        def project_rows(block, _, w=w, target=target):
            rows = pl.ds(pl.multiple_of(block * 256, 256), 256)
            target[rows, :] = jnp.dot(
                acts_ref[rows, :], w_ref[w], preferred_element_type=F32
            ).astype(BF16)
            return 0

        lax.fori_loop(0, 4, project_rows, 0)
    load_bias.wait()
    keep = valid_ref[...] == 1

    def head_bias(head):
        return jnp.concatenate(
            [
                jnp.concatenate([bias_ref[r, c, head] for c in range(4)], axis=1)
                for r in range(4)
            ],
            axis=0,
        )

    def one_copy(s, _):
        q_rows = pl.ds(pl.multiple_of(s * 64, 64), 64)
        k_rows = pl.ds(pl.multiple_of(s * 512, 512), 512)
        for start, first, count in WINDOWS:
            lanes = slice(start, start + 256)
            stacked = slice(0, count * 64)
            k_win = key[k_rows, lanes]
            v_win = value[k_rows, lanes]
            q_win = query[q_rows, lanes]
            g_win = grad[q_rows, lanes]
            masks = [head_mask(start, first + n) for n in range(count)]
            zero = jnp.zeros_like(q_win)
            q_stack = jnp.concatenate([jnp.where(m, q_win, zero) for m in masks], axis=0)
            g_stack = jnp.concatenate([jnp.where(m, g_win, zero) for m in masks], axis=0)
            scores[stacked, :] = lax.dot_general(
                q_stack, k_win, (((1,), (1,)), ((), ())), preferred_element_type=F32
            )
            pulled[stacked, :] = lax.dot_general(
                g_stack, v_win, (((1,), (1,)), ((), ())), preferred_element_type=F32
            )
            inverses = []
            for n in range(count):
                rows = slice(n * 64, n * 64 + 64)
                block = scores[rows, :] * scaling + head_bias(first + n)
                block = jnp.where(keep, block, MASKED)
                shifted = jnp.exp(block - jnp.max(block, axis=1, keepdims=True))
                inverses.append(1.0 / jnp.sum(shifted, axis=1, keepdims=True))
                scores[rows, :] = shifted
                weights[rows, :] = shifted.astype(BF16)
            merged = jnp.dot(weights[stacked, :], v_win, preferred_element_type=F32)
            attended_win = jnp.zeros((64, 256), F32)
            for n in range(count):
                attended_win = jnp.where(
                    masks[n], merged[n * 64 : n * 64 + 64] * inverses[n], attended_win
                )
            attention[q_rows, lanes] += attended_win
            product = g_win.astype(F32) * attended_win.astype(BF16).astype(F32)
            for n in range(count):
                rows = slice(n * 64, n * 64 + 64)
                delta = jnp.sum(jnp.where(masks[n], product, 0.0), axis=1, keepdims=True)
                probs = scores[rows, :] * inverses[n]
                probs_low[rows, :] = probs.astype(BF16)
                change = (probs * (pulled[rows, :] - delta)).astype(BF16)
                score_grad[rows, :] = change
                bias_total[first + n] += change.astype(F32)
            back = jnp.dot(score_grad[stacked, :], k_win, preferred_element_type=F32)
            back_win = jnp.zeros((64, 256), F32)
            for n in range(count):
                back_win = jnp.where(masks[n], back[n * 64 : n * 64 + 64], back_win)
            query_grad[q_rows, lanes] += back_win
            key_win = lax.dot_general(
                score_grad[stacked, :], q_stack, (((0,), (0,)), ((), ())),
                preferred_element_type=F32,
            )
            value_win = lax.dot_general(
                probs_low[stacked, :], g_stack, (((0,), (0,)), ((), ())),
                preferred_element_type=F32,
            )
            key_left, key_right = key_win[:, 0:128], key_win[:, 128:256]
            value_left, value_right = value_win[:, 0:128], value_win[:, 128:256]
            if start % 384 == 0:
                key_carry[...] = key_right
                value_carry[...] = value_right
            else:
                key_left = key_carry[...] + key_left
                value_left = value_carry[...] + value_left
                joint[k_rows, start + 128 : start + 256] = (key_right * scaling).astype(BF16)
                joint[k_rows, start + 896 : start + 1024] = value_right.astype(BF16)
            joint[k_rows, start : start + 128] = (key_left * scaling).astype(BF16)
            joint[k_rows, start + 768 : start + 896] = value_left.astype(BF16)
        return 0

    lax.fori_loop(0, 2, one_copy, 0)
    await_greetings(peers)
    out = Sender(send_sem, recv_sem)
    send = out.send

    for column in range(4):
        bias_grad[column] = bias_total[:, :, column * 128 : column * 128 + 128].astype(BF16)
    far_block = bias_grad.at[(x + 2) % 4]
    bias_far = [
        send(far_block.at[slice(0, 8)], bias_halves.at[0], x_next),
        send(far_block.at[slice(8, 16)], bias_halves.at[1], x_back),
    ]

    merged_heads = attention[...].astype(BF16)
    q_low = (query_grad[...] * scaling).astype(BF16)
    core_copies = {}

    def store_grads(w, half, product):
        g_ref[w, 2 * half : 2 * half + 2] = product.reshape(2, 2, 4, 24, 768).astype(BF16)
        part = slice(2 * half, 2 * half + 2)
        core_copies[w, half] = send(
            g_ref.at[w, part, 1 - core], from_core.at[w, part], partner
        )

    def own_products(half):
        lanes = slice(half * 384, half * 384 + 384)
        store_grads(3, half, transposed_product(merged_heads[:, lanes], cot))
        store_grads(0, half, transposed_product(own[:, lanes], q_low))

    def all_products(half):
        lanes = slice(half * 384, half * 384 + 384)
        both = transposed_product(acts_ref[:, lanes], joint[...])
        store_grads(1, half, both[:, 0:768])
        store_grads(2, half, both[:, 768:1536])

    first_next, first_back = (y_next, x_next), (y_back, x_back)
    second_next, second_back = (x_next, y_next), (x_back, y_back)

    def both_cores(half, a, b, n):
        w = (y + (a, b)[half]) % 4
        c = (x + (b, a)[half]) % 4
        k = 2 * half + n
        return g_ref[w, k, core, c].astype(F32) + from_core[w, k, c].astype(F32)

    far, near = {}, {}

    def start_chunk(half, b):
        if b == 2:
            for w in range(4):
                core_copies[w, half].wait_recv()
        for n in range(2):
            to_far[b, 2 * half + n] = both_cores(half, 2, b, n).astype(BF16)
        far[half, b] = (
            send(to_far.at[b, 2 * half], from_far.at[0, half, b], first_next[half]),
            send(to_far.at[b, 2 * half + 1], from_far.at[1, half, b], first_back[half]),
        )

    def pass_chunk(half, b):
        to_y[0, half, b, 1] = both_cores(half, 1, b, 1).astype(BF16)
        to_y[1, half, b, 0] = both_cores(half, 3, b, 0).astype(BF16)
        far[half, b][0].wait_recv()
        to_y[0, half, b, 0] = (
            both_cores(half, 1, b, 0) + from_far[0, half, b].astype(F32)
        ).astype(BF16)
        up = send(to_y.at[0, half, b], from_y.at[0, half, b], first_next[half])
        far[half, b][1].wait_recv()
        to_y[1, half, b, 1] = (
            both_cores(half, 3, b, 1) + from_far[1, half, b].astype(F32)
        ).astype(BF16)
        down = send(to_y.at[1, half, b], from_y.at[1, half, b], first_back[half])
        near[half, b] = (up, down)

    own_products(0)
    all_products(0)
    own_products(1)
    start_chunk(0, 2)
    start_chunk(0, 1)
    for copy in bias_far:
        copy.wait_recv()

    def add_bias(h, _):
        up, down = (x + 1) % 4, (x + 3) % 4
        bias_sent[0, h] = (
            bias_grad[up, h].astype(F32) + bias_halves[0, h].astype(F32)
        ).astype(BF16)
        bias_sent[0, h + 8] = bias_grad[up, h + 8]
        bias_sent[1, h] = bias_grad[down, h]
        bias_sent[1, h + 8] = (
            bias_grad[down, h + 8].astype(F32) + bias_halves[1, h].astype(F32)
        ).astype(BF16)
        return 0

    lax.fori_loop(0, 8, add_bias, 0)
    bias_near = [
        send(bias_sent.at[0], bias_in.at[0], x_next),
        send(bias_sent.at[1], bias_in.at[1], x_back),
    ]
    all_products(1)
    pass_chunk(0, 2)
    start_chunk(1, 2)
    start_chunk(0, 3)
    pass_chunk(0, 1)
    start_chunk(1, 1)
    start_chunk(0, 0)
    pass_chunk(1, 2)
    pass_chunk(0, 3)
    start_chunk(1, 3)
    pass_chunk(1, 1)
    pass_chunk(0, 0)
    start_chunk(1, 0)
    attended_ref[...] = jnp.dot(merged_heads, w_ref[3], preferred_element_type=F32).astype(BF16)
    pass_chunk(1, 3)

    for copy in bias_near:
        copy.wait_recv()

    def sum_bias(h, _):
        summed = (
            bias_grad[x, h].astype(F32) + bias_in[0, h].astype(F32) + bias_in[1, h].astype(F32)
        )
        bias_sum[h] = summed.astype(BF16).astype(F32)
        return 0

    lax.fori_loop(0, 16, sum_bias, 0)
    load_normed.wait()

    def tile_rows(block, total):
        rows = [bias_sum[:, block * 8 + u, :].astype(BF16) for u in range(8)]
        tile = normed_ref[block * 8 : block * 8 + 8].reshape(1024, 128)
        return total + jnp.dot(
            jnp.concatenate(rows, axis=1), tile, preferred_element_type=F32
        )

    early = jnp.zeros((16, 128), F32)
    for block in range(4):
        early = tile_rows(block, early)
    partial[0] = early
    pass_chunk(1, 0)
    late = partial[0]
    for block in range(4, 8):
        late = tile_rows(block, late)
    partial[0] = late
    stages = ([partner], y_peers, x_peers, z_peers, pair_peers[0:1])
    starts = (0, 1, 4, 7, 10)
    in_flight = {}

    def start_stage(n):
        in_flight[n] = [
            send(partial.at[n], partial_in.at[starts[n] + d], peer)
            for d, peer in enumerate(stages[n])
        ]

    def end_stage(n):
        total = partial[n]
        for d, copy in enumerate(in_flight[n]):
            copy.wait_recv()
            total = total + partial_in[starts[n] + d]
        if n < 4:
            partial[n + 1] = total
            start_stage(n + 1)
        else:
            bias_out_ref[...] = total

    def first_sum(half, b, n):
        return (
            both_cores(half, 0, b, n)
            + from_y[0, half, b, n].astype(F32)
            + from_y[1, half, b, n].astype(F32)
        )

    def wait_first(half, b):
        near[half, b][0].wait_recv()
        near[half, b][1].wait_recv()

    x_far, x_near, pair_copies = {}, {}, {}

    def start_second(half):
        wait_first(half, 2)
        for n in range(2):
            to_x[2, half, n] = first_sum(half, 2, n).astype(BF16)
        x_far[half] = (
            send(to_x.at[2, half, 0], x_halves.at[0, half], second_next[half]),
            send(to_x.at[2, half, 1], x_halves.at[1, half], second_back[half]),
        )

    def pass_second(half):
        wait_first(half, 1)
        to_x[0, half, 1] = first_sum(half, 1, 1).astype(BF16)
        x_far[half][0].wait_recv()
        to_x[0, half, 0] = (
            first_sum(half, 1, 0) + x_halves[0, half].astype(F32)
        ).astype(BF16)
        up = send(to_x.at[0, half], from_x.at[0, half], second_next[half])
        wait_first(half, 3)
        to_x[1, half, 0] = first_sum(half, 3, 0).astype(BF16)
        x_far[half][1].wait_recv()
        to_x[1, half, 1] = (
            first_sum(half, 3, 1) + x_halves[1, half].astype(F32)
        ).astype(BF16)
        down = send(to_x.at[1, half], from_x.at[1, half], second_back[half])
        x_near[half] = (up, down)

    def end_second(half):
        wait_first(half, 0)
        for copy in x_near[half]:
            copy.wait_recv()
        for n in range(2):
            total = (
                first_sum(half, 0, n)
                + from_x[0, half, n].astype(F32)
                + from_x[1, half, n].astype(F32)
            )
            for side in range(2):
                lanes = total[:, side * 384 : side * 384 + 384]
                own_sum[side, 2 * half + n] = lanes
                to_pair[side, 2 * half + n] = lanes.astype(BF16)
        part = slice(2 * half, 2 * half + 2)
        pair_copies[half] = send(
            to_pair.at[1 - z_lo, part], from_pair.at[part], pair_peers[0]
        )

    start_stage(0)
    start_second(0)
    start_second(1)
    end_stage(0)
    pass_second(0)
    pass_second(1)
    end_stage(1)
    end_second(0)
    end_second(1)
    end_stage(2)
    for half in range(2):
        pair_copies[half].wait_recv()
        for k in (2 * half, 2 * half + 1):
            total = own_sum[z_lo, k] + from_pair[k].astype(F32)
            own_sum[z_lo, k] = total
            to_z[k] = total.astype(BF16)
    z_copies = [
        send(to_z.at[(z_hi + 1 + d) % 4], from_z.at[d], z_peers[d]) for d in range(3)
    ]
    end_stage(3)
    total = own_sum[z_lo, z_hi]
    for d, copy in enumerate(z_copies):
        copy.wait_recv()
        total = total + from_z[d].astype(F32)
    last[...] = total.astype(BF16)
    last_copies = [
        send(last, from_last.at[d], peer) for d, peer in enumerate(y_peers + pair_peers)
    ]
    results[y, z_lo] = total.astype(BF16).astype(F32)
    end_stage(4)
    for d, copy in enumerate(last_copies):
        copy.wait_recv()
        if d < 3:
            results[(y + 3 - d) % 4, z_lo] = from_last[d].astype(F32)
        else:
            results[(y + 7 - d) % 4, 1 - z_lo] = from_last[d].astype(F32)
    out.finish()


def attend(own, cot, valid, acts, weights, bias, normed):
    vmem = pl.BlockSpec(memory_space=pltpu.VMEM)
    any_space = pl.BlockSpec(memory_space=pl.ANY)
    return pl.pallas_call(
        attention_kernel,
        out_shape=(
            jax.ShapeDtypeStruct((128, 768), BF16),
            jax.ShapeDtypeStruct((4, 2, 24, 384), F32),
            jax.ShapeDtypeStruct((16, 128), F32),
        ),
        in_specs=[vmem] * 3 + [any_space] * 4,
        out_specs=[vmem] * 3,
        scratch_shapes=[
            pltpu.VMEM((1024, 768), BF16),
            pltpu.VMEM((4, 768, 768), BF16),
            pltpu.VMEM((4, 4, 16, 16, 128), F32),
            pltpu.VMEM((64, 128, 128), BF16),
            pltpu.VMEM((128, 768), BF16),
            pltpu.VMEM((1024, 768), BF16),
            pltpu.VMEM((1024, 768), BF16),
            pltpu.VMEM((128, 768), BF16),
            pltpu.VMEM((128, 768), F32),
            pltpu.VMEM((128, 768), F32),
            pltpu.VMEM((512, 128), F32),
            pltpu.VMEM((512, 128), F32),
            pltpu.VMEM((16, 64, 512), F32),
            pltpu.VMEM((320, 512), F32),
            pltpu.VMEM((320, 512), F32),
            pltpu.VMEM((320, 512), BF16),
            pltpu.VMEM((320, 512), BF16),
            pltpu.VMEM((320, 512), BF16),
            pltpu.VMEM((1024, 1536), BF16),
            pltpu.VMEM((4, 16, 64, 128), BF16),
            pltpu.VMEM((4, 4, 2, 4, 24, 768), BF16),
            pltpu.VMEM((4, 4, 4, 24, 768), BF16),
            pltpu.VMEM((4, 4, 24, 768), BF16),
            pltpu.VMEM((2, 2, 4, 24, 768), BF16),
            pltpu.VMEM((2, 2, 4, 2, 24, 768), BF16),
            pltpu.VMEM((2, 2, 4, 2, 24, 768), BF16),
            pltpu.VMEM((3, 2, 2, 24, 768), BF16),
            pltpu.VMEM((2, 2, 2, 24, 768), BF16),
            pltpu.VMEM((2, 2, 24, 768), BF16),
            pltpu.VMEM((2, 4, 24, 384), F32),
            pltpu.VMEM((2, 4, 24, 384), BF16),
            pltpu.VMEM((4, 24, 384), BF16),
            pltpu.VMEM((4, 24, 384), BF16),
            pltpu.VMEM((3, 24, 384), BF16),
            pltpu.VMEM((24, 384), BF16),
            pltpu.VMEM((7, 24, 384), BF16),
            pltpu.VMEM((2, 8, 64, 128), BF16),
            pltpu.VMEM((2, 16, 64, 128), BF16),
            pltpu.VMEM((2, 16, 64, 128), BF16),
            pltpu.VMEM((16, 64, 128), F32),
            pltpu.VMEM((5, 16, 128), F32),
            pltpu.VMEM((11, 16, 128), F32),
            pltpu.SemaphoreType.DMA((7,)),
            pltpu.SemaphoreType.DMA((76,)),
            pltpu.SemaphoreType.DMA((76,)),
        ],
        compiler_params=pltpu.CompilerParams(
            collective_id=1, has_side_effects=True, vmem_limit_bytes=VMEM_LIMIT
        ),
        name="attend",
    )(own, cot, valid, acts, weights, bias, normed)


def finish_kernel(
    attended_in, results_in, bias_in, attended_ref, gq_ref, gk_ref, gv_ref, go_ref, bias_ref
):
    attended_ref[...] = attended_in[...]
    for n, ref in enumerate((gq_ref, gk_ref, gv_ref, go_ref)):
        ref[:, 0:384] = results_in[n, 0]
        ref[:, 384:768] = results_in[n, 1]
    bias_ref[...] = bias_in[...]


def finish(attended, results, grad_bias):
    vmem = pl.BlockSpec(memory_space=pltpu.VMEM)
    grads = jax.ShapeDtypeStruct((24, 768), F32)
    return pl.pallas_call(
        finish_kernel,
        out_shape=(
            jax.ShapeDtypeStruct((128, 768), BF16),
            grads, grads, grads, grads,
            jax.ShapeDtypeStruct((16, 128), F32),
        ),
        in_specs=[vmem] * 3,
        out_specs=[vmem] * 6,
        name="finish",
    )(attended, results, grad_bias)


def per_device(
    single, pair_features, key_valid, pair_gain, w_query, w_key, w_value, w_out, pair_bias_weight,
    out_cotangent,
):
    own_acts = single[0]
    copies, own_count, features = own_acts.shape
    w_all, acts_all, bias, normed = gather(
        w_query, w_key, w_value, w_out, own_acts,
        pair_features[0],
        pair_gain[None],
        pair_bias_weight.T,
    )
    summed = attend(
        own_acts.reshape(copies * own_count, features),
        out_cotangent[0].reshape(copies * own_count, features),
        key_valid,
        acts_all.reshape(copies * 512, features),
        w_all.reshape(4, features, features),
        bias,
        normed,
    )
    attended, grad_query, grad_key, grad_value, grad_out, grad_bias = finish(*summed)
    attended = attended.reshape(1, copies, own_count, features)
    return (attended, grad_query, grad_key, grad_value, grad_out, grad_bias.T)


def solution(mesh):
    weight = P(("row", "col"), None)
    tokens = P("dp", "col", "row", None)
    return jax.shard_map(
        per_device,
        mesh=mesh,
        in_specs=(
            tokens, P("dp", "row", "col", None), P("dp", None), P(), weight, weight, weight, weight,
            P(), tokens,
        ),
        out_specs=(tokens, weight, weight, weight, weight, P()),
        check_vma=False,
    )
```

```python
import math

import jax
import jax.numpy as jnp
from jax import lax
from jax.experimental import pallas as pl
from jax.experimental.pallas import tpu as pltpu
from jax.sharding import PartitionSpec as P

NORM_EPSILON = 1e-05
MASKED = -1000000000.0
MESH = pl.DeviceIdType.MESH
F32 = jnp.float32
BF16 = jnp.bfloat16
VMEM_LIMIT = 56 * 1024 * 1024


def place():
    dp, row, col = lax.axis_index("dp"), lax.axis_index("row"), lax.axis_index("col")
    return dp // 2, dp % 2, row // 2, row % 2, col


def device(y, z_lo, z_hi, core, x):
    return (y * 2 + z_lo, z_hi * 2 + core, x)


def greet(peers):
    barrier = pltpu.get_barrier_semaphore()
    for peer in peers:
        pl.semaphore_signal(barrier, inc=1, device_id=peer, device_id_type=MESH)


def await_greetings(peers):
    pl.semaphore_wait(pltpu.get_barrier_semaphore(), len(peers))


class Sender:
    def __init__(self, send_sem, recv_sem):
        self.send_sem, self.recv_sem, self.started = send_sem, recv_sem, []

    def send(self, src, dst, peer):
        key = len(self.started)
        copy = pltpu.make_async_remote_copy(
            src_ref=src,
            dst_ref=dst,
            send_sem=self.send_sem.at[key],
            recv_sem=self.recv_sem.at[key],
            device_id=peer,
            device_id_type=MESH,
        )
        copy.start()
        self.started.append(copy)
        return copy

    def finish(self):
        for copy in self.started:
            copy.wait_send()


def gather_kernel(
    wq_ref, wk_ref, wv_ref, wo_ref, acts_ref, pair_ref, gain_ref, pair_weight_ref,
    w_full, acts_full, bias_full, normed_ref,
    tile_bias, pair, normed_rows, local_sem, send_sem, recv_sem,
):
    y, z_lo, z_hi, core, x = place()
    row = z_hi * 2 + core
    y_next, y_back = [device((y + d) % 4, z_lo, z_hi, core, x) for d in (1, 3)]
    x_next, x_back = [device(y, z_lo, z_hi, core, (x + d) % 4) for d in (1, 3)]
    z_peers = [device(y, z_lo, (z_hi + d) % 4, core, x) for d in (1, 2, 3)]
    z_next, z_back = z_peers[0], z_peers[2]
    partner = device(y, z_lo, z_hi, 1 - core, x)
    peers = [y_next, y_back, x_next, x_back, partner] + z_peers
    greet(peers)

    def block_rows(block):
        return slice(block * 16, block * 16 + 16)

    loads = [
        pltpu.make_async_copy(
            pair_ref.at[block_rows(b)], pair.at[block_rows(b)], local_sem.at[3 + b]
        )
        for b in range(4)
    ]
    for load in loads:
        load.start()
    stores = []

    def normalize_rows(block):
        loads[block].wait()

        def one_row(k, _):
            i = block * 16 + k
            values = pair[i].astype(F32)
            center = jnp.mean(values, axis=-1, keepdims=True)
            centered = values - center
            variance = jnp.mean(centered * centered, axis=-1, keepdims=True)
            normed = (
                centered * lax.rsqrt(variance + NORM_EPSILON) * gain_ref[...]
            ).astype(BF16)
            normed_rows[i] = normed
            tile_bias[block, :, k, :] = lax.dot_general(
                pair_weight_ref[...], normed, (((1,), (1,)), ((), ())),
                preferred_element_type=F32,
            )
            return 0

        lax.fori_loop(0, 16, one_row, 0, unroll=4)
        store = pltpu.make_async_copy(
            normed_rows.at[block_rows(block)], normed_ref.at[block_rows(block)],
            local_sem.at[7 + block],
        )
        store.start()
        stores.append(store)

    def line(plane, owner, part=slice(0, 4)):
        return w_full.at[plane % 4, part, core, owner % 4]

    def rows(z_owner):
        return acts_full.at[:, (z_owner % 4) * 2 + core]

    normalize_rows(0)
    await_greetings(peers)
    out = Sender(send_sem, recv_sem)
    send = out.send
    first, second = slice(0, 2), slice(2, 4)
    for plane, w_ref in enumerate((wq_ref, wk_ref, wv_ref, wo_ref)):

        @pl.when(y == plane)
        def _(plane=plane, w_ref=w_ref):
            target = w_full.at[plane, z_hi, core, x]
            pltpu.make_async_copy(w_ref, target, local_sem.at[0]).start()
            for d, peer in enumerate(z_peers):
                pltpu.make_async_remote_copy(
                    src_ref=w_ref, dst_ref=target, send_sem=send_sem.at[d],
                    recv_sem=recv_sem.at[d], device_id=peer, device_id_type=MESH,
                ).start()

    own_w = pltpu.make_async_copy(wq_ref, w_full.at[y, z_hi, core, x], local_sem.at[0])
    own_acts = pltpu.make_async_copy(acts_ref, acts_full.at[:, row], local_sem.at[1])
    z_copies = [
        pltpu.make_async_remote_copy(
            src_ref=wq_ref, dst_ref=w_full.at[y, z_hi, core, x], send_sem=send_sem.at[d],
            recv_sem=recv_sem.at[d], device_id=peer, device_id_type=MESH,
        )
        for d, peer in enumerate(z_peers)
    ]
    out.started.extend(z_copies)
    own_acts.start()
    core_copies = [send(acts_ref, rows(z_hi), partner)]

    def swap_planes(owner):
        own = line(y, owner)
        core_copies.append(send(own, own, partner))
        return send(own, own, y_next), send(own, own, y_back)

    def bias_block(owner, chunk, heads=slice(0, 16)):
        return bias_full.at[chunk, owner % 4, heads]

    bias_near, bias_far = [], []

    def send_bias(chunk):
        source = tile_bias.at[chunk]
        bias_near.append(
            (send(source, bias_block(x, chunk), x_next), send(source, bias_block(x, chunk), x_back))
        )

    def relay_bias(chunk):
        up, down = bias_near[chunk]
        up.wait_recv()
        part = bias_block(x + 3, chunk, slice(0, 8))
        bias_far.append(send(part, part, x_next))
        down.wait_recv()
        part = bias_block(x + 1, chunk, slice(8, 16))
        bias_far.append(send(part, part, x_back))

    send_bias(0)
    normalize_rows(1)
    own_w.wait()
    for copy in z_copies:
        copy.wait_recv()
    own = line(y, x)
    x_up = send(own, own, x_next)
    x_down = send(own, own, x_back)
    planes = [swap_planes(x)]
    acts_up = send(acts_ref, rows(z_hi), z_next)
    acts_down = send(acts_ref, rows(z_hi), z_back)
    send_bias(1)
    normalize_rows(2)
    x_up.wait_recv()
    part = line(y, x + 3, first)
    x_far_up = send(part, part, x_next)
    x_down.wait_recv()
    part = line(y, x + 1, second)
    x_far_down = send(part, part, x_back)
    planes.append(swap_planes(x + 3))
    planes.append(swap_planes(x + 1))
    send_bias(2)
    acts_up.wait_recv()
    part = acts_full.at[0, ((z_hi + 3) % 4) * 2 + core]
    acts_far_up = send(part, part, z_next)
    acts_down.wait_recv()
    part = acts_full.at[1, ((z_hi + 1) % 4) * 2 + core]
    acts_far_down = send(part, part, z_back)
    core_copies.append(send(rows(z_hi + 3), rows(z_hi + 3), partner))
    core_copies.append(send(rows(z_hi + 1), rows(z_hi + 1), partner))
    relay_bias(0)
    normalize_rows(3)
    send_bias(3)
    x_far_up.wait_recv()
    x_far_down.wait_recv()
    planes.append(swap_planes(x + 2))
    owners = (x, x + 3, x + 1, x + 2)
    far = []

    def relay_planes(n):
        up, down = planes[n]
        owner = owners[n]
        up.wait_recv()
        part = line(y + 3, owner, first)
        far_up = send(part, part, y_next)
        down.wait_recv()
        part = line(y + 1, owner, second)
        far.append((far_up, send(part, part, y_back)))
        for plane in (y + 3, y + 1):
            whole = line(plane, owner)
            core_copies.append(send(whole, whole, partner))

    relay_planes(0)
    own_bias = pltpu.make_async_copy(tile_bias, bias_full.at[:, x], local_sem.at[2])
    own_bias.start()
    relay_bias(1)
    relay_planes(1)
    relay_bias(2)
    relay_planes(2)
    relay_bias(3)
    relay_planes(3)
    acts_far_up.wait_recv()
    acts_far_down.wait_recv()
    core_copies.append(send(rows(z_hi + 2), rows(z_hi + 2), partner))
    for n in range(4):
        for copy in far[n]:
            copy.wait_recv()
        whole = line(y + 2, owners[n])
        core_copies.append(send(whole, whole, partner))
    for copy in core_copies + bias_far:
        copy.wait_recv()
    own_acts.wait()
    own_bias.wait()
    for store in stores:
        store.wait()
    out.finish()


def gather(w_query, w_key, w_value, w_out, acts, pair_tile, pair_gain, pair_weight):
    any_space = pl.BlockSpec(memory_space=pl.ANY)
    vmem = pl.BlockSpec(memory_space=pltpu.VMEM)
    return pl.pallas_call(
        gather_kernel,
        out_shape=(
            jax.ShapeDtypeStruct((4, 4, 2, 4, 24, 768), BF16),
            jax.ShapeDtypeStruct((2, 8, 64, 768), BF16),
            jax.ShapeDtypeStruct((4, 4, 16, 16, 128), F32),
            jax.ShapeDtypeStruct((64, 128, 128), BF16),
        ),
        in_specs=[any_space] * 6 + [vmem] * 2,
        out_specs=[any_space] * 4,
        scratch_shapes=[
            pltpu.VMEM((4, 16, 16, 128), F32),
            pltpu.VMEM((64, 128, 128), BF16),
            pltpu.VMEM((64, 128, 128), BF16),
            pltpu.SemaphoreType.DMA((11,)),
            pltpu.SemaphoreType.DMA((63,)),
            pltpu.SemaphoreType.DMA((63,)),
        ],
        compiler_params=pltpu.CompilerParams(
            collective_id=0, has_side_effects=True, vmem_limit_bytes=VMEM_LIMIT
        ),
        name="gather",
    )(w_query, w_key, w_value, w_out, acts, pair_tile, pair_gain, pair_weight)


def transposed_product(left, right):
    return lax.dot_general(left, right, (((0,), (0,)), ((), ())), preferred_element_type=F32)


WINDOWS = ((0, 0, 5), (128, 5, 3), (384, 8, 5), (512, 13, 3))


def head_mask(start, head):
    lanes = lax.broadcasted_iota(jnp.int32, (64, 256), 1) + start
    return (lanes >= head * 48) & (lanes < head * 48 + 48)


def attention_kernel(
    own_ref, cot_ref, valid_ref, acts_hbm, w_hbm, bias_hbm, normed_hbm,
    attended_hbm, results, bias_out_ref,
    attended_ref, acts_ref, w_ref, bias_ref, normed_ref,
    query, key, value, grad, attention, query_grad, key_carry, value_carry, bias_total,
    scores, pulled, weights, probs_low, score_grad, joint, bias_grad,
    g_ref, from_core, to_far, from_far, to_y, from_y, to_x, from_x, x_halves,
    own_sum, to_pair, from_pair, to_z, from_z, last, from_last,
    bias_halves, bias_sent, bias_in, bias_sum, partial, partial_in,
    local_sem, send_sem, recv_sem,
):
    y, z_lo, z_hi, core, x = place()
    y_peers = [device((y + d) % 4, z_lo, z_hi, core, x) for d in (1, 2, 3)]
    x_peers = [device(y, z_lo, z_hi, core, (x + d) % 4) for d in (1, 2, 3)]
    z_peers = [device(y, z_lo, (z_hi + d) % 4, core, x) for d in (1, 2, 3)]
    pair_peers = [device((y + d) % 4, 1 - z_lo, z_hi, core, x) for d in range(4)]
    partner = device(y, z_lo, z_hi, 1 - core, x)
    y_next, y_back, x_next, x_back = y_peers[0], y_peers[2], x_peers[0], x_peers[2]
    peers = y_peers + x_peers + z_peers + pair_peers + [partner]
    greet(peers)

    load_acts = pltpu.make_async_copy(acts_hbm, acts_ref, local_sem.at[0])
    load_w = [
        pltpu.make_async_copy(w_hbm.at[n], w_ref.at[n], local_sem.at[1 + n]) for n in range(4)
    ]
    load_bias = pltpu.make_async_copy(bias_hbm, bias_ref, local_sem.at[5])
    load_normed = pltpu.make_async_copy(normed_hbm, normed_ref, local_sem.at[6])
    load_w[3].start()
    load_w[0].start()
    load_acts.start()
    load_w[1].start()
    load_w[2].start()
    load_bias.start()
    load_normed.start()

    scaling = 1.0 / math.sqrt(48)
    own = own_ref[...]
    cot = cot_ref[...]
    bias_total[...] = jnp.zeros_like(bias_total)
    attention[...] = jnp.zeros_like(attention)
    query_grad[...] = jnp.zeros_like(query_grad)
    load_w[3].wait()
    grad[...] = lax.dot_general(
        cot, w_ref[3], (((1,), (1,)), ((), ())), preferred_element_type=F32
    ).astype(BF16)
    load_w[0].wait()
    query[...] = jnp.dot(own, w_ref[0], preferred_element_type=F32).astype(BF16)
    load_acts.wait()
    for w, target in ((1, key), (2, value)):
        load_w[w].wait()

        def project_rows(block, _, w=w, target=target):
            rows = pl.ds(pl.multiple_of(block * 256, 256), 256)
            target[rows, :] = jnp.dot(
                acts_ref[rows, :], w_ref[w], preferred_element_type=F32
            ).astype(BF16)
            return 0

        lax.fori_loop(0, 4, project_rows, 0)
    load_bias.wait()
    keep = valid_ref[...] == 1

    def head_bias(head):
        return jnp.concatenate(
            [
                jnp.concatenate([bias_ref[r, c, head] for c in range(4)], axis=1)
                for r in range(4)
            ],
            axis=0,
        )

    def one_copy(s, _):
        q_rows = pl.ds(pl.multiple_of(s * 64, 64), 64)
        k_rows = pl.ds(pl.multiple_of(s * 512, 512), 512)
        for start, first, count in WINDOWS:
            lanes = slice(start, start + 256)
            stacked = slice(0, count * 64)
            k_win = key[k_rows, lanes]
            v_win = value[k_rows, lanes]
            q_win = query[q_rows, lanes]
            g_win = grad[q_rows, lanes]
            masks = [head_mask(start, first + n) for n in range(count)]
            zero = jnp.zeros_like(q_win)
            q_stack = jnp.concatenate([jnp.where(m, q_win, zero) for m in masks], axis=0)
            g_stack = jnp.concatenate([jnp.where(m, g_win, zero) for m in masks], axis=0)
            scores[stacked, :] = lax.dot_general(
                q_stack, k_win, (((1,), (1,)), ((), ())), preferred_element_type=F32
            )
            pulled[stacked, :] = lax.dot_general(
                g_stack, v_win, (((1,), (1,)), ((), ())), preferred_element_type=F32
            )
            inverses = []
            for n in range(count):
                rows = slice(n * 64, n * 64 + 64)
                block = scores[rows, :] * scaling + head_bias(first + n)
                block = jnp.where(keep, block, MASKED)
                shifted = jnp.exp(block - jnp.max(block, axis=1, keepdims=True))
                inverses.append(1.0 / jnp.sum(shifted, axis=1, keepdims=True))
                scores[rows, :] = shifted
                weights[rows, :] = shifted.astype(BF16)
            merged = jnp.dot(weights[stacked, :], v_win, preferred_element_type=F32)
            attended_win = jnp.zeros((64, 256), F32)
            for n in range(count):
                attended_win = jnp.where(
                    masks[n], merged[n * 64 : n * 64 + 64] * inverses[n], attended_win
                )
            attention[q_rows, lanes] += attended_win
            product = g_win.astype(F32) * attended_win.astype(BF16).astype(F32)
            for n in range(count):
                rows = slice(n * 64, n * 64 + 64)
                delta = jnp.sum(jnp.where(masks[n], product, 0.0), axis=1, keepdims=True)
                probs = scores[rows, :] * inverses[n]
                probs_low[rows, :] = probs.astype(BF16)
                change = (probs * (pulled[rows, :] - delta)).astype(BF16)
                score_grad[rows, :] = change
                bias_total[first + n] += change.astype(F32)
            back = jnp.dot(score_grad[stacked, :], k_win, preferred_element_type=F32)
            back_win = jnp.zeros((64, 256), F32)
            for n in range(count):
                back_win = jnp.where(masks[n], back[n * 64 : n * 64 + 64], back_win)
            query_grad[q_rows, lanes] += back_win
            key_win = lax.dot_general(
                score_grad[stacked, :], q_stack, (((0,), (0,)), ((), ())),
                preferred_element_type=F32,
            )
            value_win = lax.dot_general(
                probs_low[stacked, :], g_stack, (((0,), (0,)), ((), ())),
                preferred_element_type=F32,
            )
            key_left, key_right = key_win[:, 0:128], key_win[:, 128:256]
            value_left, value_right = value_win[:, 0:128], value_win[:, 128:256]
            if start % 384 == 0:
                key_carry[...] = key_right
                value_carry[...] = value_right
            else:
                key_left = key_carry[...] + key_left
                value_left = value_carry[...] + value_left
                joint[k_rows, start + 128 : start + 256] = (key_right * scaling).astype(BF16)
                joint[k_rows, start + 896 : start + 1024] = value_right.astype(BF16)
            joint[k_rows, start : start + 128] = (key_left * scaling).astype(BF16)
            joint[k_rows, start + 768 : start + 896] = value_left.astype(BF16)
        return 0

    lax.fori_loop(0, 2, one_copy, 0)
    await_greetings(peers)
    out = Sender(send_sem, recv_sem)
    send = out.send

    for column in range(4):
        bias_grad[column] = bias_total[:, :, column * 128 : column * 128 + 128].astype(BF16)
    far_block = bias_grad.at[(x + 2) % 4]
    bias_far = [
        send(far_block.at[slice(0, 8)], bias_halves.at[0], x_next),
        send(far_block.at[slice(8, 16)], bias_halves.at[1], x_back),
    ]

    merged_heads = attention[...].astype(BF16)
    q_low = (query_grad[...] * scaling).astype(BF16)
    core_copies = {}

    def store_grads(w, half, product):
        g_ref[w, 2 * half : 2 * half + 2] = product.reshape(2, 2, 4, 24, 768).astype(BF16)
        part = slice(2 * half, 2 * half + 2)
        core_copies[w, half] = send(
            g_ref.at[w, part, 1 - core], from_core.at[w, part], partner
        )

    def own_products(half):
        lanes = slice(half * 384, half * 384 + 384)
        store_grads(3, half, transposed_product(merged_heads[:, lanes], cot))
        store_grads(0, half, transposed_product(own[:, lanes], q_low))

    def all_products(half):
        lanes = slice(half * 384, half * 384 + 384)
        both = transposed_product(acts_ref[:, lanes], joint[...])
        store_grads(1, half, both[:, 0:768])
        store_grads(2, half, both[:, 768:1536])

    first_next, first_back = (y_next, x_next), (y_back, x_back)
    second_next, second_back = (x_next, y_next), (x_back, y_back)

    def both_cores(half, a, b, n):
        w = (y + (a, b)[half]) % 4
        c = (x + (b, a)[half]) % 4
        k = 2 * half + n
        return g_ref[w, k, core, c].astype(F32) + from_core[w, k, c].astype(F32)

    far, near = {}, {}

    def start_chunk(half, b):
        if b == 2:
            for w in range(4):
                core_copies[w, half].wait_recv()
        for n in range(2):
            to_far[b, 2 * half + n] = both_cores(half, 2, b, n).astype(BF16)
        far[half, b] = (
            send(to_far.at[b, 2 * half], from_far.at[0, half, b], first_next[half]),
            send(to_far.at[b, 2 * half + 1], from_far.at[1, half, b], first_back[half]),
        )

    def pass_chunk(half, b):
        to_y[0, half, b, 1] = both_cores(half, 1, b, 1).astype(BF16)
        to_y[1, half, b, 0] = both_cores(half, 3, b, 0).astype(BF16)
        far[half, b][0].wait_recv()
        to_y[0, half, b, 0] = (
            both_cores(half, 1, b, 0) + from_far[0, half, b].astype(F32)
        ).astype(BF16)
        up = send(to_y.at[0, half, b], from_y.at[0, half, b], first_next[half])
        far[half, b][1].wait_recv()
        to_y[1, half, b, 1] = (
            both_cores(half, 3, b, 1) + from_far[1, half, b].astype(F32)
        ).astype(BF16)
        down = send(to_y.at[1, half, b], from_y.at[1, half, b], first_back[half])
        near[half, b] = (up, down)

    own_products(0)
    all_products(0)
    own_products(1)
    start_chunk(0, 2)
    start_chunk(0, 1)
    for copy in bias_far:
        copy.wait_recv()

    def add_bias(h, _):
        up, down = (x + 1) % 4, (x + 3) % 4
        bias_sent[0, h] = (
            bias_grad[up, h].astype(F32) + bias_halves[0, h].astype(F32)
        ).astype(BF16)
        bias_sent[0, h + 8] = bias_grad[up, h + 8]
        bias_sent[1, h] = bias_grad[down, h]
        bias_sent[1, h + 8] = (
            bias_grad[down, h + 8].astype(F32) + bias_halves[1, h].astype(F32)
        ).astype(BF16)
        return 0

    lax.fori_loop(0, 8, add_bias, 0)
    bias_near = [
        send(bias_sent.at[0], bias_in.at[0], x_next),
        send(bias_sent.at[1], bias_in.at[1], x_back),
    ]
    all_products(1)
    pass_chunk(0, 2)
    start_chunk(1, 2)
    start_chunk(0, 3)
    pass_chunk(0, 1)
    start_chunk(1, 1)
    start_chunk(0, 0)
    pass_chunk(1, 2)
    pass_chunk(0, 3)
    start_chunk(1, 3)
    pass_chunk(1, 1)
    pass_chunk(0, 0)
    start_chunk(1, 0)
    attended_ref[...] = jnp.dot(merged_heads, w_ref[3], preferred_element_type=F32).astype(BF16)
    store_attended = pltpu.make_async_copy(attended_ref, attended_hbm, local_sem.at[7])
    store_attended.start()
    pass_chunk(1, 3)

    for copy in bias_near:
        copy.wait_recv()

    def sum_bias(h, _):
        summed = (
            bias_grad[x, h].astype(F32) + bias_in[0, h].astype(F32) + bias_in[1, h].astype(F32)
        )
        bias_sum[h] = summed.astype(BF16).astype(F32)
        return 0

    lax.fori_loop(0, 16, sum_bias, 0)
    load_normed.wait()

    def tile_rows(block, total):
        rows = [bias_sum[:, block * 8 + u, :].astype(BF16) for u in range(8)]
        tile = normed_ref[block * 8 : block * 8 + 8].reshape(1024, 128)
        return total + jnp.dot(
            jnp.concatenate(rows, axis=1), tile, preferred_element_type=F32
        )

    early = jnp.zeros((16, 128), F32)
    for block in range(4):
        early = tile_rows(block, early)
    partial[0] = early
    pass_chunk(1, 0)
    stages = ([partner], y_peers, x_peers, z_peers, pair_peers[0:1])
    starts = (0, 1, 4, 7, 10)
    in_flight = {}

    def start_stage(n):
        in_flight[n] = [
            send(partial.at[n], partial_in.at[starts[n] + d], peer)
            for d, peer in enumerate(stages[n])
        ]

    def end_stage(n):
        total = partial[n]
        for d, copy in enumerate(in_flight[n]):
            copy.wait_recv()
            total = total + partial_in[starts[n] + d]
        if n < 4:
            partial[n + 1] = total
            start_stage(n + 1)
        else:
            bias_out_ref[...] = total

    def first_sum(half, b, n):
        return (
            both_cores(half, 0, b, n)
            + from_y[0, half, b, n].astype(F32)
            + from_y[1, half, b, n].astype(F32)
        )

    def wait_first(half, b):
        near[half, b][0].wait_recv()
        near[half, b][1].wait_recv()

    x_far, x_near, pair_copies = {}, {}, {}

    def start_second(half):
        wait_first(half, 2)
        for n in range(2):
            to_x[2, half, n] = first_sum(half, 2, n).astype(BF16)
        x_far[half] = (
            send(to_x.at[2, half, 0], x_halves.at[0, half], second_next[half]),
            send(to_x.at[2, half, 1], x_halves.at[1, half], second_back[half]),
        )

    def pass_second(half):
        wait_first(half, 1)
        to_x[0, half, 1] = first_sum(half, 1, 1).astype(BF16)
        x_far[half][0].wait_recv()
        to_x[0, half, 0] = (
            first_sum(half, 1, 0) + x_halves[0, half].astype(F32)
        ).astype(BF16)
        up = send(to_x.at[0, half], from_x.at[0, half], second_next[half])
        wait_first(half, 3)
        to_x[1, half, 0] = first_sum(half, 3, 0).astype(BF16)
        x_far[half][1].wait_recv()
        to_x[1, half, 1] = (
            first_sum(half, 3, 1) + x_halves[1, half].astype(F32)
        ).astype(BF16)
        down = send(to_x.at[1, half], from_x.at[1, half], second_back[half])
        x_near[half] = (up, down)

    def end_second(half):
        wait_first(half, 0)
        for copy in x_near[half]:
            copy.wait_recv()
        for n in range(2):
            total = (
                first_sum(half, 0, n)
                + from_x[0, half, n].astype(F32)
                + from_x[1, half, n].astype(F32)
            )
            for side in range(2):
                lanes = total[:, side * 384 : side * 384 + 384]
                own_sum[side, 2 * half + n] = lanes
                to_pair[side, 2 * half + n] = lanes.astype(BF16)
        part = slice(2 * half, 2 * half + 2)
        pair_copies[half] = send(
            to_pair.at[1 - z_lo, part], from_pair.at[part], pair_peers[0]
        )

    start_second(0)
    late = partial[0]
    for block in range(4, 8):
        late = tile_rows(block, late)
    partial[0] = late
    start_stage(0)
    start_second(1)
    end_stage(0)
    pass_second(0)
    pass_second(1)
    end_stage(1)
    end_second(0)
    end_second(1)
    end_stage(2)
    for half in range(2):
        pair_copies[half].wait_recv()
        for k in (2 * half, 2 * half + 1):
            total = own_sum[z_lo, k] + from_pair[k].astype(F32)
            own_sum[z_lo, k] = total
            to_z[k] = total.astype(BF16)
    z_copies = [
        send(to_z.at[(z_hi + 1 + d) % 4], from_z.at[d], z_peers[d]) for d in range(3)
    ]
    end_stage(3)
    total = own_sum[z_lo, z_hi]
    for d, copy in enumerate(z_copies):
        copy.wait_recv()
        total = total + from_z[d].astype(F32)
    last[...] = total.astype(BF16)
    last_copies = [
        send(last, from_last.at[d], peer) for d, peer in enumerate(y_peers + pair_peers)
    ]
    results[y, z_lo] = total.astype(BF16).astype(F32)
    end_stage(4)
    for d, copy in enumerate(last_copies):
        copy.wait_recv()
        if d < 3:
            results[(y + 3 - d) % 4, z_lo] = from_last[d].astype(F32)
        else:
            results[(y + 7 - d) % 4, 1 - z_lo] = from_last[d].astype(F32)
    store_attended.wait()
    out.finish()


def attend(own, cot, valid, acts, weights, bias, normed):
    vmem = pl.BlockSpec(memory_space=pltpu.VMEM)
    any_space = pl.BlockSpec(memory_space=pl.ANY)
    return pl.pallas_call(
        attention_kernel,
        out_shape=(
            jax.ShapeDtypeStruct((128, 768), BF16),
            jax.ShapeDtypeStruct((4, 2, 24, 384), F32),
            jax.ShapeDtypeStruct((16, 128), F32),
        ),
        in_specs=[vmem] * 3 + [any_space] * 4,
        out_specs=[any_space, vmem, vmem],
        scratch_shapes=[
            pltpu.VMEM((128, 768), BF16),
            pltpu.VMEM((1024, 768), BF16),
            pltpu.VMEM((4, 768, 768), BF16),
            pltpu.VMEM((4, 4, 16, 16, 128), F32),
            pltpu.VMEM((64, 128, 128), BF16),
            pltpu.VMEM((128, 768), BF16),
            pltpu.VMEM((1024, 768), BF16),
            pltpu.VMEM((1024, 768), BF16),
            pltpu.VMEM((128, 768), BF16),
            pltpu.VMEM((128, 768), F32),
            pltpu.VMEM((128, 768), F32),
            pltpu.VMEM((512, 128), F32),
            pltpu.VMEM((512, 128), F32),
            pltpu.VMEM((16, 64, 512), F32),
            pltpu.VMEM((320, 512), F32),
            pltpu.VMEM((320, 512), F32),
            pltpu.VMEM((320, 512), BF16),
            pltpu.VMEM((320, 512), BF16),
            pltpu.VMEM((320, 512), BF16),
            pltpu.VMEM((1024, 1536), BF16),
            pltpu.VMEM((4, 16, 64, 128), BF16),
            pltpu.VMEM((4, 4, 2, 4, 24, 768), BF16),
            pltpu.VMEM((4, 4, 4, 24, 768), BF16),
            pltpu.VMEM((4, 4, 24, 768), BF16),
            pltpu.VMEM((2, 2, 4, 24, 768), BF16),
            pltpu.VMEM((2, 2, 4, 2, 24, 768), BF16),
            pltpu.VMEM((2, 2, 4, 2, 24, 768), BF16),
            pltpu.VMEM((3, 2, 2, 24, 768), BF16),
            pltpu.VMEM((2, 2, 2, 24, 768), BF16),
            pltpu.VMEM((2, 2, 24, 768), BF16),
            pltpu.VMEM((2, 4, 24, 384), F32),
            pltpu.VMEM((2, 4, 24, 384), BF16),
            pltpu.VMEM((4, 24, 384), BF16),
            pltpu.VMEM((4, 24, 384), BF16),
            pltpu.VMEM((3, 24, 384), BF16),
            pltpu.VMEM((24, 384), BF16),
            pltpu.VMEM((7, 24, 384), BF16),
            pltpu.VMEM((2, 8, 64, 128), BF16),
            pltpu.VMEM((2, 16, 64, 128), BF16),
            pltpu.VMEM((2, 16, 64, 128), BF16),
            pltpu.VMEM((16, 64, 128), F32),
            pltpu.VMEM((5, 16, 128), F32),
            pltpu.VMEM((11, 16, 128), F32),
            pltpu.SemaphoreType.DMA((8,)),
            pltpu.SemaphoreType.DMA((76,)),
            pltpu.SemaphoreType.DMA((76,)),
        ],
        compiler_params=pltpu.CompilerParams(
            collective_id=1, has_side_effects=True, vmem_limit_bytes=VMEM_LIMIT
        ),
        name="attend",
    )(own, cot, valid, acts, weights, bias, normed)


def finish_kernel(
    attended_in, results_in, bias_in, attended_ref, gq_ref, gk_ref, gv_ref, go_ref, bias_ref, sem
):
    moves = [(attended_in, attended_ref), (bias_in, bias_ref)]
    for n, ref in enumerate((gq_ref, gk_ref, gv_ref, go_ref)):
        moves.append((results_in.at[n, 0], ref.at[:, 0:384]))
        moves.append((results_in.at[n, 1], ref.at[:, 384:768]))
    copies = [
        pltpu.make_async_copy(source, target, sem.at[k])
        for k, (source, target) in enumerate(moves)
    ]
    for copy in copies:
        copy.start()
    for copy in copies:
        copy.wait()


def finish(attended, results, grad_bias):
    any_space = pl.BlockSpec(memory_space=pl.ANY)
    grads = jax.ShapeDtypeStruct((24, 768), F32)
    return pl.pallas_call(
        finish_kernel,
        out_shape=(
            jax.ShapeDtypeStruct((128, 768), BF16),
            grads, grads, grads, grads,
            jax.ShapeDtypeStruct((16, 128), F32),
        ),
        in_specs=[any_space] * 3,
        out_specs=[any_space] * 6,
        scratch_shapes=[pltpu.SemaphoreType.DMA((10,))],
        name="finish",
    )(attended, results, grad_bias)


def per_device(
    single, pair_features, key_valid, pair_gain, w_query, w_key, w_value, w_out, pair_bias_weight,
    out_cotangent,
):
    own_acts = single[0]
    copies, own_count, features = own_acts.shape
    w_all, acts_all, bias, normed = gather(
        w_query, w_key, w_value, w_out, own_acts,
        pair_features[0],
        pair_gain[None],
        pair_bias_weight.T,
    )
    summed = attend(
        own_acts.reshape(copies * own_count, features),
        out_cotangent[0].reshape(copies * own_count, features),
        key_valid,
        acts_all.reshape(copies * 512, features),
        w_all.reshape(4, features, features),
        bias,
        normed,
    )
    attended, grad_query, grad_key, grad_value, grad_out, grad_bias = finish(*summed)
    attended = attended.reshape(1, copies, own_count, features)
    return (attended, grad_query, grad_key, grad_value, grad_out, grad_bias.T)


def solution(mesh):
    weight = P(("row", "col"), None)
    tokens = P("dp", "col", "row", None)
    return jax.shard_map(
        per_device,
        mesh=mesh,
        in_specs=(
            tokens, P("dp", "row", "col", None), P("dp", None), P(), weight, weight, weight, weight,
            P(), tokens,
        ),
        out_specs=(tokens, weight, weight, weight, weight, P()),
        check_vma=False,
    )
```

```python
import math

import jax
import jax.numpy as jnp
from jax import lax
from jax.experimental import pallas as pl
from jax.experimental.pallas import tpu as pltpu
from jax.sharding import PartitionSpec as P

NORM_EPSILON = 1e-05
MASKED = -1000000000.0
MESH = pl.DeviceIdType.MESH
F32 = jnp.float32
BF16 = jnp.bfloat16
VMEM_LIMIT = 56 * 1024 * 1024


def place():
    dp, row, col = lax.axis_index("dp"), lax.axis_index("row"), lax.axis_index("col")
    return dp // 2, dp % 2, row // 2, row % 2, col


def device(y, z_lo, z_hi, core, x):
    return (y * 2 + z_lo, z_hi * 2 + core, x)


def greet(peers):
    barrier = pltpu.get_barrier_semaphore()
    for peer in peers:
        pl.semaphore_signal(barrier, inc=1, device_id=peer, device_id_type=MESH)


def await_greetings(peers):
    pl.semaphore_wait(pltpu.get_barrier_semaphore(), len(peers))


class Sender:
    def __init__(self, send_sem, recv_sem):
        self.send_sem, self.recv_sem, self.started = send_sem, recv_sem, []

    def send(self, src, dst, peer):
        key = len(self.started)
        copy = pltpu.make_async_remote_copy(
            src_ref=src,
            dst_ref=dst,
            send_sem=self.send_sem.at[key],
            recv_sem=self.recv_sem.at[key],
            device_id=peer,
            device_id_type=MESH,
        )
        copy.start()
        self.started.append(copy)
        return copy

    def finish(self):
        for copy in self.started:
            copy.wait_send()


def gather_kernel(
    wq_ref, wk_ref, wv_ref, wo_ref, acts_ref, pair_ref, gain_ref, pair_weight_ref,
    w_full, acts_full, bias_full, normed_ref,
    tile_bias, pair, normed_rows, local_sem, send_sem, recv_sem,
):
    y, z_lo, z_hi, core, x = place()
    row = z_hi * 2 + core
    y_next, y_back = [device((y + d) % 4, z_lo, z_hi, core, x) for d in (1, 3)]
    x_next, x_back = [device(y, z_lo, z_hi, core, (x + d) % 4) for d in (1, 3)]
    z_peers = [device(y, z_lo, (z_hi + d) % 4, core, x) for d in (1, 2, 3)]
    z_next, z_back = z_peers[0], z_peers[2]
    partner = device(y, z_lo, z_hi, 1 - core, x)
    peers = [y_next, y_back, x_next, x_back, partner] + z_peers
    greet(peers)

    def block_rows(block):
        return slice(block * 16, block * 16 + 16)

    loads = [
        pltpu.make_async_copy(
            pair_ref.at[block_rows(b)], pair.at[block_rows(b)], local_sem.at[3 + b]
        )
        for b in range(4)
    ]
    for load in loads:
        load.start()
    stores = []

    def normalize_rows(block):
        loads[block].wait()

        def one_row(k, _):
            i = block * 16 + k
            values = pair[i].astype(F32)
            center = jnp.mean(values, axis=-1, keepdims=True)
            centered = values - center
            variance = jnp.mean(centered * centered, axis=-1, keepdims=True)
            normed = (
                centered * lax.rsqrt(variance + NORM_EPSILON) * gain_ref[...]
            ).astype(BF16)
            normed_rows[i] = normed
            tile_bias[block, :, k, :] = lax.dot_general(
                pair_weight_ref[...], normed, (((1,), (1,)), ((), ())),
                preferred_element_type=F32,
            )
            return 0

        lax.fori_loop(0, 16, one_row, 0, unroll=4)
        store = pltpu.make_async_copy(
            normed_rows.at[block_rows(block)], normed_ref.at[block_rows(block)],
            local_sem.at[7 + block],
        )
        store.start()
        stores.append(store)

    def line(plane, owner, part=slice(0, 4)):
        return w_full.at[plane % 4, part, core, owner % 4]

    def rows(z_owner):
        return acts_full.at[:, (z_owner % 4) * 2 + core]

    normalize_rows(0)
    await_greetings(peers)
    out = Sender(send_sem, recv_sem)
    send = out.send
    first, second = slice(0, 2), slice(2, 4)
    for plane, w_ref in enumerate((wq_ref, wk_ref, wv_ref, wo_ref)):

        @pl.when(y == plane)
        def _(plane=plane, w_ref=w_ref):
            target = w_full.at[plane, z_hi, core, x]
            pltpu.make_async_copy(w_ref, target, local_sem.at[0]).start()
            for d, peer in enumerate(z_peers):
                pltpu.make_async_remote_copy(
                    src_ref=w_ref, dst_ref=target, send_sem=send_sem.at[d],
                    recv_sem=recv_sem.at[d], device_id=peer, device_id_type=MESH,
                ).start()

    own_w = pltpu.make_async_copy(wq_ref, w_full.at[y, z_hi, core, x], local_sem.at[0])
    own_acts = pltpu.make_async_copy(acts_ref, acts_full.at[:, row], local_sem.at[1])
    z_copies = [
        pltpu.make_async_remote_copy(
            src_ref=wq_ref, dst_ref=w_full.at[y, z_hi, core, x], send_sem=send_sem.at[d],
            recv_sem=recv_sem.at[d], device_id=peer, device_id_type=MESH,
        )
        for d, peer in enumerate(z_peers)
    ]
    out.started.extend(z_copies)
    own_acts.start()
    core_copies = [send(acts_ref, rows(z_hi), partner)]

    def swap_planes(owner):
        own = line(y, owner)
        core_copies.append(send(own, own, partner))
        return send(own, own, y_next), send(own, own, y_back)

    def bias_block(owner, chunk, heads=slice(0, 16)):
        return bias_full.at[chunk, owner % 4, heads]

    bias_near, bias_far = [], []

    def send_bias(chunk):
        source = tile_bias.at[chunk]
        bias_near.append(
            (send(source, bias_block(x, chunk), x_next), send(source, bias_block(x, chunk), x_back))
        )

    def relay_bias(chunk):
        up, down = bias_near[chunk]
        up.wait_recv()
        part = bias_block(x + 3, chunk, slice(0, 8))
        bias_far.append(send(part, part, x_next))
        down.wait_recv()
        part = bias_block(x + 1, chunk, slice(8, 16))
        bias_far.append(send(part, part, x_back))

    send_bias(0)
    normalize_rows(1)
    own_w.wait()
    for copy in z_copies:
        copy.wait_recv()
    own = line(y, x)
    x_up = send(own, own, x_next)
    x_down = send(own, own, x_back)
    planes = [swap_planes(x)]
    acts_up = send(acts_ref, rows(z_hi), z_next)
    acts_down = send(acts_ref, rows(z_hi), z_back)
    send_bias(1)
    normalize_rows(2)
    x_up.wait_recv()
    part = line(y, x + 3, first)
    x_far_up = send(part, part, x_next)
    x_down.wait_recv()
    part = line(y, x + 1, second)
    x_far_down = send(part, part, x_back)
    planes.append(swap_planes(x + 3))
    planes.append(swap_planes(x + 1))
    send_bias(2)
    acts_up.wait_recv()
    part = acts_full.at[0, ((z_hi + 3) % 4) * 2 + core]
    acts_far_up = send(part, part, z_next)
    acts_down.wait_recv()
    part = acts_full.at[1, ((z_hi + 1) % 4) * 2 + core]
    acts_far_down = send(part, part, z_back)
    core_copies.append(send(rows(z_hi + 3), rows(z_hi + 3), partner))
    core_copies.append(send(rows(z_hi + 1), rows(z_hi + 1), partner))
    relay_bias(0)
    normalize_rows(3)
    send_bias(3)
    x_far_up.wait_recv()
    x_far_down.wait_recv()
    planes.append(swap_planes(x + 2))
    owners = (x, x + 3, x + 1, x + 2)
    far = []

    def relay_planes(n):
        up, down = planes[n]
        owner = owners[n]
        up.wait_recv()
        part = line(y + 3, owner, first)
        far_up = send(part, part, y_next)
        down.wait_recv()
        part = line(y + 1, owner, second)
        far.append((far_up, send(part, part, y_back)))
        for plane in (y + 3, y + 1):
            whole = line(plane, owner)
            core_copies.append(send(whole, whole, partner))

    relay_planes(0)
    own_bias = pltpu.make_async_copy(tile_bias, bias_full.at[:, x], local_sem.at[2])
    own_bias.start()
    relay_bias(1)
    relay_planes(1)
    relay_bias(2)
    relay_planes(2)
    relay_bias(3)
    relay_planes(3)
    acts_far_up.wait_recv()
    acts_far_down.wait_recv()
    core_copies.append(send(rows(z_hi + 2), rows(z_hi + 2), partner))
    for n in range(4):
        for copy in far[n]:
            copy.wait_recv()
        whole = line(y + 2, owners[n])
        core_copies.append(send(whole, whole, partner))
    for copy in core_copies + bias_far:
        copy.wait_recv()
    own_acts.wait()
    own_bias.wait()
    for store in stores:
        store.wait()
    out.finish()


def gather(w_query, w_key, w_value, w_out, acts, pair_tile, pair_gain, pair_weight):
    any_space = pl.BlockSpec(memory_space=pl.ANY)
    vmem = pl.BlockSpec(memory_space=pltpu.VMEM)
    return pl.pallas_call(
        gather_kernel,
        out_shape=(
            jax.ShapeDtypeStruct((4, 4, 2, 4, 24, 768), BF16),
            jax.ShapeDtypeStruct((2, 8, 64, 768), BF16),
            jax.ShapeDtypeStruct((4, 4, 16, 16, 128), F32),
            jax.ShapeDtypeStruct((64, 128, 128), BF16),
        ),
        in_specs=[vmem] * 5 + [any_space] + [vmem] * 2,
        out_specs=[any_space] * 4,
        scratch_shapes=[
            pltpu.VMEM((4, 16, 16, 128), F32),
            pltpu.VMEM((64, 128, 128), BF16),
            pltpu.VMEM((64, 128, 128), BF16),
            pltpu.SemaphoreType.DMA((11,)),
            pltpu.SemaphoreType.DMA((63,)),
            pltpu.SemaphoreType.DMA((63,)),
        ],
        compiler_params=pltpu.CompilerParams(
            collective_id=0, has_side_effects=True, vmem_limit_bytes=VMEM_LIMIT
        ),
        name="gather",
    )(w_query, w_key, w_value, w_out, acts, pair_tile, pair_gain, pair_weight)


def transposed_product(left, right):
    return lax.dot_general(left, right, (((0,), (0,)), ((), ())), preferred_element_type=F32)


WINDOWS = ((0, 0, 5), (128, 5, 3), (384, 8, 5), (512, 13, 3))


def head_mask(start, head):
    lanes = lax.broadcasted_iota(jnp.int32, (64, 256), 1) + start
    return (lanes >= head * 48) & (lanes < head * 48 + 48)


def attention_kernel(
    own_ref, cot_ref, valid_ref, acts_hbm, w_hbm, bias_hbm, normed_hbm,
    attended_ref, results, bias_out_ref,
    acts_ref, w_ref, bias_ref, normed_ref,
    query, key, value, grad, attention, query_grad, key_carry, value_carry, bias_total,
    scores, pulled, weights, probs_low, score_grad, joint, bias_grad,
    g_ref, from_core, to_far, from_far, to_y, from_y, to_x, from_x, x_halves,
    own_sum, to_pair, from_pair, to_z, from_z, last, from_last,
    bias_halves, bias_sent, bias_in, bias_sum, partial, partial_in,
    local_sem, send_sem, recv_sem,
):
    y, z_lo, z_hi, core, x = place()
    y_peers = [device((y + d) % 4, z_lo, z_hi, core, x) for d in (1, 2, 3)]
    x_peers = [device(y, z_lo, z_hi, core, (x + d) % 4) for d in (1, 2, 3)]
    z_peers = [device(y, z_lo, (z_hi + d) % 4, core, x) for d in (1, 2, 3)]
    pair_peers = [device((y + d) % 4, 1 - z_lo, z_hi, core, x) for d in range(4)]
    partner = device(y, z_lo, z_hi, 1 - core, x)
    y_next, y_back, x_next, x_back = y_peers[0], y_peers[2], x_peers[0], x_peers[2]
    peers = y_peers + x_peers + z_peers + pair_peers + [partner]
    greet(peers)

    load_acts = pltpu.make_async_copy(acts_hbm, acts_ref, local_sem.at[0])
    load_w = [
        pltpu.make_async_copy(w_hbm.at[n], w_ref.at[n], local_sem.at[1 + n]) for n in range(4)
    ]
    load_bias = pltpu.make_async_copy(bias_hbm, bias_ref, local_sem.at[5])
    load_normed = pltpu.make_async_copy(normed_hbm, normed_ref, local_sem.at[6])
    load_w[3].start()
    load_w[0].start()
    load_acts.start()
    load_w[1].start()
    load_w[2].start()
    load_bias.start()
    load_normed.start()

    scaling = 1.0 / math.sqrt(48)
    own = own_ref[...]
    cot = cot_ref[...]
    bias_total[...] = jnp.zeros_like(bias_total)
    attention[...] = jnp.zeros_like(attention)
    query_grad[...] = jnp.zeros_like(query_grad)
    load_w[3].wait()
    grad[...] = lax.dot_general(
        cot, w_ref[3], (((1,), (1,)), ((), ())), preferred_element_type=F32
    ).astype(BF16)
    load_w[0].wait()
    query[...] = jnp.dot(own, w_ref[0], preferred_element_type=F32).astype(BF16)
    load_acts.wait()
    for w, target in ((1, key), (2, value)):
        load_w[w].wait()

        def project_rows(block, _, w=w, target=target):
            rows = pl.ds(pl.multiple_of(block * 256, 256), 256)
            target[rows, :] = jnp.dot(
                acts_ref[rows, :], w_ref[w], preferred_element_type=F32
            ).astype(BF16)
            return 0

        lax.fori_loop(0, 4, project_rows, 0)
    load_bias.wait()
    keep = valid_ref[...] == 1

    def head_bias(head):
        return jnp.concatenate(
            [
                jnp.concatenate([bias_ref[r, c, head] for c in range(4)], axis=1)
                for r in range(4)
            ],
            axis=0,
        )

    def one_copy(s, _):
        q_rows = pl.ds(pl.multiple_of(s * 64, 64), 64)
        k_rows = pl.ds(pl.multiple_of(s * 512, 512), 512)
        for start, first, count in WINDOWS:
            lanes = slice(start, start + 256)
            stacked = slice(0, count * 64)
            k_win = key[k_rows, lanes]
            v_win = value[k_rows, lanes]
            q_win = query[q_rows, lanes]
            g_win = grad[q_rows, lanes]
            masks = [head_mask(start, first + n) for n in range(count)]
            zero = jnp.zeros_like(q_win)
            q_stack = jnp.concatenate([jnp.where(m, q_win, zero) for m in masks], axis=0)
            g_stack = jnp.concatenate([jnp.where(m, g_win, zero) for m in masks], axis=0)
            scores[stacked, :] = lax.dot_general(
                q_stack, k_win, (((1,), (1,)), ((), ())), preferred_element_type=F32
            )
            pulled[stacked, :] = lax.dot_general(
                g_stack, v_win, (((1,), (1,)), ((), ())), preferred_element_type=F32
            )
            inverses = []
            for n in range(count):
                rows = slice(n * 64, n * 64 + 64)
                block = scores[rows, :] * scaling + head_bias(first + n)
                block = jnp.where(keep, block, MASKED)
                shifted = jnp.exp(block - jnp.max(block, axis=1, keepdims=True))
                inverses.append(1.0 / jnp.sum(shifted, axis=1, keepdims=True))
                scores[rows, :] = shifted
                weights[rows, :] = shifted.astype(BF16)
            merged = jnp.dot(weights[stacked, :], v_win, preferred_element_type=F32)
            attended_win = jnp.zeros((64, 256), F32)
            for n in range(count):
                attended_win = jnp.where(
                    masks[n], merged[n * 64 : n * 64 + 64] * inverses[n], attended_win
                )
            attention[q_rows, lanes] += attended_win
            product = g_win.astype(F32) * attended_win.astype(BF16).astype(F32)
            for n in range(count):
                rows = slice(n * 64, n * 64 + 64)
                delta = jnp.sum(jnp.where(masks[n], product, 0.0), axis=1, keepdims=True)
                probs = scores[rows, :] * inverses[n]
                probs_low[rows, :] = probs.astype(BF16)
                change = (probs * (pulled[rows, :] - delta)).astype(BF16)
                score_grad[rows, :] = change
                bias_total[first + n] += change.astype(F32)
            back = jnp.dot(score_grad[stacked, :], k_win, preferred_element_type=F32)
            back_win = jnp.zeros((64, 256), F32)
            for n in range(count):
                back_win = jnp.where(masks[n], back[n * 64 : n * 64 + 64], back_win)
            query_grad[q_rows, lanes] += back_win
            key_win = lax.dot_general(
                score_grad[stacked, :], q_stack, (((0,), (0,)), ((), ())),
                preferred_element_type=F32,
            )
            value_win = lax.dot_general(
                probs_low[stacked, :], g_stack, (((0,), (0,)), ((), ())),
                preferred_element_type=F32,
            )
            key_left, key_right = key_win[:, 0:128], key_win[:, 128:256]
            value_left, value_right = value_win[:, 0:128], value_win[:, 128:256]
            if start % 384 == 0:
                key_carry[...] = key_right
                value_carry[...] = value_right
            else:
                key_left = key_carry[...] + key_left
                value_left = value_carry[...] + value_left
                joint[k_rows, start + 128 : start + 256] = (key_right * scaling).astype(BF16)
                joint[k_rows, start + 896 : start + 1024] = value_right.astype(BF16)
            joint[k_rows, start : start + 128] = (key_left * scaling).astype(BF16)
            joint[k_rows, start + 768 : start + 896] = value_left.astype(BF16)
        return 0

    lax.fori_loop(0, 2, one_copy, 0)
    await_greetings(peers)
    out = Sender(send_sem, recv_sem)
    send = out.send

    for column in range(4):
        bias_grad[column] = bias_total[:, :, column * 128 : column * 128 + 128].astype(BF16)
    far_block = bias_grad.at[(x + 2) % 4]
    bias_far = [
        send(far_block.at[slice(0, 8)], bias_halves.at[0], x_next),
        send(far_block.at[slice(8, 16)], bias_halves.at[1], x_back),
    ]

    merged_heads = attention[...].astype(BF16)
    q_low = (query_grad[...] * scaling).astype(BF16)
    core_copies = {}

    def store_grads(w, half, product):
        g_ref[w, 2 * half : 2 * half + 2] = product.reshape(2, 2, 4, 24, 768).astype(BF16)
        part = slice(2 * half, 2 * half + 2)
        core_copies[w, half] = send(
            g_ref.at[w, part, 1 - core], from_core.at[w, part], partner
        )

    def own_products(half):
        lanes = slice(half * 384, half * 384 + 384)
        store_grads(3, half, transposed_product(merged_heads[:, lanes], cot))
        store_grads(0, half, transposed_product(own[:, lanes], q_low))

    def all_products(half):
        lanes = slice(half * 384, half * 384 + 384)
        both = transposed_product(acts_ref[:, lanes], joint[...])
        store_grads(1, half, both[:, 0:768])
        store_grads(2, half, both[:, 768:1536])

    first_next, first_back = (y_next, x_next), (y_back, x_back)
    second_next, second_back = (x_next, y_next), (x_back, y_back)

    def both_cores(half, a, b, n):
        w = (y + (a, b)[half]) % 4
        c = (x + (b, a)[half]) % 4
        k = 2 * half + n
        return g_ref[w, k, core, c].astype(F32) + from_core[w, k, c].astype(F32)

    far, near = {}, {}

    def start_chunk(half, b):
        if b == 2:
            for w in range(4):
                core_copies[w, half].wait_recv()
        for n in range(2):
            to_far[b, 2 * half + n] = both_cores(half, 2, b, n).astype(BF16)
        far[half, b] = (
            send(to_far.at[b, 2 * half], from_far.at[0, half, b], first_next[half]),
            send(to_far.at[b, 2 * half + 1], from_far.at[1, half, b], first_back[half]),
        )

    def pass_chunk(half, b):
        to_y[0, half, b, 1] = both_cores(half, 1, b, 1).astype(BF16)
        to_y[1, half, b, 0] = both_cores(half, 3, b, 0).astype(BF16)
        far[half, b][0].wait_recv()
        to_y[0, half, b, 0] = (
            both_cores(half, 1, b, 0) + from_far[0, half, b].astype(F32)
        ).astype(BF16)
        up = send(to_y.at[0, half, b], from_y.at[0, half, b], first_next[half])
        far[half, b][1].wait_recv()
        to_y[1, half, b, 1] = (
            both_cores(half, 3, b, 1) + from_far[1, half, b].astype(F32)
        ).astype(BF16)
        down = send(to_y.at[1, half, b], from_y.at[1, half, b], first_back[half])
        near[half, b] = (up, down)

    own_products(0)
    all_products(0)
    own_products(1)
    start_chunk(0, 2)
    start_chunk(0, 1)
    for copy in bias_far:
        copy.wait_recv()

    def add_bias(h, _):
        up, down = (x + 1) % 4, (x + 3) % 4
        bias_sent[0, h] = (
            bias_grad[up, h].astype(F32) + bias_halves[0, h].astype(F32)
        ).astype(BF16)
        bias_sent[0, h + 8] = bias_grad[up, h + 8]
        bias_sent[1, h] = bias_grad[down, h]
        bias_sent[1, h + 8] = (
            bias_grad[down, h + 8].astype(F32) + bias_halves[1, h].astype(F32)
        ).astype(BF16)
        return 0

    lax.fori_loop(0, 8, add_bias, 0)
    bias_near = [
        send(bias_sent.at[0], bias_in.at[0], x_next),
        send(bias_sent.at[1], bias_in.at[1], x_back),
    ]
    all_products(1)
    pass_chunk(0, 2)
    start_chunk(1, 2)
    start_chunk(0, 3)
    pass_chunk(0, 1)
    start_chunk(1, 1)
    start_chunk(0, 0)
    pass_chunk(1, 2)
    pass_chunk(0, 3)
    start_chunk(1, 3)
    pass_chunk(1, 1)
    pass_chunk(0, 0)
    start_chunk(1, 0)
    attended_ref[...] = jnp.dot(merged_heads, w_ref[3], preferred_element_type=F32).astype(BF16)
    pass_chunk(1, 3)

    for copy in bias_near:
        copy.wait_recv()

    def sum_bias(h, _):
        summed = (
            bias_grad[x, h].astype(F32) + bias_in[0, h].astype(F32) + bias_in[1, h].astype(F32)
        )
        bias_sum[h] = summed.astype(BF16).astype(F32)
        return 0

    lax.fori_loop(0, 16, sum_bias, 0)
    load_normed.wait()

    def tile_rows(block, total):
        rows = [bias_sum[:, block * 8 + u, :].astype(BF16) for u in range(8)]
        tile = normed_ref[block * 8 : block * 8 + 8].reshape(1024, 128)
        return total + jnp.dot(
            jnp.concatenate(rows, axis=1), tile, preferred_element_type=F32
        )

    early = jnp.zeros((16, 128), F32)
    for block in range(4):
        early = tile_rows(block, early)
    partial[0] = early
    pass_chunk(1, 0)
    late = partial[0]
    for block in range(4, 8):
        late = tile_rows(block, late)
    partial[0] = late
    stages = ([partner], y_peers, x_peers, z_peers, pair_peers[0:1])
    starts = (0, 1, 4, 7, 10)
    in_flight = {}

    def start_stage(n):
        in_flight[n] = [
            send(partial.at[n], partial_in.at[starts[n] + d], peer)
            for d, peer in enumerate(stages[n])
        ]

    def end_stage(n):
        total = partial[n]
        for d, copy in enumerate(in_flight[n]):
            copy.wait_recv()
            total = total + partial_in[starts[n] + d]
        if n < 4:
            partial[n + 1] = total
            start_stage(n + 1)
        else:
            bias_out_ref[...] = total

    def first_sum(half, b, n):
        return (
            both_cores(half, 0, b, n)
            + from_y[0, half, b, n].astype(F32)
            + from_y[1, half, b, n].astype(F32)
        )

    def wait_first(half, b):
        near[half, b][0].wait_recv()
        near[half, b][1].wait_recv()

    x_far, x_near, pair_copies = {}, {}, {}

    def start_second(half):
        wait_first(half, 2)
        for n in range(2):
            to_x[2, half, n] = first_sum(half, 2, n).astype(BF16)
        x_far[half] = (
            send(to_x.at[2, half, 0], x_halves.at[0, half], second_next[half]),
            send(to_x.at[2, half, 1], x_halves.at[1, half], second_back[half]),
        )

    def pass_second(half):
        wait_first(half, 1)
        to_x[0, half, 1] = first_sum(half, 1, 1).astype(BF16)
        x_far[half][0].wait_recv()
        to_x[0, half, 0] = (
            first_sum(half, 1, 0) + x_halves[0, half].astype(F32)
        ).astype(BF16)
        up = send(to_x.at[0, half], from_x.at[0, half], second_next[half])
        wait_first(half, 3)
        to_x[1, half, 0] = first_sum(half, 3, 0).astype(BF16)
        x_far[half][1].wait_recv()
        to_x[1, half, 1] = (
            first_sum(half, 3, 1) + x_halves[1, half].astype(F32)
        ).astype(BF16)
        down = send(to_x.at[1, half], from_x.at[1, half], second_back[half])
        x_near[half] = (up, down)

    def end_second(half):
        wait_first(half, 0)
        for copy in x_near[half]:
            copy.wait_recv()
        for n in range(2):
            total = (
                first_sum(half, 0, n)
                + from_x[0, half, n].astype(F32)
                + from_x[1, half, n].astype(F32)
            )
            for side in range(2):
                lanes = total[:, side * 384 : side * 384 + 384]
                own_sum[side, 2 * half + n] = lanes
                to_pair[side, 2 * half + n] = lanes.astype(BF16)
        part = slice(2 * half, 2 * half + 2)
        pair_copies[half] = send(
            to_pair.at[1 - z_lo, part], from_pair.at[part], pair_peers[0]
        )

    start_stage(0)
    start_second(0)
    start_second(1)
    end_stage(0)
    pass_second(0)
    pass_second(1)
    end_stage(1)
    end_second(0)
    end_second(1)
    end_stage(2)
    for half in range(2):
        pair_copies[half].wait_recv()
        for k in (2 * half, 2 * half + 1):
            total = own_sum[z_lo, k] + from_pair[k].astype(F32)
            own_sum[z_lo, k] = total
            to_z[k] = total.astype(BF16)
    z_copies = [
        send(to_z.at[(z_hi + 1 + d) % 4], from_z.at[d], z_peers[d]) for d in range(3)
    ]
    end_stage(3)
    total = own_sum[z_lo, z_hi]
    for d, copy in enumerate(z_copies):
        copy.wait_recv()
        total = total + from_z[d].astype(F32)
    last[...] = total.astype(BF16)
    last_copies = [
        send(last, from_last.at[d], peer) for d, peer in enumerate(y_peers + pair_peers)
    ]
    results[y, z_lo] = total.astype(BF16).astype(F32)
    end_stage(4)
    for d, copy in enumerate(last_copies):
        copy.wait_recv()
        if d < 3:
            results[(y + 3 - d) % 4, z_lo] = from_last[d].astype(F32)
        else:
            results[(y + 7 - d) % 4, 1 - z_lo] = from_last[d].astype(F32)
    out.finish()


def attend(own, cot, valid, acts, weights, bias, normed):
    vmem = pl.BlockSpec(memory_space=pltpu.VMEM)
    any_space = pl.BlockSpec(memory_space=pl.ANY)
    return pl.pallas_call(
        attention_kernel,
        out_shape=(
            jax.ShapeDtypeStruct((128, 768), BF16),
            jax.ShapeDtypeStruct((4, 2, 24, 384), F32),
            jax.ShapeDtypeStruct((16, 128), F32),
        ),
        in_specs=[vmem] * 3 + [any_space] * 4,
        out_specs=[vmem] * 3,
        scratch_shapes=[
            pltpu.VMEM((1024, 768), BF16),
            pltpu.VMEM((4, 768, 768), BF16),
            pltpu.VMEM((4, 4, 16, 16, 128), F32),
            pltpu.VMEM((64, 128, 128), BF16),
            pltpu.VMEM((128, 768), BF16),
            pltpu.VMEM((1024, 768), BF16),
            pltpu.VMEM((1024, 768), BF16),
            pltpu.VMEM((128, 768), BF16),
            pltpu.VMEM((128, 768), F32),
            pltpu.VMEM((128, 768), F32),
            pltpu.VMEM((512, 128), F32),
            pltpu.VMEM((512, 128), F32),
            pltpu.VMEM((16, 64, 512), F32),
            pltpu.VMEM((320, 512), F32),
            pltpu.VMEM((320, 512), F32),
            pltpu.VMEM((320, 512), BF16),
            pltpu.VMEM((320, 512), BF16),
            pltpu.VMEM((320, 512), BF16),
            pltpu.VMEM((1024, 1536), BF16),
            pltpu.VMEM((4, 16, 64, 128), BF16),
            pltpu.VMEM((4, 4, 2, 4, 24, 768), BF16),
            pltpu.VMEM((4, 4, 4, 24, 768), BF16),
            pltpu.VMEM((4, 4, 24, 768), BF16),
            pltpu.VMEM((2, 2, 4, 24, 768), BF16),
            pltpu.VMEM((2, 2, 4, 2, 24, 768), BF16),
            pltpu.VMEM((2, 2, 4, 2, 24, 768), BF16),
            pltpu.VMEM((3, 2, 2, 24, 768), BF16),
            pltpu.VMEM((2, 2, 2, 24, 768), BF16),
            pltpu.VMEM((2, 2, 24, 768), BF16),
            pltpu.VMEM((2, 4, 24, 384), F32),
            pltpu.VMEM((2, 4, 24, 384), BF16),
            pltpu.VMEM((4, 24, 384), BF16),
            pltpu.VMEM((4, 24, 384), BF16),
            pltpu.VMEM((3, 24, 384), BF16),
            pltpu.VMEM((24, 384), BF16),
            pltpu.VMEM((7, 24, 384), BF16),
            pltpu.VMEM((2, 8, 64, 128), BF16),
            pltpu.VMEM((2, 16, 64, 128), BF16),
            pltpu.VMEM((2, 16, 64, 128), BF16),
            pltpu.VMEM((16, 64, 128), F32),
            pltpu.VMEM((5, 16, 128), F32),
            pltpu.VMEM((11, 16, 128), F32),
            pltpu.SemaphoreType.DMA((7,)),
            pltpu.SemaphoreType.DMA((76,)),
            pltpu.SemaphoreType.DMA((76,)),
        ],
        compiler_params=pltpu.CompilerParams(
            collective_id=1, has_side_effects=True, vmem_limit_bytes=VMEM_LIMIT
        ),
        name="attend",
    )(own, cot, valid, acts, weights, bias, normed)


def finish_kernel(
    attended_in, results_in, bias_in, attended_ref, gq_ref, gk_ref, gv_ref, go_ref, bias_ref
):
    attended_ref[...] = attended_in[...]
    for n, ref in enumerate((gq_ref, gk_ref, gv_ref, go_ref)):
        ref[:, 0:384] = results_in[n, 0]
        ref[:, 384:768] = results_in[n, 1]
    bias_ref[...] = bias_in[...]


def finish(attended, results, grad_bias):
    vmem = pl.BlockSpec(memory_space=pltpu.VMEM)
    grads = jax.ShapeDtypeStruct((24, 768), F32)
    return pl.pallas_call(
        finish_kernel,
        out_shape=(
            jax.ShapeDtypeStruct((128, 768), BF16),
            grads, grads, grads, grads,
            jax.ShapeDtypeStruct((16, 128), F32),
        ),
        in_specs=[vmem] * 3,
        out_specs=[vmem] * 6,
        name="finish",
    )(attended, results, grad_bias)


def per_device(
    single, pair_features, key_valid, pair_gain, w_query, w_key, w_value, w_out, pair_bias_weight,
    out_cotangent,
):
    own_acts = single[0]
    copies, own_count, features = own_acts.shape
    w_all, acts_all, bias, normed = gather(
        w_query, w_key, w_value, w_out, own_acts,
        pair_features[0],
        pair_gain[None],
        pair_bias_weight.T,
    )
    summed = attend(
        own_acts.reshape(copies * own_count, features),
        out_cotangent[0].reshape(copies * own_count, features),
        key_valid,
        acts_all.reshape(copies * 512, features),
        w_all.reshape(4, features, features),
        bias,
        normed,
    )
    attended, grad_query, grad_key, grad_value, grad_out, grad_bias = finish(*summed)
    attended = attended.reshape(1, copies, own_count, features)
    return (attended, grad_query, grad_key, grad_value, grad_out, grad_bias.T)


def solution(mesh):
    weight = P(("row", "col"), None)
    tokens = P("dp", "col", "row", None)
    return jax.shard_map(
        per_device,
        mesh=mesh,
        in_specs=(
            tokens, P("dp", "row", "col", None), P("dp", None), P(), weight, weight, weight, weight,
            P(), tokens,
        ),
        out_specs=(tokens, weight, weight, weight, weight, P()),
        check_vma=False,
    )
```
